32 devices in a mesh: dp: 8 (over z, y), mp: 4 (over x, core).
Axes of the slice: x: 2, y: 2, z: 4, core: 2. Of those that a mesh axis runs over, the one named last changes fastest.
Arguments:
- pixels: float32 [3072, 768], P('dp'), may hold values from 0 to 1
- patch_owner: int32 [3072], replicated, may hold values from 0 to 8, as said below
- seq_lengths: int32 [8, 3], P('dp'), may hold values from 1 to 256, 512 in all within a row
- text_embed: float32 [4096, 768], P('dp'), may hold values from -6 to 6
- cotangent: float32 [4096, 768], P('dp'), may hold values from -6 to 6
- w_stem: bfloat16 [768, 1024], replicated, may hold values from -0.21875 to 0.21875
- bn_gain: float32 [1024], replicated, may hold values from 0.5 to 1.5
- bn_bias: float32 [1024], replicated, may hold values from -3 to 3
- w_patch: bfloat16 [1024, 768], replicated, may hold values from -0.1875 to 0.1875
- b_patch: float32 [768], replicated, may hold values from -3 to 3
- ln1_gain: float32 [768], replicated, may hold values from 0.5 to 1.5
- ln1_bias: float32 [768], replicated, may hold values from -2 to 2
- w_qkv: bfloat16 [3, 768, 768], P(None, None, 'mp'), may hold values from -0.21875 to 0.21875
- w_out: bfloat16 [768, 768], P('mp'), may hold values from -3.5 to 3.5
- b_out: float32 [768], replicated, may hold values from -3 to 3
- ln2_gain: float32 [768], replicated, may hold values from 0.5 to 1.5
- ln2_bias: float32 [768], replicated, may hold values from -2 to 2
- w_up: bfloat16 [768, 3072], P(None, 'mp'), may hold values from -0.21875 to 0.21875
- b_up: float32 [3072], P('mp'), may hold values from -3 to 3
- w_down: bfloat16 [3072, 768], P('mp'), may hold values from -0.109375 to 0.109375
- b_down: float32 [768], replicated, may hold values from -3 to 3
Outputs:
- output: float32 [4096, 768], P('dp')
- grad_pixels: float32 [3072, 768], P('dp')
- grad_text: float32 [4096, 768], P('dp')
- grad_w_stem: float32 [768, 1024], replicated
- grad_bn_gain: float32 [1024], replicated
- grad_bn_bias: float32 [1024], replicated
- grad_w_patch: float32 [1024, 768], replicated
- grad_b_patch: float32 [768], replicated
- grad_ln1_gain: float32 [768], replicated
- grad_ln1_bias: float32 [768], replicated
- grad_w_qkv: float32 [3, 768, 768], P(None, None, 'mp')
- grad_w_out: float32 [768, 768], P('mp')
- grad_b_out: float32 [768], replicated
- grad_ln2_gain: float32 [768], replicated
- grad_ln2_bias: float32 [768], replicated
- grad_w_up: float32 [768, 3072], P(None, 'mp')
- grad_b_up: float32 [3072], P('mp')
- grad_w_down: float32 [3072, 768], P('mp')
- grad_b_down: float32 [768], replicated
The draws below stay inside these ranges and needn't reach their ends.
Inputs may be any that keep to these rules, and one draw needn't show every extreme that they name: `patch_owner`: entry i * 384 + r names the dp group that receives stem row r of device i. Each device's live rows come first, from 48 to 384 of them, and one device has all 384 live; the rest hold 8. No device sends more than 48 rows to one group; one group, drawn from the seed, receives exactly 48 rows from every device, and they are the first rows of each device.
All inputs are finite; a program needn't handle non-finite values.
Results may differ from the reference program's by a relative error of at most 0.023.
Values may be sent and summed in bfloat16 or wider, within the bound.
No kernel may reach another device: no remote copies, remote signals or barrier semaphores. Data moves between devices by JAX's collectives and lax.ppermute only.
A program may use at most 128 MiB of HBM per device.

```python
import math
import jax
import jax.numpy as jnp
import numpy as np
from jax import lax

D = 768
HEADS = 12
HEAD = 64
FF = 3072
CHANNELS = 1024
PIX = 768
ROWS = 512
PR_DEV = 384
SEQ_DEV = 3
MOST = 256
CAP = 48
NPATCH = 3072
TOKENS = 4096
QBLK = 512
N_DP = 8


def owner_rows(sub_key, favored):
    shuffled = jax.random.permutation(sub_key, PR_DEV)
    owners = (shuffled // CAP).astype(jnp.int32)
    sort_key = jnp.where(owners == favored, 0, 1) * PR_DEV + jnp.arange(PR_DEV, dtype=jnp.int32)
    return owners[jnp.argsort(sort_key)]


def draw_patch_owner(key, part):
    favored = jax.random.randint(jax.random.fold_in(key, 11), (), 0, N_DP)
    fullest = jax.random.randint(jax.random.fold_in(key, 12), (), 0, N_DP)
    live_count = jax.random.randint(jax.random.fold_in(key, 13), (N_DP,), CAP, PR_DEV + 1)
    live_count = jnp.where(jnp.arange(N_DP) == fullest, PR_DEV, live_count)
    sub_keys = jax.random.split(jax.random.fold_in(key, 14), N_DP)
    owner_grid = jax.vmap(owner_rows, in_axes=(0, None))(sub_keys, favored)
    within = jnp.arange(PR_DEV)[None, :]
    owner_grid = jnp.where(within < live_count[:, None], owner_grid, N_DP)
    return owner_grid.reshape(-1).astype(jnp.int32)


def level_of(key, shape, cuts, smallest, top_value):
    factor_of = 1.0
    for dim, parts in cuts:
        heights = jax.random.uniform(jax.random.fold_in(jax.random.fold_in(key, 6), dim), (parts,), jnp.float32, smallest / len(cuts), top_value / len(cuts))
        factor_of = factor_of * jnp.repeat(jnp.exp(heights), shape[dim] // parts).reshape((-1,) + (1,) * (len(shape) - 1 - dim))
    return factor_of


def split_up(amount, total, limit, skew):
    portions = [(1 << 20) // math.isqrt(standing ** skew) + 1 for standing in range(2, amount + 1)]
    spare, holding = total - limit - (amount - 1), [1] * (amount - 1)
    while spare > 0:
        candidates = [i for i in range(amount - 1) if holding[i] < limit]
        whole, budget = sum([portions[i] for i in candidates]), spare
        for i in candidates:
            extra = min(limit - holding[i], max(1, budget * portions[i] // whole), spare)
            holding[i] = holding[i] + extra
            spare = spare - extra
    return np.array([limit] + holding)


def uneven(key, number_of, total, reach, slope):
    if number_of == 2:
        one = jax.random.randint(key, (), max(1, total - reach), min(reach, total - 1) + 1)
        return jnp.stack([one, total - one])
    lengths = jnp.asarray(split_up(number_of, total, reach, slope), jnp.int32)
    pairs = (number_of - 1) // 2
    giver, sink = lengths[1:1 + 2 * pairs:2], lengths[2:2 + 2 * pairs:2]
    margin = jnp.minimum(giver - 1, reach - sink)
    passed = jax.random.randint(jax.random.fold_in(key, 1), (pairs,), 0, 1 << 20) % (margin + 1)
    lengths = lengths.at[1:1 + 2 * pairs:2].set(giver - passed).at[2:2 + 2 * pairs:2].set(sink + passed)
    return lengths[jax.random.permutation(jax.random.fold_in(key, 2), number_of)]


def centred(stream_key, shape, width, most, cuts=(), kind=jnp.bfloat16):
    level = level_of(stream_key, shape, cuts, -0.22, 0.18) if cuts else 1.0
    result = jax.random.normal(stream_key, shape, jnp.float32) * width * level
    return jnp.minimum(jnp.maximum(result, -most), most).astype(kind)


def setup_inputs(seed: int = 0) -> dict:
    keys = jax.random.split(jax.random.key(seed), 22)
    return {
        "pixels": jnp.clip(1.0 * jax.random.uniform(keys[0], (NPATCH, PIX), jnp.float32) ** level_of(keys[0], (NPATCH, PIX), ((0, 8),), -0.2, 0.2), 0.0, 1.0),
        "patch_owner": draw_patch_owner(jax.random.fold_in(keys[21], 71), 0),
        "seq_lengths": jax.vmap(lambda own: uneven(own, SEQ_DEV, ROWS, MOST, 1))(jax.random.split(keys[2], N_DP)).reshape((N_DP, SEQ_DEV)).astype(jnp.int32),
        "text_embed": centred(keys[3], (TOKENS, D), 1.0, 6.0, ((0, 8),), jnp.float32),
        "cotangent": centred(keys[4], (TOKENS, D), 1.0, 6.0, ((0, 8),), jnp.float32),
        "w_stem": centred(keys[5], (PIX, CHANNELS), PIX ** -0.5, 0.21875),
        "bn_gain": jnp.clip(1.0 + 0.1 * jax.random.normal(keys[6], (CHANNELS,), jnp.float32), 0.5, 1.5),
        "bn_bias": centred(keys[7], (CHANNELS,), 0.5, 3.0, (), jnp.float32),
        "w_patch": centred(keys[8], (CHANNELS, D), CHANNELS ** -0.5, 0.1875),
        "b_patch": centred(keys[9], (D,), 0.5, 3.0, (), jnp.float32),
        "ln1_gain": jnp.clip(1.0 + 0.1 * jax.random.normal(keys[10], (D,), jnp.float32), 0.5, 1.5),
        "ln1_bias": centred(keys[11], (D,), 0.3, 2.0, (), jnp.float32),
        "w_qkv": centred(keys[12], (3, D, D), D ** -0.5, 0.21875, ((2, 4),)),
        "w_out": centred(keys[13], (D, D), (max(D // 256, 1)) ** -0.5, 3.5, ((0, 4),)),
        "b_out": centred(keys[14], (D,), 0.5, 3.0, (), jnp.float32),
        "ln2_gain": jnp.clip(1.0 + 0.1 * jax.random.normal(keys[15], (D,), jnp.float32), 0.5, 1.5),
        "ln2_bias": centred(keys[16], (D,), 0.3, 2.0, (), jnp.float32),
        "w_up": centred(keys[17], (D, FF), D ** -0.5, 0.21875, ((1, 4),)),
        "b_up": centred(keys[18], (FF,), 0.5, 3.0, ((0, 4),), jnp.float32),
        "w_down": centred(keys[19], (FF, D), FF ** -0.5, 0.109375, ((0, 4),)),
        "b_down": centred(keys[20], (D,), 0.5, 3.0, (), jnp.float32),
    }


highest = lax.Precision.HIGHEST
norm_eps = 1e-05
masked_score = -1e+30

@jax.custom_vjp
def low(v):
    return lax.optimization_barrier(v.astype(jnp.bfloat16)).astype(jnp.float32)

@jax.custom_vjp
def low_back(v):
    return v

def low_keep(v):
    return (low(v), None)

def low_pass(kept, grad):
    return (grad,)

def back_keep(v):
    return (v, None)

def back_low(kept, grad):
    return (low(grad),)
low.defvjp(low_keep, low_pass)
low_back.defvjp(back_keep, back_low)

def gelu_exact(values):
    return jax.nn.gelu(values, approximate=False)

def layer_norm(values, gain, shift):
    center = values - lax.optimization_barrier(jnp.mean(values, axis=-1, keepdims=True))
    return center * lax.rsqrt(lax.optimization_barrier(jnp.mean(center * center, axis=-1, keepdims=True)) + norm_eps) * gain + shift

def routing(patch_owner):
    owner_table = patch_owner.reshape(N_DP, PR_DEV)
    peer_ids = jnp.arange(N_DP, dtype=jnp.int32)
    onehot = (owner_table[:, :, None] == peer_ids[None, None, :]).astype(jnp.int32)
    counts = lax.optimization_barrier(jnp.sum(onehot, axis=1)).astype(jnp.int32)
    row_rank = (lax.optimization_barrier(jnp.sum(jnp.cumsum(onehot, axis=1) * onehot, axis=2)) - 1).astype(jnp.int32)
    before = (jnp.cumsum(counts, axis=0) - counts).astype(jnp.int32)
    live_rows = owner_table < N_DP
    safe_owner = jnp.minimum(owner_table, N_DP - 1).astype(jnp.int32)
    offset = jnp.take_along_axis(before, safe_owner, axis=1).astype(jnp.int32)
    dest_row = jnp.where(live_rows, safe_owner * ROWS + offset + row_rank, N_DP * ROWS)
    prefix = lax.optimization_barrier(jnp.sum(counts, axis=0)).astype(jnp.int32)
    return (live_rows.reshape(-1), dest_row.reshape(-1).astype(jnp.int32), prefix)

def segments(seq_lengths):
    seq_ends = jnp.cumsum(seq_lengths, axis=1).astype(jnp.int32)
    row_iota = jnp.arange(ROWS, dtype=jnp.int32)
    return lax.optimization_barrier(jnp.sum((seq_ends[:, None, :] <= row_iota[None, :, None]).astype(jnp.int32), axis=2)).astype(jnp.int32)

def attention(queries, key_vals, values, segment, prefix):
    score_scale = HEAD ** (-0.5)
    key_rows = jnp.arange(ROWS, dtype=jnp.int32)

    def one_block(block_id):
        row_start = block_id * QBLK
        block_q = lax.dynamic_slice_in_dim(queries, row_start, QBLK, 0)
        query_seg = lax.dynamic_slice_in_dim(segment, row_start, QBLK, 0)
        query_rows = row_start + jnp.arange(QBLK, dtype=jnp.int32)
        visible = (query_seg[:, None] == segment[None, :]) & ((key_rows[None, :] <= query_rows[:, None]) | (key_rows[None, :] < prefix))
        scores = low_back(jnp.einsum('qhd,khd->hqk', block_q, key_vals, precision=highest) * score_scale)
        scores = jnp.where(visible[None], scores, masked_score)
        row_top = lax.optimization_barrier(jnp.max(scores, axis=-1, keepdims=True))
        weights = jnp.exp(scores - row_top)
        weights_low = low(weights / lax.optimization_barrier(jnp.sum(weights, axis=-1, keepdims=True)))
        return low_back(low(jnp.einsum('hqk,khd->qhd', weights_low, values, precision=highest)))
    blocks_out = lax.map(jax.checkpoint(one_block), jnp.arange(ROWS // QBLK, dtype=jnp.int32))
    return blocks_out.reshape(ROWS, D)

def layer(x_rows, segment, prefix, layer_weights):
    ln1_gain, ln1_bias, w_qkv, w_out, b_out, ln2_gain, ln2_bias, w_up, b_up, w_down, b_down = layer_weights
    a_low = low(layer_norm(x_rows, ln1_gain, ln1_bias))
    proj_qkv = low_back(low(jnp.einsum('rd,tde->tre', a_low, w_qkv, precision=highest)))
    split_qkv = proj_qkv.reshape(3, ROWS, HEADS, HEAD)
    merged = attention(split_qkv[0], split_qkv[1], split_qkv[2], segment, prefix)
    hidden = x_rows + low_back(jnp.dot(merged, w_out, precision=highest)) + b_out
    b_low = low(layer_norm(hidden, ln2_gain, ln2_bias))
    middle = low_back(jnp.dot(b_low, w_up, precision=highest) + b_up)
    activated = low(gelu_exact(middle))
    return hidden + low_back(jnp.dot(activated, w_down, precision=highest)) + b_down

def forward(pixels, text_embed, w_stem, bn_gain, bn_bias, w_patch, b_patch, layer_weights, live_rows, dest_row, prefix, segment):
    pixel_low = low_back(low(pixels))
    stem_pre = low_back(jnp.dot(pixel_low, w_stem, precision=highest))
    live_mask = live_rows.astype(stem_pre.dtype)[:, None]
    live_total = jnp.sum(live_mask)
    row_mean = lax.optimization_barrier(jnp.sum(stem_pre * live_mask, axis=0)) / live_total
    row_var = lax.optimization_barrier(jnp.sum(stem_pre * stem_pre * live_mask, axis=0)) / live_total - row_mean * row_mean
    bn_out = (stem_pre - row_mean) * lax.rsqrt(row_var + norm_eps) * bn_gain + bn_bias
    stem_act = low(gelu_exact(bn_out))
    embedded = low_back(low(jnp.dot(stem_act, w_patch, precision=highest) + b_patch))
    x_all = text_embed.at[dest_row].add(embedded, mode='drop')
    x_groups = x_all.reshape(N_DP, ROWS, D)

    def run_group(packed):
        return layer(packed[0], packed[1], packed[2], layer_weights)
    return lax.map(run_group, (x_groups, segment, prefix)).reshape(N_DP * ROWS, D)

def reference(pixels, patch_owner, seq_lengths, text_embed, cotangent, w_stem, bn_gain, bn_bias, w_patch, b_patch, ln1_gain, ln1_bias, w_qkv, w_out, b_out, ln2_gain, ln2_bias, w_up, b_up, w_down, b_down):
    live_rows, dest_row, prefix = routing(patch_owner)
    segment = segments(seq_lengths)

    def wrapped(pixels_in, text_in, stem_in, gain_in, shift_in, patch_in, patch_bias_in, gain_one, shift_one, qkv_in, out_in, out_bias, gain_two, shift_two, up_in, up_bias, down_in, down_bias):
        layer_weights = (gain_one, shift_one, qkv_in, out_in, out_bias, gain_two, shift_two, up_in, up_bias, down_in, down_bias)
        return forward(pixels_in, text_in, stem_in, gain_in, shift_in, patch_in, patch_bias_in, layer_weights, live_rows, dest_row, prefix, segment)
    output, pullback = jax.vjp(wrapped, pixels, text_embed, w_stem.astype(jnp.float32), bn_gain, bn_bias, w_patch.astype(jnp.float32), b_patch, ln1_gain, ln1_bias, w_qkv.astype(jnp.float32), w_out.astype(jnp.float32), b_out, ln2_gain, ln2_bias, w_up.astype(jnp.float32), b_up, w_down.astype(jnp.float32), b_down)
    grads = pullback(cotangent)
    return (output, grads[0], grads[1], grads[2], grads[3], grads[4], grads[5], grads[6], grads[7], grads[8], grads[9], grads[10], grads[11], grads[12], grads[13], grads[14], grads[15], grads[16], grads[17])
```

```python
import jax
import jax.numpy as jnp
from jax import lax
from jax.sharding import PartitionSpec as P

HEAD = 64

norm_eps = 1e-05
masked_score = -1e30
f32 = jnp.float32
bf16 = jnp.bfloat16


def gelu_exact(values):
    return jax.nn.gelu(values, approximate=False)


def gelu_grad(values, grad_out):
    return jax.vjp(gelu_exact, values)[1](grad_out)[0]


def dot(left, right):
    return jnp.dot(left, right, preferred_element_type=f32)


def inner_rows(left, right):
    return lax.dot_general(left, right, (((0,), (0,)), ((), ())), preferred_element_type=f32)


def times_trans(left, right):
    return lax.dot_general(left, right, (((1,), (1,)), ((), ())), preferred_element_type=f32)


def layer_norm(values, gain, shift):
    center = values - jnp.mean(values, axis=-1, keepdims=True)
    inv_std = lax.rsqrt(jnp.mean(center * center, axis=-1, keepdims=True) + norm_eps)
    normal = center * inv_std
    return (normal * gain + shift, normal, inv_std)


def norm_back(grad_out, normal, inv_std, gain):
    scaled = grad_out * gain
    inner = (
        scaled
        - jnp.mean(scaled, axis=-1, keepdims=True)
        - normal * jnp.mean(scaled * normal, axis=-1, keepdims=True)
    )
    return (inv_std * inner, jnp.sum(grad_out * normal, axis=0), jnp.sum(grad_out, axis=0))


def bits_of(axis):
    size = lax.axis_size(axis)
    bits = []
    step = 1
    while step < size:
        bits.append(step)
        step *= 2
    assert step == size
    return bits


def swap(values, axis, step):
    size = lax.axis_size(axis)
    return lax.ppermute(values, axis, [(i, i ^ step) for i in range(size)])


def is_high(axis, step):
    return (lax.axis_index(axis) & step) != 0


def halve(values, axis, step):
    half = values.shape[0] // 2
    low, high = values[:half], values[half:]
    top = is_high(axis, step)
    send = jnp.where(top, low, high)
    keep = jnp.where(top, high, low)
    got = swap(send, axis, step)
    return (keep.astype(f32) + got.astype(f32)).astype(values.dtype)


def unhalve(values, axis, step):
    got = swap(values, axis, step)
    top = is_high(axis, step)
    return jnp.concatenate([jnp.where(top, got, values), jnp.where(top, values, got)], axis=0)


def sum_small(values, axis):
    for step in bits_of(axis):
        values = values + swap(values, axis, step)
    return values


def sum_rows(values, axis):
    bits = bits_of(axis)
    part = halve(values, axis, bits[0])
    for step in bits[1:]:
        got = swap(part, axis, step)
        part = (part.astype(f32) + got.astype(f32)).astype(values.dtype)
    return unhalve(part, axis, bits[0])


def sum_large(values, axis):
    bits = bits_of(axis)
    for step in bits:
        values = halve(values, axis, step)
    for step in reversed(bits):
        values = unhalve(values, axis, step)
    return values


def gather_mp(values):
    for at, step in enumerate(reversed(bits_of("mp"))):
        got = swap(values, "mp", step)
        top = is_high("mp", step)
        values = jnp.stack([jnp.where(top, got, values), jnp.where(top, values, got)], axis=at)
    return values


def block_scores(block_q, key_vals, segment, prefix, score_scale):
    rows = jnp.arange(segment.shape[0], dtype=jnp.int32)
    raw_scores = (
        jnp.einsum("qhd,khd->hqk", block_q, key_vals, preferred_element_type=f32) * score_scale
    )
    visible = (segment[:, None] == segment[None, :]) & (
        (rows[None, :] <= rows[:, None]) | (rows[None, :] < prefix)
    )
    return jnp.where(visible[None], raw_scores, masked_score)


def shards(
    pixels,
    patch_owner,
    seq_lengths,
    text_embed,
    cotangent,
    w_stem,
    bn_gain,
    bn_bias,
    w_patch,
    b_patch,
    ln1_gain,
    ln1_bias,
    w_qkv,
    w_out,
    b_out,
    ln2_gain,
    ln2_bias,
    w_up,
    b_up,
    w_down,
    b_down,
):
    groups = lax.axis_size("dp")
    ways = lax.axis_size("mp")
    self_index = lax.axis_index("dp")
    part_index = lax.axis_index("mp")
    stem_count, pix = pixels.shape
    row_count, model_width = text_embed.shape
    channels = w_stem.shape[1]
    capacity = stem_count // groups
    slots = groups * capacity
    owner_table = patch_owner.reshape(groups, stem_count)
    own_owners = lax.dynamic_index_in_dim(owner_table, self_index, 0, keepdims=False)
    live_send = own_owners < groups
    live_total = jnp.sum((owner_table < groups).astype(f32))
    stem_iota = jnp.arange(stem_count, dtype=jnp.int32)
    same = (own_owners[:, None] == own_owners[None, :]) & (stem_iota[None, :] < stem_iota[:, None])
    row_rank = jnp.sum(same.astype(jnp.int32), axis=1)
    send_slot = jnp.where(live_send, own_owners * capacity + row_rank, -1)
    slot_iota = jnp.arange(slots, dtype=jnp.int32)
    send_pick = (send_slot[None, :] == slot_iota[:, None]).astype(bf16)
    from_source = jnp.sum((owner_table == self_index).astype(jnp.int32), axis=1)
    peers = jnp.arange(groups, dtype=jnp.int32)
    start_rows = jnp.sum(
        jnp.where(peers[None, :] < peers[:, None], from_source[None, :], 0), axis=1
    )
    prefix = jnp.sum(from_source)
    within = jnp.arange(capacity, dtype=jnp.int32)
    packed_row = jnp.where(
        within[None, :] < from_source[:, None], start_rows[:, None] + within[None, :], -1
    ).reshape(-1)
    place = (packed_row[None, :] == stem_iota[:, None]).astype(bf16)
    live_packed = stem_iota < prefix

    pixel_low = pixels.astype(bf16)
    pixel_slots = dot(send_pick, pixel_low).astype(bf16)
    arrived = lax.all_to_all(
        pixel_slots.reshape(groups, capacity, pix), "dp", split_axis=0, concat_axis=0, tiled=True
    ).reshape(slots, pix)
    own_pre = jnp.where(live_send[:, None], dot(pixel_low, w_stem), 0.0)
    own_live = jnp.where(live_send[:, None], pixel_low.astype(f32), 0.0)
    stats = sum_small(
        jnp.concatenate(
            [jnp.sum(own_pre, axis=0), jnp.sum(own_pre * own_pre, axis=0), jnp.sum(own_live, axis=0)]
        ),
        "dp",
    )
    row_mean = stats[:channels] / live_total
    inv_std = lax.rsqrt(
        stats[channels : 2 * channels] / live_total - row_mean * row_mean + norm_eps
    )
    pixel_mean = stats[2 * channels :] / live_total
    packed = dot(place, arrived).astype(bf16)
    stem_pre = dot(packed, w_stem)
    normal = (stem_pre - row_mean) * inv_std
    bn_out = normal * bn_gain + bn_bias
    stem_act = gelu_exact(bn_out).astype(bf16)
    embedded = (dot(stem_act, w_patch) + b_patch).astype(bf16)
    image = jnp.where(live_packed[:, None], embedded.astype(f32), 0.0)
    x_rows = jnp.concatenate(
        [text_embed[:stem_count] + image, text_embed[stem_count:]], axis=0
    )

    seq_iota = jnp.arange(seq_lengths.shape[1], dtype=jnp.int32)
    seq_ends = jnp.sum(
        jnp.where(seq_iota[None, :] <= seq_iota[:, None], seq_lengths[0][None, :], 0), axis=1
    )
    row_iota = jnp.arange(row_count, dtype=jnp.int32)
    segment = jnp.sum((seq_ends[None, :] <= row_iota[:, None]).astype(jnp.int32), axis=1)

    a_vals, norm_one, inv_one = layer_norm(x_rows, ln1_gain, ln1_bias)
    a_low = a_vals.astype(bf16)
    proj_qkv = jnp.einsum("rd,tde->tre", a_low, w_qkv, preferred_element_type=f32).astype(bf16)
    local_width = proj_qkv.shape[2]
    head_count = local_width // HEAD
    queries, key_vals, values = proj_qkv.reshape(3, row_count, head_count, HEAD)
    score_scale = HEAD ** (-0.5)
    scores = block_scores(queries, key_vals, segment, prefix, score_scale)
    row_top = jnp.max(scores, axis=-1, keepdims=True)
    weights = jnp.exp(scores - row_top)
    probs = weights / jnp.sum(weights, axis=-1, keepdims=True)
    weights_low = probs.astype(bf16)
    merged = (
        jnp.einsum("hqk,khd->qhd", weights_low, values, preferred_element_type=f32)
        .astype(bf16)
        .reshape(row_count, local_width)
    )
    attn = sum_rows(dot(merged, w_out).astype(bf16), "mp")
    hidden = x_rows + attn.astype(f32) + b_out
    b_vals, norm_two, inv_two = layer_norm(hidden, ln2_gain, ln2_bias)
    b_low = b_vals.astype(bf16)
    middle = dot(b_low, w_up) + b_up
    activated = gelu_exact(middle).astype(bf16)
    grad_low = cotangent.astype(bf16)
    grad_mid = gelu_grad(middle, times_trans(grad_low, w_down)).astype(bf16)
    grad_b_vals = sum_rows(times_trans(grad_mid, w_up).astype(bf16), "mp").astype(f32)
    down = sum_rows(dot(activated, w_down).astype(bf16), "mp")
    output = hidden + down.astype(f32) + b_down
    grad_b_down = jnp.sum(cotangent, axis=0)
    grad_b_up = jnp.sum(grad_mid.astype(f32), axis=0)
    grad_w_down = sum_large(inner_rows(activated, grad_low).astype(bf16), "dp").astype(f32)
    grad_w_up = sum_large(inner_rows(b_low, grad_mid).astype(bf16), "dp").astype(f32)

    grad_from_two, grad_ln2_gain, grad_ln2_bias = norm_back(
        grad_b_vals, norm_two, inv_two, ln2_gain
    )
    grad_hidden = cotangent + grad_from_two
    grad_b_out = jnp.sum(grad_hidden, axis=0)
    grad_hidden_low = grad_hidden.astype(bf16)
    grad_w_out = inner_rows(merged, grad_hidden_low)
    grad_merged = (
        times_trans(grad_hidden_low, w_out).astype(bf16).reshape(row_count, head_count, HEAD)
    )
    grad_values = jnp.einsum("hqk,qhd->khd", weights_low, grad_merged, preferred_element_type=f32)
    grad_weights = jnp.einsum("qhd,khd->hqk", grad_merged, values, preferred_element_type=f32)
    row_delta = jnp.sum(probs * grad_weights, axis=-1, keepdims=True)
    grad_scores = (probs * (grad_weights - row_delta)).astype(bf16)
    grad_queries = (
        jnp.einsum("hqk,khd->qhd", grad_scores, key_vals, preferred_element_type=f32) * score_scale
    )
    grad_keys = (
        jnp.einsum("hqk,qhd->khd", grad_scores, queries, preferred_element_type=f32) * score_scale
    )
    grad_qkv = (
        jnp.stack([grad_queries, grad_keys, grad_values], axis=0)
        .reshape(3, row_count, local_width)
        .astype(bf16)
    )
    grad_a_vals = sum_rows(
        jnp.einsum("tre,tde->rd", grad_qkv, w_qkv, preferred_element_type=f32).astype(bf16), "mp"
    ).astype(f32)
    grad_w_qkv = jnp.einsum("rd,tre->tde", a_low, grad_qkv, preferred_element_type=f32)
    grad_w_qkv = sum_large(
        grad_w_qkv.astype(bf16).reshape(3 * model_width, local_width), "dp"
    ).astype(f32).reshape(3, model_width, local_width)
    grad_w_out = sum_large(grad_w_out.astype(bf16), "dp").astype(f32)
    grad_from_one, grad_ln1_gain, grad_ln1_bias = norm_back(
        grad_a_vals, norm_one, inv_one, ln1_gain
    )
    grad_text = grad_hidden + grad_from_one

    grad_embed = jnp.where(live_packed[:, None], grad_text[:stem_count], 0.0).astype(bf16)
    grad_b_patch = jnp.sum(grad_embed.astype(f32), axis=0)
    slice_c = channels // ways
    act_part = lax.dynamic_slice_in_dim(stem_act, part_index * slice_c, slice_c, 1)
    grad_w_patch = sum_large(inner_rows(act_part, grad_embed).astype(bf16), "dp")
    grad_w_patch = gather_mp(grad_w_patch).astype(f32).reshape(channels, model_width)
    grad_zed = jnp.where(
        live_packed[:, None], gelu_grad(bn_out, times_trans(grad_embed, w_patch)), 0.0
    )
    small = [
        jnp.sum(grad_zed * normal, axis=0),
        jnp.sum(grad_zed, axis=0),
        grad_b_patch,
        grad_ln1_gain,
        grad_ln1_bias,
        grad_b_out,
        grad_ln2_gain,
        grad_ln2_bias,
        grad_b_up,
        grad_b_down,
    ]
    sizes = [v.shape[0] for v in small]
    flat = sum_small(jnp.concatenate(small), "dp")
    cuts = []
    offset = 0
    for size in sizes:
        cuts.append(flat[offset : offset + size])
        offset += size
    (
        grad_bn_gain,
        grad_bn_bias,
        grad_b_patch,
        grad_ln1_gain,
        grad_ln1_bias,
        grad_b_out,
        grad_ln2_gain,
        grad_ln2_bias,
        grad_b_up,
        grad_b_down,
    ) = cuts
    inner = (
        grad_zed * bn_gain
        - grad_bn_bias * bn_gain / live_total
        - normal * (grad_bn_gain * bn_gain) / live_total
    )
    grad_pre = jnp.where(live_packed[:, None], inv_std * inner, 0.0).astype(bf16)
    slice_p = pix // ways
    centred = (packed.astype(f32) - pixel_mean).astype(bf16)
    pixel_part = lax.dynamic_slice_in_dim(centred, part_index * slice_p, slice_p, 1)
    grad_w_stem = sum_large(inner_rows(pixel_part, grad_pre).astype(bf16), "dp")
    grad_w_stem = gather_mp(grad_w_stem).astype(f32).reshape(pix, channels)
    grad_rows = times_trans(grad_pre, w_stem).astype(bf16)
    row_slots = inner_rows(place, grad_rows).astype(bf16)
    returned = lax.all_to_all(
        row_slots.reshape(groups, capacity, pix), "dp", split_axis=0, concat_axis=0, tiled=True
    ).reshape(slots, pix)
    grad_pixels = inner_rows(send_pick, returned)
    return (
        output,
        grad_pixels,
        grad_text,
        grad_w_stem,
        grad_bn_gain,
        grad_bn_bias,
        grad_w_patch,
        grad_b_patch,
        grad_ln1_gain,
        grad_ln1_bias,
        grad_w_qkv,
        grad_w_out,
        grad_b_out,
        grad_ln2_gain,
        grad_ln2_bias,
        grad_w_up,
        grad_b_up,
        grad_w_down,
        grad_b_down,
    )


def solution(mesh):
    in_specs = (
        P("dp", None),
        P(),
        P("dp", None),
        P("dp", None),
        P("dp", None),
        P(),
        P(),
        P(),
        P(),
        P(),
        P(),
        P(),
        P(None, None, "mp"),
        P("mp", None),
        P(),
        P(),
        P(),
        P(None, "mp"),
        P("mp"),
        P("mp", None),
        P(),
    )
    out_specs = (
        P("dp", None),
        P("dp", None),
        P("dp", None),
        P(),
        P(),
        P(),
        P(),
        P(),
        P(),
        P(),
        P(None, None, "mp"),
        P("mp", None),
        P(),
        P(),
        P(),
        P(None, "mp"),
        P("mp"),
        P("mp", None),
        P(),
    )
    return jax.shard_map(shards, mesh=mesh, in_specs=in_specs, out_specs=out_specs, check_vma=False)
```

```python
import functools

import jax
import jax.numpy as jnp
from jax import lax
from jax.experimental import pallas as pl
from jax.experimental.pallas import tpu as pltpu
from jax.sharding import PartitionSpec as P

HEAD = 64
BLK = 256
SCALE = HEAD ** (-0.5)

norm_eps = 1e-05
masked_score = -1e30
f32 = jnp.float32
bf16 = jnp.bfloat16
i32 = jnp.int32


def dot(left, right):
    return lax.dot_general(left, right, (((1,), (0,)), ((), ())), preferred_element_type=f32)


def dot_tn(left, right):
    return lax.dot_general(left, right, (((0,), (0,)), ((), ())), preferred_element_type=f32)


def dot_nt(left, right):
    return lax.dot_general(left, right, (((1,), (1,)), ((), ())), preferred_element_type=f32)


def iota(shape, dim):
    return lax.broadcasted_iota(i32, shape, dim)


def gelu_parts(values):
    cdf = 0.5 * (1.0 + lax.erf(values * (0.5**0.5)))
    pdf = jnp.exp(-0.5 * values * values) * 0.3989422804014327
    return cdf, cdf + values * pdf


def normed(values):
    center = values - jnp.mean(values, axis=-1, keepdims=True)
    inv_std = lax.rsqrt(jnp.mean(center * center, axis=-1, keepdims=True) + norm_eps)
    return center * inv_std, inv_std


def norm_back(grad_out, normal, inv_std, gain):
    scaled = grad_out * gain
    return inv_std * (
        scaled
        - jnp.mean(scaled, axis=-1, keepdims=True)
        - normal * jnp.mean(scaled * normal, axis=-1, keepdims=True)
    )


def col_sum(values):
    return jnp.sum(values, axis=0, keepdims=True)


VMEM = pl.BlockSpec(memory_space=pltpu.VMEM)
SMEM = pl.BlockSpec(memory_space=pltpu.SMEM)
ANY = pl.BlockSpec(memory_space=pl.ANY)
PER_US = 1.1e9


def call(kernel, name, outs, *args, scratch=(), cost=1.0, after=()):
    shapes = [jax.ShapeDtypeStruct(s, t) for s, t in outs]
    first = len(args)

    def body(*refs):
        kernel(*refs[:first], *refs[first + len(after) :])

    return pl.pallas_call(
        body,
        name=name,
        out_shape=shapes,
        in_specs=[SMEM] + [VMEM] * (first - 1) + [ANY] * len(after),
        out_specs=[VMEM] * len(outs),
        scratch_shapes=list(scratch),
        compiler_params=pltpu.CompilerParams(vmem_limit_bytes=20 << 20),
        cost_estimate=pl.CostEstimate(
            flops=int(cost * PER_US), bytes_accessed=0, transcendentals=0
        ),
    )(*args, *after)


def bits_of(axis):
    size = lax.axis_size(axis)
    bits = []
    step = 1
    while step < size:
        bits.append(step)
        step *= 2
    assert step == size
    return bits


def swap(values, axis, step):
    size = lax.axis_size(axis)
    return lax.ppermute(values, axis, [(i, i ^ step) for i in range(size)])


def put_half(keep_ref, send_ref, top, start, value):
    half = keep_ref.shape[0]
    at = pl.ds(start % half, value.shape[0])
    mine = top == (start // half)

    @pl.when(mine)
    def _():
        keep_ref[at] = value.astype(keep_ref.dtype)

    @pl.when(jnp.logical_not(mine))
    def _():
        send_ref[at] = value.astype(send_ref.dtype)


def bit_set(idx_ref, which, step):
    return (idx_ref[which] // step) % 2


def plan(order, rows):
    steps = []
    for step in order:
        cut = rows % 32 == 0
        rows = rows // 2 if cut else rows
        steps.append((step, cut))
    return steps


def add_split_kernel(step, idx_ref, keep_ref, got_ref, next_ref, send_ref):
    top = bit_set(idx_ref, 0, step)
    half = next_ref.shape[0]
    for part in range(2):
        at = pl.ds(part * half, half)
        total = keep_ref[at].astype(f32) + got_ref[at].astype(f32)
        put_half(next_ref, send_ref, top, part * half, total)


def add_kernel(idx_ref, keep_ref, got_ref, out_ref):
    out_ref[...] = (keep_ref[...].astype(f32) + got_ref[...].astype(f32)).astype(out_ref.dtype)


def add(idx, keep, got):
    return call(add_kernel, "add", [(keep.shape, keep.dtype)], idx, keep, got)[0]


def scatter_sum(idx, keep, send, steps):
    for at, (step, cut) in enumerate(steps):
        got = swap(send, "dp", step)
        if at + 1 < len(steps):
            following, cut_next = steps[at + 1]
            if cut_next:
                half = (keep.shape[0] // 2, keep.shape[1])
                keep, send = call(
                    functools.partial(add_split_kernel, following),
                    "add_split",
                    [(half, keep.dtype)] * 2,
                    idx,
                    keep,
                    got,
                )
                continue
        keep = send = add(idx, keep, got)
    return keep


def join_kernel(idx_ref, *refs):
    out_ref = refs[-1]
    start = 0
    for ref in refs[:-1]:
        out_ref[pl.ds(start, ref.shape[0])] = ref[...]
        start += ref.shape[0]


def join(idx, pieces):
    if len(pieces) == 1:
        return pieces[0]
    rows = sum(p.shape[0] for p in pieces)
    outs = [((rows, pieces[0].shape[1]), pieces[0].dtype)]
    return call(join_kernel, "join", outs, idx, *pieces, cost=0.5)[0]


def gather(idx, piece, steps):
    pieces = [piece]
    for step, cut in reversed(steps):
        if cut:
            pieces.append(swap(join(idx, pieces), "dp", step))
    return pieces


def place_pieces(idx_ref, piece_refs, steps, store):
    cuts = [step for step, cut in steps if cut]
    rows = piece_refs[0].shape[0]
    total = rows << len(cuts)
    back = list(reversed(cuts))
    count = 0
    for ref in piece_refs:
        for start in range(0, ref.shape[0], rows):
            row = 0
            size = total
            for step in cuts:
                size //= 2
                flip = (count >> back.index(step)) & 1
                bit = bit_set(idx_ref, 0, step)
                row = row + (1 - bit if flip else bit) * size
            store(pl.multiple_of(row, rows), ref[pl.ds(start, rows)])
            count += 1


def slots_kernel(groups, idx_ref, owner_ref, pixel_ref, slots_ref, slot_ref, dest_ref, info_ref):
    count = pixel_ref.shape[0]
    slots = slots_ref.shape[0]
    capacity = slots // groups
    own = owner_ref[pl.ds(idx_ref[0], 1), :]
    hot = (iota((groups, count), 0) == own).astype(f32)
    before = (iota((count, count), 0) < iota((count, count), 1)).astype(bf16)
    rank = jnp.sum(hot * dot(hot.astype(bf16), before), axis=0, keepdims=True).astype(i32)
    slot = jnp.where(own < groups, own * capacity + rank, -1)
    slot_ref[...] = slot
    pick = (iota((slots, count), 0) == slot).astype(bf16)
    slots_ref[...] = dot(pick, pixel_ref[...].astype(bf16)).astype(bf16)
    table = owner_ref[...]
    sources = jnp.sum((table == idx_ref[0]).astype(f32), axis=1, keepdims=True)
    lower = (iota((groups, groups), 1) < iota((groups, groups), 0)).astype(bf16)
    starts = dot(lower, jnp.broadcast_to(sources, (groups, 128)).astype(bf16))[:, :1].astype(i32)
    within = iota((groups, slots), 1) - capacity * iota((groups, slots), 0)
    taken = (within >= 0) & (within < sources.astype(i32))
    dest_ref[...] = jnp.max(jnp.where(taken, starts + within, -1), axis=0, keepdims=True)
    prefix = jnp.sum(sources, axis=0, keepdims=True)
    live = jnp.sum((table < groups).astype(f32), axis=1, keepdims=True)
    live_total = jnp.sum(live, axis=0, keepdims=True)
    own_live = jnp.sum((own < groups).astype(f32), axis=1, keepdims=True)
    row = iota(info_ref.shape, 0)
    info_ref[...] = jnp.where(row == 0, prefix, jnp.where(row == 1, live_total, own_live))


def stats_kernel(idx_ref, info_ref, pixel_ref, w_stem_ref, stats_ref):
    channels = w_stem_ref.shape[1]
    live = info_ref[2:3, :1].astype(i32)
    sums = [jnp.zeros((1, channels), f32), jnp.zeros((1, channels), f32)]
    pixel_sum = jnp.zeros((1, pixel_ref.shape[1]), f32)
    size = pixel_ref.shape[0] // 2
    for start in range(0, pixel_ref.shape[0], size):
        here = iota((size, 1), 0) + start < live
        low = jnp.where(here, pixel_ref[pl.ds(start, size)], 0.0).astype(bf16)
        pre = dot(low, w_stem_ref[...])
        sums = [sums[0] + col_sum(pre), sums[1] + col_sum(pre * pre)]
        pixel_sum = pixel_sum + col_sum(low.astype(f32))
    stats_ref[...] = jnp.zeros(stats_ref.shape, f32)
    stats_ref[0:1] = sums[0]
    stats_ref[1:2] = sums[1]
    stats_ref[2:3, : pixel_ref.shape[1]] = pixel_sum


def early_kernel(idx_ref, cot_ref, w_down_ref, low_ref, act_ref, sum_ref):
    total = jnp.zeros(sum_ref.shape, f32)
    for start in range(0, cot_ref.shape[0], BLK):
        at = pl.ds(start, BLK)
        cot = cot_ref[at]
        low = cot.astype(bf16)
        low_ref[at] = low
        act_ref[at] = dot_nt(low, w_down_ref[...])
        total = total + col_sum(cot)
    sum_ref[...] = total


def bn_rows(stats_ref, info_ref):
    total = info_ref[1:2, :1]
    mean = stats_ref[0:1] / total
    inv = lax.rsqrt(stats_ref[1:2] / total - mean * mean + norm_eps)
    return mean, inv, total


def stem_kernel(
    idx_ref,
    info_ref,
    dest_ref,
    arrived_ref,
    stats_ref,
    w_stem_ref,
    bn_gain_ref,
    bn_bias_ref,
    w_patch_ref,
    b_patch_ref,
    text_ref,
    ln1_gain_ref,
    ln1_bias_ref,
    centred_ref,
    normal_ref,
    act_ref,
    slope_ref,
    x_ref,
    a_low_ref,
):
    count, pix = arrived_ref.shape
    prefix = info_ref[0:1, :1].astype(i32)
    mean, inv, total = bn_rows(stats_ref, info_ref)
    pixel_mean = stats_ref[2:3, :pix] / total
    for start, size in stem_blocks(count, text_ref.shape[0]):
        at = pl.ds(start, size)
        x = text_ref[at]
        if start < count:
            place = (iota((size, count), 0) + start == dest_ref[...]).astype(bf16)
            packed = dot(place, arrived_ref[...])
            centred_ref[at] = (packed - pixel_mean).astype(bf16)
            normal = (dot(packed.astype(bf16), w_stem_ref[...]) - mean) * inv
            normal_ref[at] = normal
            bn_out = normal * bn_gain_ref[...] + bn_bias_ref[...]
            cdf, slope = gelu_parts(bn_out)
            slope_ref[at] = slope
            act = (bn_out * cdf).astype(bf16)
            act_ref[at] = act
            embedded = (dot(act, w_patch_ref[...]) + b_patch_ref[...]).astype(bf16)
            here = iota((size, 1), 0) + start < prefix
            x = x + jnp.where(here, embedded.astype(f32), 0.0)
        x_ref[at] = x
        normal_one, _ = normed(x)
        a_low_ref[at] = (normal_one * ln1_gain_ref[...] + ln1_bias_ref[...]).astype(bf16)


def stem_blocks(count, rows):
    half = count // 2
    return [(0, half), (half, half)] + ([(count, rows - count)] if rows > count else [])


def segments(seq_ref, shape, dim):
    rows = iota(shape, dim)
    end = jnp.zeros((1, 1), i32)
    segment = jnp.zeros(shape, i32)
    for at in range(seq_ref.shape[1]):
        end = end + seq_ref[0:1, at : at + 1]
        segment = segment + (end <= rows).astype(i32)
    return segment


def head_lanes(width, head):
    lane = iota((1, width), 1)
    return (lane >= head * HEAD) & (lane < (head + 1) * HEAD)


def attention_kernel(
    idx_ref,
    info_ref,
    seq_ref,
    a_low_ref,
    w_qkv_ref,
    w_out_ref,
    *refs,
):
    base_ref = refs[0] if len(refs) == 6 else None
    q_ref, k_ref, v_ref, merged_ref, out_ref = refs[-5:]
    rows = a_low_ref.shape[0]
    width = w_out_ref.shape[0]
    low = a_low_ref[...]
    for t, (ref, scale) in enumerate(((q_ref, SCALE), (k_ref, 1.0), (v_ref, 1.0))):
        part = dot_nt(low, w_qkv_ref[pl.ds(t * width, width)])
        ref[...] = (part * scale if scale != 1.0 else part).astype(bf16)
    prefix = info_ref[0:1, :1].astype(i32)
    key_rows, query_rows = iota((rows, rows), 1), iota((rows, rows), 0)
    visible = (segments(seq_ref, (rows, 1), 0) == segments(seq_ref, (1, rows), 1)) & (
        (key_rows <= query_rows) | (key_rows < prefix)
    )
    bias = jnp.where(visible, 0.0, masked_score)
    zero = jnp.zeros((), bf16)
    merged = jnp.zeros((rows, width), f32)
    for head in range(width // HEAD):
        mask = head_lanes(width, head)
        scores = dot_nt(jnp.where(mask, q_ref[...], zero), k_ref[...]) + bias
        weights = jnp.exp(scores - jnp.max(scores, axis=-1, keepdims=True))
        share = 1.0 / jnp.sum(weights, axis=-1, keepdims=True)
        merged = jnp.where(mask, dot(weights.astype(bf16), v_ref[...]) * share, merged)
    merged = merged.astype(bf16)
    merged_ref[...] = merged
    part = dot(merged, w_out_ref[...])
    if base_ref is not None:
        part = part + base_ref[...]
    out_ref[...] = part.astype(out_ref.dtype)


def mlp_kernel(
    idx_ref,
    x_ref,
    part_ref,
    got_ref,
    b_out_ref,
    ln2_gain_ref,
    ln2_bias_ref,
    w_up_ref,
    b_up_ref,
    grad_act_ref,
    hidden_ref,
    b_low_ref,
    act_ref,
    grad_mid_ref,
    keep_ref,
    send_ref,
    sum_ref,
):
    top = bit_set(idx_ref, 1, 1)
    total = jnp.zeros(sum_ref.shape, f32)
    for start in range(0, x_ref.shape[0], BLK):
        at = pl.ds(start, BLK)
        attn = part_ref[at].astype(f32) + got_ref[at].astype(f32)
        hidden = x_ref[at] + attn + b_out_ref[...]
        hidden_ref[at] = hidden
        normal, _ = normed(hidden)
        b_low = (normal * ln2_gain_ref[...] + ln2_bias_ref[...]).astype(bf16)
        b_low_ref[at] = b_low
        middle = dot(b_low, w_up_ref[...]) + b_up_ref[...]
        cdf, slope = gelu_parts(middle)
        act_ref[at] = (middle * cdf).astype(bf16)
        grad_mid = (slope * grad_act_ref[at]).astype(bf16)
        grad_mid_ref[at] = grad_mid
        total = total + col_sum(grad_mid.astype(f32))
        put_half(keep_ref, send_ref, top, start, dot_nt(grad_mid, w_up_ref[...]))
    sum_ref[...] = total


def mlp_grads_kernel(
    steps,
    idx_ref,
    b_low_ref,
    act_ref,
    grad_mid_ref,
    grad_low_ref,
    down_keep_ref,
    down_send_ref,
    up_keep_ref,
    up_send_ref,
):
    for step, left, right, keep, send in (
        (steps[0], act_ref, grad_low_ref, down_keep_ref, down_send_ref),
        (steps[1], b_low_ref, grad_mid_ref, up_keep_ref, up_send_ref),
    ):
        top = bit_set(idx_ref, 0, step)
        half = keep.shape[0]
        for start in (0, half):
            put_half(keep, send, top, start, dot_tn(left[:, pl.ds(start, half)], right[...]))


def down_kernel(idx_ref, act_ref, w_down_ref, keep_ref, send_ref):
    top = bit_set(idx_ref, 1, 1)
    for start in range(0, act_ref.shape[0], BLK):
        put_half(keep_ref, send_ref, top, start, dot(act_ref[pl.ds(start, BLK)], w_down_ref[...]))


def output_kernel(idx_ref, hidden_ref, mine_ref, other_ref, b_down_ref, out_ref):
    top = bit_set(idx_ref, 1, 1)
    half = mine_ref.shape[0]
    for start in range(0, hidden_ref.shape[0], BLK):
        at = pl.ds(start, BLK)
        down = pick_half(mine_ref, other_ref, top, start, half)
        out_ref[at] = hidden_ref[at] + down + b_down_ref[...]


def pick_half(mine_ref, other_ref, top, start, half):
    at = pl.ds(start % half, BLK)
    mine = top == (start // half)
    return jnp.where(mine, mine_ref[at].astype(f32), other_ref[at].astype(f32))


def hidden_back_kernel(
    idx_ref,
    mine_ref,
    other_ref,
    cot_ref,
    hidden_ref,
    ln2_gain_ref,
    w_out_own_ref,
    w_out_far_ref,
    grad_hidden_ref,
    low_ref,
    own_ref,
    far_ref,
    sums_ref,
):
    top = bit_set(idx_ref, 1, 1)
    half = mine_ref.shape[0]
    width = cot_ref.shape[1]
    sums = [jnp.zeros((1, width), f32)] * 3
    for start in range(0, cot_ref.shape[0], BLK):
        at = pl.ds(start, BLK)
        grad = pick_half(mine_ref, other_ref, top, start, half)
        normal, inv = normed(hidden_ref[at])
        grad_hidden = cot_ref[at] + norm_back(grad, normal, inv, ln2_gain_ref[...])
        grad_hidden_ref[at] = grad_hidden
        low = grad_hidden.astype(bf16)
        low_ref[at] = low
        own_ref[at] = dot_nt(low, w_out_own_ref[...]).astype(bf16)
        far_ref[at] = dot_nt(low, w_out_far_ref[...]).astype(bf16)
        sums = [
            sums[0] + col_sum(grad_hidden),
            sums[1] + col_sum(grad * normal),
            sums[2] + col_sum(grad),
        ]
    for at in range(3):
        sums_ref[at : at + 1] = sums[at]


def attention_back_kernel(
    idx_ref,
    info_ref,
    seq_ref,
    q_ref,
    k_ref,
    v_ref,
    grad_ref,
    w_qkv_ref,
    *refs,
):
    base_ref = refs[0] if len(refs) == 3 else None
    grad_qkv_ref, out_ref = refs[-2:]
    rows, width = q_ref.shape
    prefix = info_ref[0:1, :1].astype(i32)
    zero = jnp.zeros((), bf16)
    key_rows, query_rows = iota((rows, rows), 0), iota((rows, rows), 1)
    visible = (segments(seq_ref, (rows, 1), 0) == segments(seq_ref, (1, rows), 1)) & (
        (key_rows <= query_rows) | (key_rows < prefix)
    )
    bias = jnp.where(visible, 0.0, masked_score)
    grad_values = jnp.zeros((rows, width), f32)
    grad_keys = jnp.zeros((rows, width), f32)
    grad_queries = jnp.zeros((rows, width), f32)
    for head in range(width // HEAD):
        mask = head_lanes(width, head)
        query = jnp.where(mask, q_ref[...], zero)
        grad = jnp.where(mask, grad_ref[...], zero)
        scores = dot_nt(k_ref[...], query) + bias
        weights = jnp.exp(scores - jnp.max(scores, axis=0, keepdims=True))
        probs = weights * (1.0 / jnp.sum(weights, axis=0, keepdims=True))
        grad_weights = dot_nt(v_ref[...], grad)
        delta = jnp.sum(probs * grad_weights, axis=0, keepdims=True)
        grad_scores = (probs * (grad_weights - delta)).astype(bf16)
        grad_values = grad_values + dot(probs.astype(bf16), grad)
        grad_keys = grad_keys + dot(grad_scores, query)
        grad_queries = jnp.where(mask, dot_tn(grad_scores, k_ref[...]), grad_queries)
    total = jnp.zeros((rows, w_qkv_ref.shape[1]), f32)
    for t, value in enumerate((grad_queries * SCALE, grad_keys, grad_values)):
        low = value.astype(bf16)
        grad_qkv_ref[t] = low
        total = total + dot(low, w_qkv_ref[pl.ds(t * width, width)])
    if base_ref is not None:
        total = total + base_ref[...]
    out_ref[...] = total.astype(out_ref.dtype)


def attention_grads_kernel(
    step, idx_ref, grad_qkv_ref, a_low_ref, merged_ref, low_ref, keep_ref, send_ref
):
    top = bit_set(idx_ref, 0, step)
    width = merged_ref.shape[1]
    for t in range(3):
        put_half(keep_ref, send_ref, top, t * width, dot_tn(grad_qkv_ref[t], a_low_ref[...]))
    put_half(keep_ref, send_ref, top, 3 * width, dot_tn(merged_ref[...], low_ref[...]))


def text_back_kernel(
    idx_ref,
    info_ref,
    part_ref,
    got_ref,
    grad_hidden_ref,
    x_ref,
    ln1_gain_ref,
    normal_ref,
    slope_ref,
    w_patch_ref,
    late_ref,
    up_sum_ref,
    down_sum_ref,
    grad_text_ref,
    embed_ref,
    zed_ref,
    small_ref,
):
    count, channels = normal_ref.shape
    width = x_ref.shape[1]
    prefix = info_ref[0:1, :1].astype(i32)
    bn_sums = [jnp.zeros((1, channels), f32)] * 2
    sums = [jnp.zeros((1, width), f32)] * 3
    for start, size in stem_blocks(count, x_ref.shape[0]):
        at = pl.ds(start, size)
        grad = part_ref[at].astype(f32) + got_ref[at].astype(f32)
        normal, inv = normed(x_ref[at])
        grad_text = grad_hidden_ref[at] + norm_back(grad, normal, inv, ln1_gain_ref[...])
        grad_text_ref[at] = grad_text
        sums[1] = sums[1] + col_sum(grad * normal)
        sums[2] = sums[2] + col_sum(grad)
        if start < count:
            here = iota((size, 1), 0) + start < prefix
            embed = jnp.where(here, grad_text, 0.0).astype(bf16)
            embed_ref[at] = embed
            sums[0] = sums[0] + col_sum(embed.astype(f32))
            zed = slope_ref[at] * dot_nt(embed, w_patch_ref[...])
            zed_ref[at] = zed
            bn_sums = [bn_sums[0] + col_sum(zed * normal_ref[at]), bn_sums[1] + col_sum(zed)]
    small_ref[...] = jnp.zeros(small_ref.shape, f32)
    small_ref[0:1] = bn_sums[0]
    small_ref[1:2] = bn_sums[1]
    for at in range(3):
        small_ref[2 + at : 3 + at, :width] = sums[at]
    small_ref[5:8, :width] = late_ref[...]
    small_ref[8:9, : up_sum_ref.shape[1]] = up_sum_ref[...]
    small_ref[9:10, :width] = down_sum_ref[...]


def patch_grad_kernel(step, idx_ref, act_ref, embed_ref, keep_ref, send_ref):
    top = bit_set(idx_ref, 0, step)
    half = keep_ref.shape[0]
    first = idx_ref[1] * (2 * half)
    for part in range(2):
        columns = pl.ds(pl.multiple_of(first + part * half, half), half)
        put_half(keep_ref, send_ref, top, part * half, dot_tn(act_ref[:, columns], embed_ref[...]))


def stem_back_kernel(
    step,
    idx_ref,
    info_ref,
    stats_ref,
    small_ref,
    bn_gain_ref,
    zed_ref,
    normal_ref,
    centred_ref,
    keep_ref,
    send_ref,
    pre_ref,
):
    mean, inv, total = bn_rows(stats_ref, info_ref)
    prefix = info_ref[0:1, :1].astype(i32)
    gain_mean = small_ref[0:1] / total
    bias_mean = small_ref[1:2] / total
    factor = inv * bn_gain_ref[...]
    size = zed_ref.shape[0] // 2
    for start in range(0, zed_ref.shape[0], size):
        at = pl.ds(start, size)
        here = iota((size, 1), 0) + start < prefix
        inner = zed_ref[at] - bias_mean - normal_ref[at] * gain_mean
        pre_ref[at] = jnp.where(here, factor * inner, 0.0).astype(bf16)
    top = bit_set(idx_ref, 0, step)
    half = keep_ref.shape[0]
    first = idx_ref[1] * (2 * half)
    for part in range(2):
        columns = pl.ds(pl.multiple_of(first + part * half, half), half)
        put_half(keep_ref, send_ref, top, part * half, dot_tn(pre_ref[:, columns], centred_ref[...]))


def pixel_back_kernel(idx_ref, dest_ref, pre_ref, w_stem_ref, slots_ref):
    slots = slots_ref.shape[0]
    place = (iota((pre_ref.shape[0], slots), 0) == dest_ref[...]).astype(bf16)
    rows = dot_nt(pre_ref[...], w_stem_ref[...]).astype(bf16)
    slots_ref[...] = dot_tn(place, rows).astype(bf16)


def pixel_kernel(idx_ref, slot_ref, back_ref, out_ref):
    slots, count = back_ref.shape[0], out_ref.shape[0]
    pick = (iota((slots, count), 0) == slot_ref[...]).astype(bf16)
    out_ref[...] = dot_tn(pick, back_ref[...])


def widen_kernel(steps, idx_ref, *refs):
    out_ref = refs[-1]

    def store(row, value):
        out_ref[pl.ds(row, value.shape[0])] = value.astype(out_ref.dtype)

    place_pieces(idx_ref, refs[:-1], steps, store)


def widen_heads_kernel(steps, idx_ref, *refs):
    qkv_ref, out_ref, held_ref = refs[-3:]

    def store(row, value):
        held_ref[pl.ds(row, value.shape[0])] = value.astype(f32)

    place_pieces(idx_ref, refs[:-3], steps, store)
    split = qkv_ref.shape[0]
    qkv_ref[...] = held_ref[pl.ds(0, split)]
    out_ref[...] = held_ref[pl.ds(split, out_ref.shape[0])]


def gather_mp_kernel(turned, idx_ref, own_ref, far_ref, near_ref, out_ref):
    rows = own_ref.shape[0]
    for flip, value in (
        (0, own_ref[...]),
        (2, far_ref[...]),
        (1, near_ref[pl.ds(0, rows)]),
        (3, near_ref[pl.ds(rows, rows)]),
    ):
        at = bit_set(idx_ref, 1, 1) ^ (flip & 1)
        at = at + 2 * (bit_set(idx_ref, 1, 2) ^ (flip >> 1))
        part = pl.ds(pl.multiple_of(at * rows, rows), rows)
        if turned:
            out_ref[:, part] = value.astype(f32).T
        else:
            out_ref[part] = value.astype(f32)


def sum_mp(idx, keep, send):
    near, far = bits_of("mp")
    first = add(idx, keep, swap(send, "mp", near))
    half = add(idx, first, swap(first, "mp", far))
    return half, swap(half, "mp", near), first


def gather_mp(idx, name, values, turned):
    near, far = bits_of("mp")
    got_far = swap(values, "mp", far)
    got_near = swap(join(idx, [values, got_far]), "mp", near)
    rows, width = values.shape
    shape = (width, 4 * rows) if turned else (4 * rows, width)
    kernel = functools.partial(gather_mp_kernel, turned)
    return call(kernel, name, [(shape, f32)], idx, values, got_far, got_near)[0]


def shards(
    pixels,
    patch_owner,
    seq_lengths,
    text_embed,
    cotangent,
    w_stem,
    bn_gain,
    bn_bias,
    w_patch,
    b_patch,
    ln1_gain,
    ln1_bias,
    w_qkv,
    w_out,
    b_out,
    ln2_gain,
    ln2_bias,
    w_up,
    b_up,
    w_down,
    b_down,
):
    groups = lax.axis_size("dp")
    assert lax.axis_size("mp") == 4
    near, far = bits_of("mp")
    bits = bits_of("dp")
    count, pix = pixels.shape
    rows, width = text_embed.shape
    channels = w_stem.shape[1]
    local = w_out.shape[0]
    units = w_up.shape[1]
    capacity = count // groups
    slots = groups * capacity
    idx = jnp.stack([lax.axis_index("dp"), lax.axis_index("mp")]).astype(i32)
    bn_gain, bn_bias, b_patch, ln1_gain, ln1_bias, b_out, ln2_gain, ln2_bias, b_up, b_down = (
        v.reshape(1, -1)
        for v in (
            bn_gain,
            bn_bias,
            b_patch,
            ln1_gain,
            ln1_bias,
            b_out,
            ln2_gain,
            ln2_bias,
            b_up,
            b_down,
        )
    )

    pixel_slots, slot, dest, info = call(
        functools.partial(slots_kernel, groups),
        "slots",
        [((slots, pix), bf16), ((1, count), i32), ((1, slots), i32), ((8, 128), f32)],
        idx,
        patch_owner.reshape(groups, count),
        pixels,
    )
    arrived = lax.all_to_all(
        pixel_slots.reshape(groups, capacity, pix), "dp", split_axis=0, concat_axis=0, tiled=True
    ).reshape(slots, pix)
    own_qkv = jnp.swapaxes(w_qkv, 1, 2).reshape(3 * local, width)
    far_qkv = swap(own_qkv, "mp", far)
    far_out = swap(w_out, "mp", far)
    (stats,) = call(stats_kernel, "stats", [((3, channels), f32)], idx, info, pixels, w_stem)
    for step in bits:
        stats = stats + swap(stats, "dp", step)
    grad_low, grad_act, down_sum = call(
        early_kernel,
        "early",
        [((rows, width), bf16), ((rows, units), f32), ((1, width), f32)],
        idx,
        cotangent,
        w_down,
    )
    centred, normal, stem_act, slope, x_rows, a_low = call(
        stem_kernel,
        "stem",
        [
            ((count, pix), bf16),
            ((count, channels), f32),
            ((count, channels), bf16),
            ((count, channels), f32),
            ((rows, width), f32),
            ((rows, width), bf16),
        ],
        idx,
        info,
        dest,
        arrived,
        stats,
        w_stem,
        bn_gain,
        bn_bias,
        w_patch,
        b_patch,
        text_embed,
        ln1_gain,
        ln1_bias,
    )
    head_shapes = [((rows, local), bf16)] * 4
    q_own, k_own, v_own, merged, attn = call(
        attention_kernel,
        "attention_own",
        head_shapes + [((rows, width), f32)],
        idx,
        info,
        seq_lengths,
        a_low,
        own_qkv,
        w_out,
    )
    q_far, k_far, v_far, _, attn = call(
        attention_kernel,
        "attention_far",
        head_shapes + [((rows, width), bf16)],
        idx,
        info,
        seq_lengths,
        a_low,
        far_qkv,
        far_out,
        attn,
    )
    attn_got = swap(attn, "mp", near)
    half = (rows // 2, width)
    hidden, b_low, act, grad_mid, keep, send, up_sum = call(
        mlp_kernel,
        "mlp",
        [
            ((rows, width), f32),
            ((rows, width), bf16),
            ((rows, units), bf16),
            ((rows, units), bf16),
            (half, bf16),
            (half, bf16),
            ((1, units), f32),
        ],
        idx,
        x_rows,
        attn,
        attn_got,
        b_out,
        ln2_gain,
        ln2_bias,
        w_up,
        b_up,
        grad_act,
    )
    grad_b_mine, grad_b_other, grad_b_first = sum_mp(idx, keep, send)

    ascending = bits
    turned_order = bits[1:] + bits[:1]
    down_steps = plan(ascending, units)
    up_steps = plan(turned_order, width)
    down_keep, down_send, up_keep, up_send = call(
        functools.partial(mlp_grads_kernel, (down_steps[0][0], up_steps[0][0])),
        "mlp_grads",
        [((units // 2, width), bf16)] * 2 + [((width // 2, units), bf16)] * 2,
        idx,
        b_low,
        act,
        grad_mid,
        grad_low,
        cost=3,
        after=[grad_b_first],
    )
    down_pieces = gather(idx, scatter_sum(idx, down_keep, down_send, down_steps), down_steps)
    up_pieces = gather(idx, scatter_sum(idx, up_keep, up_send, up_steps), up_steps)
    keep, send = call(
        down_kernel, "down", [(half, bf16)] * 2, idx, act, w_down, after=[down_keep], cost=1
    )
    late_after = [keep]
    down_mine, down_other, _ = sum_mp(idx, keep, send)
    (output,) = call(
        output_kernel, "output", [((rows, width), f32)], idx, hidden, down_mine, down_other, b_down
    )

    grad_hidden, hidden_low, grad_own, grad_far, late_sums = call(
        hidden_back_kernel,
        "hidden_back",
        [
            ((rows, width), f32),
            ((rows, width), bf16),
            ((rows, local), bf16),
            ((rows, local), bf16),
            ((3, width), f32),
        ],
        idx,
        grad_b_mine,
        grad_b_other,
        cotangent,
        hidden,
        ln2_gain,
        w_out,
        far_out,
        cost=3,
        after=late_after,
    )
    grad_qkv, grad_a = call(
        attention_back_kernel,
        "attention_back_own",
        [((3, rows, local), bf16), ((rows, width), f32)],
        idx,
        info,
        seq_lengths,
        q_own,
        k_own,
        v_own,
        grad_own,
        own_qkv,
    )
    _, grad_a = call(
        attention_back_kernel,
        "attention_back_far",
        [((3, rows, local), bf16), ((rows, width), bf16)],
        idx,
        info,
        seq_lengths,
        q_far,
        k_far,
        v_far,
        grad_far,
        far_qkv,
        grad_a,
    )
    grad_a_got = swap(grad_a, "mp", near)
    heads_steps = plan(ascending, 4 * local)
    keep, send = call(
        functools.partial(attention_grads_kernel, heads_steps[0][0]),
        "attention_grads",
        [((2 * local, width), bf16)] * 2,
        idx,
        grad_qkv,
        a_low,
        merged,
        hidden_low,
    )
    heads_pieces = gather(idx, scatter_sum(idx, keep, send, heads_steps), heads_steps)

    grad_text, grad_embed, grad_zed, small = call(
        text_back_kernel,
        "text_back",
        [
            ((rows, width), f32),
            ((count, width), bf16),
            ((count, channels), f32),
            ((10, channels), f32),
        ],
        idx,
        info,
        grad_a,
        grad_a_got,
        grad_hidden,
        x_rows,
        ln1_gain,
        normal,
        slope,
        w_patch,
        late_sums,
        up_sum,
        down_sum,
    )
    for step in bits:
        small = small + swap(small, "dp", step)
    part = channels // 4
    stem_steps = plan(ascending, part)
    half_part = ((part // 2, width), bf16)
    keep, send = call(
        functools.partial(patch_grad_kernel, stem_steps[0][0]),
        "patch_grad",
        [half_part] * 2,
        idx,
        stem_act,
        grad_embed,
    )
    patch_pieces = gather(idx, scatter_sum(idx, keep, send, stem_steps), stem_steps)
    keep, send, grad_pre = call(
        functools.partial(stem_back_kernel, stem_steps[0][0]),
        "stem_back",
        [half_part] * 2 + [((count, channels), bf16)],
        idx,
        info,
        stats,
        small,
        bn_gain,
        grad_zed,
        normal,
        centred,
    )
    stem_pieces = gather(idx, scatter_sum(idx, keep, send, stem_steps), stem_steps)
    (row_slots,) = call(
        pixel_back_kernel, "pixel_back", [((slots, pix), bf16)], idx, dest, grad_pre, w_stem
    )
    returned = lax.all_to_all(
        row_slots.reshape(groups, capacity, pix), "dp", split_axis=0, concat_axis=0, tiled=True
    ).reshape(slots, pix)
    (grad_pixels,) = call(pixel_kernel, "pixel", [((count, pix), f32)], idx, slot, returned)

    (grad_w_down,) = call(
        functools.partial(widen_kernel, down_steps), "wide_down", [((units, width), f32)], idx, *down_pieces
    )
    (grad_w_up,) = call(
        functools.partial(widen_kernel, up_steps), "wide_up", [((width, units), f32)], idx, *up_pieces
    )
    grad_w_qkv, grad_w_out = call(
        functools.partial(widen_heads_kernel, heads_steps),
        "wide_heads",
        [((3 * local, width), f32), ((local, width), f32)],
        idx,
        *heads_pieces,
        scratch=[pltpu.VMEM((4 * local, width), f32)],
    )
    grad_w_qkv = jnp.swapaxes(grad_w_qkv.reshape(3, local, width), 1, 2)
    stem_whole = []
    for name, pieces in (("patch", patch_pieces), ("stem", stem_pieces)):
        (whole,) = call(
            functools.partial(widen_kernel, stem_steps),
            "join_" + name,
            [((part, width), bf16)],
            idx,
            *pieces,
        )
        stem_whole.append(gather_mp(idx, "wide_" + name, whole, name == "stem"))
    grad_w_patch, grad_w_stem = stem_whole
    return (
        output,
        grad_pixels,
        grad_text,
        grad_w_stem,
        small[0],
        small[1],
        grad_w_patch,
        small[2, :width],
        small[3, :width],
        small[4, :width],
        grad_w_qkv,
        grad_w_out,
        small[5, :width],
        small[6, :width],
        small[7, :width],
        grad_w_up,
        small[8, :units],
        grad_w_down,
        small[9, :width],
    )


def solution(mesh):
    in_specs = (
        P("dp", None),
        P(),
        P("dp", None),
        P("dp", None),
        P("dp", None),
        P(),
        P(),
        P(),
        P(),
        P(),
        P(),
        P(),
        P(None, None, "mp"),
        P("mp", None),
        P(),
        P(),
        P(),
        P(None, "mp"),
        P("mp"),
        P("mp", None),
        P(),
    )
    out_specs = (
        P("dp", None),
        P("dp", None),
        P("dp", None),
        P(),
        P(),
        P(),
        P(),
        P(),
        P(),
        P(),
        P(None, None, "mp"),
        P("mp", None),
        P(),
        P(),
        P(),
        P(None, "mp"),
        P("mp"),
        P("mp", None),
        P(),
    )
    return jax.shard_map(shards, mesh=mesh, in_specs=in_specs, out_specs=out_specs, check_vma=False)
```

```python
import functools

import jax
import jax.numpy as jnp
from jax import lax
from jax.experimental import pallas as pl
from jax.experimental.pallas import tpu as pltpu
from jax.sharding import PartitionSpec as P

HEAD = 64
BLK = 256
SCALE = HEAD ** (-0.5)

norm_eps = 1e-05
masked_score = -1e30
f32 = jnp.float32
bf16 = jnp.bfloat16
i32 = jnp.int32


def dot(left, right):
    return lax.dot_general(left, right, (((1,), (0,)), ((), ())), preferred_element_type=f32)


def dot_tn(left, right):
    return lax.dot_general(left, right, (((0,), (0,)), ((), ())), preferred_element_type=f32)


def dot_nt(left, right):
    return lax.dot_general(left, right, (((1,), (1,)), ((), ())), preferred_element_type=f32)


def iota(shape, dim):
    return lax.broadcasted_iota(i32, shape, dim)


def gelu_parts(values):
    cdf = 0.5 * (1.0 + lax.erf(values * (0.5**0.5)))
    pdf = jnp.exp(-0.5 * values * values) * 0.3989422804014327
    return cdf, cdf + values * pdf


def normed(values):
    center = values - jnp.mean(values, axis=-1, keepdims=True)
    inv_std = lax.rsqrt(jnp.mean(center * center, axis=-1, keepdims=True) + norm_eps)
    return center * inv_std, inv_std


def norm_back(grad_out, normal, inv_std, gain):
    scaled = grad_out * gain
    return inv_std * (
        scaled
        - jnp.mean(scaled, axis=-1, keepdims=True)
        - normal * jnp.mean(scaled * normal, axis=-1, keepdims=True)
    )


def col_sum(values):
    return jnp.sum(values, axis=0, keepdims=True)


VMEM = pl.BlockSpec(memory_space=pltpu.VMEM)
SMEM = pl.BlockSpec(memory_space=pltpu.SMEM)
ANY = pl.BlockSpec(memory_space=pl.ANY)
PER_US = 1e10
HEAD_ROWS = 16


class Order:
    last = ()


def call(kernel, name, outs, *args, scratch=(), cost=1.0):
    shapes = [jax.ShapeDtypeStruct(s, t) for s, t in outs]
    first = len(args)
    after = Order.last

    def body(*refs):
        kernel(*refs[:first], *refs[first + len(after) :])

    results = pl.pallas_call(
        body,
        name=name,
        out_shape=shapes,
        in_specs=[SMEM] + [VMEM] * (first - 1) + [ANY] * len(after),
        out_specs=[VMEM] * len(outs),
        scratch_shapes=list(scratch),
        compiler_params=pltpu.CompilerParams(vmem_limit_bytes=20 << 20),
        cost_estimate=pl.CostEstimate(
            flops=int(cost * PER_US), bytes_accessed=0, transcendentals=0
        ),
    )(*args, *after)
    Order.last = (min(results, key=lambda r: r.size * r.dtype.itemsize),)
    return results


def bits_of(axis):
    size = lax.axis_size(axis)
    bits = []
    step = 1
    while step < size:
        bits.append(step)
        step *= 2
    assert step == size
    return bits


def swap(values, axis, step):
    size = lax.axis_size(axis)
    return lax.ppermute(values, axis, [(i, i ^ step) for i in range(size)])


def put_half(keep_ref, send_ref, top, start, value):
    half = keep_ref.shape[0]
    at = pl.ds(start % half, value.shape[0])
    mine = top == (start // half)

    @pl.when(mine)
    def _():
        keep_ref[at] = value.astype(keep_ref.dtype)

    @pl.when(jnp.logical_not(mine))
    def _():
        send_ref[at] = value.astype(send_ref.dtype)


def bit_set(idx_ref, which, step):
    return (idx_ref[which] // step) % 2


def plan(order, rows):
    steps = []
    for step in order:
        cut = rows % 32 == 0
        rows = rows // 2 if cut else rows
        steps.append((step, cut))
    return steps


def add_split_kernel(step, idx_ref, keep_ref, got_ref, next_ref, send_ref):
    top = bit_set(idx_ref, 0, step)
    half = next_ref.shape[0]
    for part in range(2):
        at = pl.ds(part * half, half)
        total = keep_ref[at].astype(f32) + got_ref[at].astype(f32)
        put_half(next_ref, send_ref, top, part * half, total)


def add_kernel(idx_ref, keep_ref, got_ref, out_ref):
    out_ref[...] = (keep_ref[...].astype(f32) + got_ref[...].astype(f32)).astype(out_ref.dtype)


def add(idx, keep, got):
    return call(add_kernel, "add", [(keep.shape, keep.dtype)], idx, keep, got)[0]


def join_kernel(idx_ref, *refs):
    out_ref = refs[-1]
    start = 0
    for ref in refs[:-1]:
        out_ref[pl.ds(start, ref.shape[0])] = ref[...]
        start += ref.shape[0]


def join(idx, pieces):
    if len(pieces) == 1:
        return pieces[0]
    rows = sum(p.shape[0] for p in pieces)
    outs = [((rows, pieces[0].shape[1]), pieces[0].dtype)]
    return call(join_kernel, "join", outs, idx, *pieces, cost=0.5)[0]


class Gather:
    def __init__(self, idx, piece, steps):
        self.idx, self.pieces = idx, [piece]
        self.back = [step for step, cut in reversed(steps) if cut]
        self.send(piece)

    def send(self, held):
        self.pieces.append(swap(held, "dp", self.back[len(self.pieces) - 1]))

    def advance(self):
        if len(self.pieces) <= len(self.back):
            self.send(join(self.idx, self.pieces))
            return True
        return False

    def finish(self):
        while self.advance():
            pass
        return self.pieces


class AllReduce:
    def __init__(self, idx, keep, send, steps):
        self.idx, self.steps, self.gather = idx, steps, None
        self.keep, self.at = keep, 0
        self.got = swap(send, "dp", steps[0][0])

    def scatter(self):
        idx, at = self.idx, self.at + 1
        if at == len(self.steps):
            return add(idx, self.keep, self.got)
        step, cut = self.steps[at]
        self.at = at
        if cut:
            half = (self.keep.shape[0] // 2, self.keep.shape[1])
            self.keep, send = call(
                functools.partial(add_split_kernel, step),
                "add_split",
                [(half, self.keep.dtype)] * 2,
                idx,
                self.keep,
                self.got,
            )
        else:
            self.keep = send = add(idx, self.keep, self.got)
        self.got = swap(send, "dp", step)
        return None

    def last(self):
        while self.at + 1 < len(self.steps):
            self.scatter()
        return self.keep, self.got

    def advance(self):
        if self.gather is not None:
            return self.gather.advance()
        piece = self.scatter()
        if piece is not None:
            self.gather = Gather(self.idx, piece, self.steps)
        return True

    def finish(self):
        while self.advance():
            pass
        return self.gather.pieces


def place_pieces(idx_ref, piece_refs, steps, store):
    cuts = [step for step, cut in steps if cut]
    rows = piece_refs[0].shape[0]
    total = rows << len(cuts)
    back = list(reversed(cuts))
    count = 0
    for ref in piece_refs:
        for start in range(0, ref.shape[0], rows):
            row = 0
            size = total
            for step in cuts:
                size //= 2
                flip = (count >> back.index(step)) & 1
                bit = bit_set(idx_ref, 0, step)
                row = row + (1 - bit if flip else bit) * size
            store(pl.multiple_of(row, rows), ref[pl.ds(start, rows)])
            count += 1


def per_group(shape, dim, stride):
    at = iota(shape, dim)
    group = jnp.floor((at.astype(f32) + 0.5) * (1.0 / stride)).astype(i32)
    return group, at - group * stride


def first_kernel(
    groups, idx_ref, owner_ref, pixel_ref, w_stem_ref, send_ref, slot_ref, dest_ref, info_ref, sums_ref
):
    count, pix = pixel_ref.shape
    half = pix // 2
    slots = send_ref.shape[0]
    stride = slots // groups
    core = bit_set(idx_ref, 1, 1)
    table = owner_ref[...]
    own = owner_ref[pl.ds(idx_ref[0], 1), :]
    own_live = jnp.sum((own < groups).astype(f32), axis=1, keepdims=True).astype(i32)
    low = pixel_ref[...].astype(bf16)
    live_low = jnp.where(iota((count, 1), 0) < own_live, low, jnp.zeros((), bf16))
    pre = dot(live_low, w_stem_ref[...])
    value = jnp.where(core == 0, col_sum(pre), col_sum(pre * pre))
    left, right = low[:, :half], low[:, half:]
    mine = jnp.where(core == 0, left, right)
    live_mine = jnp.where(core == 0, live_low[:, :half], live_low[:, half:])
    sums_ref[...] = jnp.zeros(sums_ref.shape, f32)
    for part in range(3):
        rounded = value.astype(bf16).astype(f32)
        for row in range(value.shape[1] // 128):
            sums_ref[row : row + 1, part * 128 : part * 128 + 128] = rounded[
                :, row * 128 : row * 128 + 128
            ]
        value = value - rounded
    value = col_sum(live_mine.astype(f32))
    for part in range(3):
        rounded = value.astype(bf16).astype(f32)
        sums_ref[8 + part : 9 + part] = rounded
        value = value - rounded
    hot = (iota((groups, count), 0) == own).astype(f32)
    before = (iota((count, count), 0) < iota((count, count), 1)).astype(bf16)
    rank = jnp.sum(hot * dot(hot.astype(bf16), before), axis=0, keepdims=True).astype(i32)
    slot = jnp.where(own < groups, own * stride + HEAD_ROWS + rank, -1)
    slot_ref[...] = slot
    pick = (iota((slots, count), 0) == slot).astype(bf16)
    _, place = per_group((slots, HEAD_ROWS), 0, stride)
    spread = (place == iota((slots, HEAD_ROWS), 1)).astype(bf16)
    send_ref[...] = (dot(pick, mine) + dot(spread, sums_ref[...].astype(bf16))).astype(bf16)
    sources = jnp.sum((table == idx_ref[0]).astype(f32), axis=1, keepdims=True)
    lower = (iota((groups, groups), 1) < iota((groups, groups), 0)).astype(bf16)
    starts = dot(lower, jnp.broadcast_to(sources, (groups, 128)).astype(bf16))[:, :1].astype(i32)
    within = iota((groups, slots), 1) - stride * iota((groups, slots), 0) - HEAD_ROWS
    taken = (within >= 0) & (within < sources.astype(i32))
    dest_ref[...] = jnp.max(jnp.where(taken, starts + within, -1), axis=0, keepdims=True)
    prefix = jnp.sum(sources, axis=0, keepdims=True)
    live = jnp.sum((table < groups).astype(f32), axis=1, keepdims=True)
    live_total = jnp.sum(live, axis=0, keepdims=True)
    info_ref[...] = jnp.where(iota(info_ref.shape, 0) == 0, prefix, live_total)


def gathered_sums(ref, groups):
    slots = ref.shape[0]
    _, place = per_group((HEAD_ROWS, slots), 1, slots // groups)
    collect = (place == iota((HEAD_ROWS, slots), 0)).astype(bf16)
    total = dot(collect, ref[...])
    value = total[:8, :128] + total[:8, 128:256] + total[:8, 256:384]
    pixel_sum = total[8:9] + total[9:10] + total[10:11]
    return jnp.concatenate([value[row : row + 1] for row in range(8)], axis=1), pixel_sum


def early_kernel(idx_ref, cot_ref, w_down_ref, low_ref, act_ref, sum_ref):
    total = jnp.zeros(sum_ref.shape, f32)
    for start in range(0, cot_ref.shape[0], BLK):
        at = pl.ds(start, BLK)
        cot = cot_ref[at]
        low = cot.astype(bf16)
        low_ref[at] = low
        act_ref[at] = dot_nt(low, w_down_ref[...])
        total = total + col_sum(cot)
    sum_ref[...] = total


def stem_kernel(
    groups,
    idx_ref,
    info_ref,
    dest_ref,
    mine_ref,
    other_ref,
    w_stem_ref,
    bn_gain_ref,
    bn_bias_ref,
    w_patch_ref,
    b_patch_ref,
    text_ref,
    ln1_gain_ref,
    ln1_bias_ref,
    centred_ref,
    normal_ref,
    act_ref,
    slope_ref,
    x_ref,
    a_low_ref,
    mean_ref,
    inv_ref,
    low_ref,
):
    count, pix = centred_ref.shape
    slots = mine_ref.shape[0]
    prefix = info_ref[0:1, :1].astype(i32)
    total = info_ref[1:2, :1]
    core = bit_set(idx_ref, 1, 1)
    sums, pixel_sums = zip(gathered_sums(mine_ref, groups), gathered_sums(other_ref, groups), strict=True)
    first, second = jnp.where(core == 0, sums[0], sums[1]), jnp.where(core == 0, sums[1], sums[0])
    mean = first / total
    inv = lax.rsqrt(second / total - mean * mean + norm_eps)
    mean_ref[...] = mean
    inv_ref[...] = inv
    halves = [
        (
            jnp.where(core == at, mine_ref[...], other_ref[...]),
            jnp.where(core == at, pixel_sums[0], pixel_sums[1]) / total,
        )
        for at in range(2)
    ]
    for start, size in stem_blocks(count, text_ref.shape[0]):
        at = pl.ds(start, size)
        x = text_ref[at]
        if start < count:
            place = (iota((size, slots), 0) + start == dest_ref[...]).astype(bf16)
            for side, (half_rows, half_mean) in enumerate(halves):
                packed = dot(place, half_rows)
                columns = pl.ds(side * (pix // 2), pix // 2)
                low_ref[at, columns] = packed.astype(bf16)
                centred_ref[at, columns] = (packed - half_mean).astype(bf16)
            normal = (dot(low_ref[at], w_stem_ref[...]) - mean) * inv
            normal_ref[at] = normal
            bn_out = normal * bn_gain_ref[...][None, :] + bn_bias_ref[...][None, :]
            cdf, slope = gelu_parts(bn_out)
            slope_ref[at] = slope
            act = (bn_out * cdf).astype(bf16)
            act_ref[at] = act
            embedded = (dot(act, w_patch_ref[...]) + b_patch_ref[...][None, :]).astype(bf16)
            here = iota((size, 1), 0) + start < prefix
            x = x + jnp.where(here, embedded.astype(f32), 0.0)
        x_ref[at] = x
        normal_one, _ = normed(x)
        a_low_ref[at] = (normal_one * ln1_gain_ref[...][None, :] + ln1_bias_ref[...][None, :]).astype(bf16)


def stem_blocks(count, rows):
    half = count // 2
    return [(0, half), (half, half)] + ([(count, rows - count)] if rows > count else [])


def segments(seq_ref, shape, dim):
    rows = iota(shape, dim)
    end = jnp.zeros((1, 1), i32)
    segment = jnp.zeros(shape, i32)
    for at in range(seq_ref.shape[1]):
        end = end + seq_ref[0:1, at : at + 1]
        segment = segment + (end <= rows).astype(i32)
    return segment


def head_lanes(width, head):
    lane = iota((1, width), 1)
    return (lane >= head * HEAD) & (lane < (head + 1) * HEAD)


def attention_kernel(
    idx_ref,
    info_ref,
    seq_ref,
    a_low_ref,
    w_qkv_ref,
    w_out_ref,
    *refs,
):
    base_ref = refs[0] if len(refs) == 6 else None
    q_ref, k_ref, v_ref, merged_ref, out_ref = refs[-5:]
    rows = a_low_ref.shape[0]
    width = w_out_ref.shape[0]
    low = a_low_ref[...]
    for t, (ref, scale) in enumerate(((q_ref, SCALE), (k_ref, 1.0), (v_ref, 1.0))):
        part = dot_nt(low, w_qkv_ref[pl.ds(t * width, width)])
        ref[...] = (part * scale if scale != 1.0 else part).astype(bf16)
    prefix = info_ref[0:1, :1].astype(i32)
    key_rows, query_rows = iota((rows, rows), 1), iota((rows, rows), 0)
    visible = (segments(seq_ref, (rows, 1), 0) == segments(seq_ref, (1, rows), 1)) & (
        (key_rows <= query_rows) | (key_rows < prefix)
    )
    bias = jnp.where(visible, 0.0, masked_score)
    zero = jnp.zeros((), bf16)
    merged = jnp.zeros((rows, width), f32)
    for head in range(width // HEAD):
        mask = head_lanes(width, head)
        scores = dot_nt(jnp.where(mask, q_ref[...], zero), k_ref[...]) + bias
        weights = jnp.exp(scores - jnp.max(scores, axis=-1, keepdims=True))
        share = 1.0 / jnp.sum(weights, axis=-1, keepdims=True)
        merged = jnp.where(mask, dot(weights.astype(bf16), v_ref[...]) * share, merged)
    merged = merged.astype(bf16)
    merged_ref[...] = merged
    part = dot(merged, w_out_ref[...])
    if base_ref is not None:
        part = part + base_ref[...]
    out_ref[...] = part.astype(out_ref.dtype)


def mlp_kernel(
    idx_ref,
    x_ref,
    part_ref,
    got_ref,
    b_out_ref,
    ln2_gain_ref,
    ln2_bias_ref,
    w_up_ref,
    b_up_ref,
    grad_act_ref,
    hidden_ref,
    b_low_ref,
    act_ref,
    grad_mid_ref,
    keep_ref,
    send_ref,
    sum_ref,
):
    top = bit_set(idx_ref, 1, 1)
    total = jnp.zeros(sum_ref.shape, f32)
    for start in range(0, x_ref.shape[0], BLK):
        at = pl.ds(start, BLK)
        attn = part_ref[at].astype(f32) + got_ref[at].astype(f32)
        hidden = x_ref[at] + attn + b_out_ref[...][None, :]
        hidden_ref[at] = hidden
        normal, _ = normed(hidden)
        b_low = (normal * ln2_gain_ref[...][None, :] + ln2_bias_ref[...][None, :]).astype(bf16)
        b_low_ref[at] = b_low
        middle = dot(b_low, w_up_ref[...]) + b_up_ref[...][None, :]
        cdf, slope = gelu_parts(middle)
        act_ref[at] = (middle * cdf).astype(bf16)
        grad_mid = (slope * grad_act_ref[at]).astype(bf16)
        grad_mid_ref[at] = grad_mid
        total = total + col_sum(grad_mid.astype(f32))
        put_half(keep_ref, send_ref, top, start, dot_nt(grad_mid, w_up_ref[...]))
    sum_ref[...] = total


def mlp_grads_kernel(
    steps,
    idx_ref,
    b_low_ref,
    act_ref,
    grad_mid_ref,
    grad_low_ref,
    down_keep_ref,
    down_send_ref,
    up_keep_ref,
    up_send_ref,
):
    for step, left, right, keep, send in (
        (steps[0], act_ref, grad_low_ref, down_keep_ref, down_send_ref),
        (steps[1], b_low_ref, grad_mid_ref, up_keep_ref, up_send_ref),
    ):
        top = bit_set(idx_ref, 0, step)
        half = keep.shape[0]
        for start in (0, half):
            put_half(keep, send, top, start, dot_tn(left[:, pl.ds(start, half)], right[...]))


def down_kernel(idx_ref, act_ref, w_down_ref, keep_ref, send_ref):
    top = bit_set(idx_ref, 1, 1)
    for start in range(0, act_ref.shape[0], BLK):
        put_half(keep_ref, send_ref, top, start, dot(act_ref[pl.ds(start, BLK)], w_down_ref[...]))


def output_kernel(idx_ref, hidden_ref, mine_ref, other_ref, b_down_ref, out_ref):
    top = bit_set(idx_ref, 1, 1)
    half = mine_ref.shape[0]
    for start in range(0, hidden_ref.shape[0], BLK):
        at = pl.ds(start, BLK)
        down = pick_half(mine_ref, other_ref, top, start, half)
        out_ref[at] = hidden_ref[at] + down + b_down_ref[...][None, :]


def pick_half(mine_ref, other_ref, top, start, half):
    at = pl.ds(start % half, BLK)
    mine = top == (start // half)
    return jnp.where(mine, mine_ref[at].astype(f32), other_ref[at].astype(f32))


def hidden_back_kernel(
    idx_ref,
    mine_ref,
    other_ref,
    cot_ref,
    hidden_ref,
    ln2_gain_ref,
    w_out_own_ref,
    w_out_far_ref,
    grad_hidden_ref,
    low_ref,
    own_ref,
    far_ref,
    sums_ref,
):
    top = bit_set(idx_ref, 1, 1)
    half = mine_ref.shape[0]
    width = cot_ref.shape[1]
    sums = [jnp.zeros((1, width), f32)] * 3
    for start in range(0, cot_ref.shape[0], BLK):
        at = pl.ds(start, BLK)
        grad = pick_half(mine_ref, other_ref, top, start, half)
        normal, inv = normed(hidden_ref[at])
        grad_hidden = cot_ref[at] + norm_back(grad, normal, inv, ln2_gain_ref[...][None, :])
        grad_hidden_ref[at] = grad_hidden
        low = grad_hidden.astype(bf16)
        low_ref[at] = low
        own_ref[at] = dot_nt(low, w_out_own_ref[...]).astype(bf16)
        far_ref[at] = dot_nt(low, w_out_far_ref[...]).astype(bf16)
        sums = [
            sums[0] + col_sum(grad_hidden),
            sums[1] + col_sum(grad * normal),
            sums[2] + col_sum(grad),
        ]
    for at in range(3):
        sums_ref[at : at + 1] = sums[at]


def attention_back_kernel(
    idx_ref,
    info_ref,
    seq_ref,
    q_ref,
    k_ref,
    v_ref,
    grad_ref,
    w_qkv_ref,
    *refs,
):
    base_ref = refs[0] if len(refs) == 3 else None
    grad_qkv_ref, out_ref = refs[-2:]
    rows, width = q_ref.shape
    prefix = info_ref[0:1, :1].astype(i32)
    zero = jnp.zeros((), bf16)
    key_rows, query_rows = iota((rows, rows), 0), iota((rows, rows), 1)
    visible = (segments(seq_ref, (rows, 1), 0) == segments(seq_ref, (1, rows), 1)) & (
        (key_rows <= query_rows) | (key_rows < prefix)
    )
    bias = jnp.where(visible, 0.0, masked_score)
    grad_values = jnp.zeros((rows, width), f32)
    grad_keys = jnp.zeros((rows, width), f32)
    grad_queries = jnp.zeros((rows, width), f32)
    for head in range(width // HEAD):
        mask = head_lanes(width, head)
        query = jnp.where(mask, q_ref[...], zero)
        grad = jnp.where(mask, grad_ref[...], zero)
        scores = dot_nt(k_ref[...], query) + bias
        weights = jnp.exp(scores - jnp.max(scores, axis=0, keepdims=True))
        probs = weights * (1.0 / jnp.sum(weights, axis=0, keepdims=True))
        grad_weights = dot_nt(v_ref[...], grad)
        delta = jnp.sum(probs * grad_weights, axis=0, keepdims=True)
        grad_scores = (probs * (grad_weights - delta)).astype(bf16)
        grad_values = grad_values + dot(probs.astype(bf16), grad)
        grad_keys = grad_keys + dot(grad_scores, query)
        grad_queries = jnp.where(mask, dot_tn(grad_scores, k_ref[...]), grad_queries)
    total = jnp.zeros((rows, w_qkv_ref.shape[1]), f32)
    for t, value in enumerate((grad_queries * SCALE, grad_keys, grad_values)):
        low = value.astype(bf16)
        grad_qkv_ref[t] = low
        total = total + dot(low, w_qkv_ref[pl.ds(t * width, width)])
    if base_ref is not None:
        total = total + base_ref[...]
    out_ref[...] = total.astype(out_ref.dtype)


def text_back_kernel(
    idx_ref,
    info_ref,
    part_ref,
    got_ref,
    grad_hidden_ref,
    x_ref,
    ln1_gain_ref,
    normal_ref,
    slope_ref,
    w_patch_ref,
    late_ref,
    up_sum_ref,
    down_sum_ref,
    grad_text_ref,
    embed_ref,
    zed_ref,
    small_ref,
):
    count, channels = normal_ref.shape
    width = x_ref.shape[1]
    prefix = info_ref[0:1, :1].astype(i32)
    bn_sums = [jnp.zeros((1, channels), f32)] * 2
    sums = [jnp.zeros((1, width), f32)] * 3
    for start, size in stem_blocks(count, x_ref.shape[0]):
        at = pl.ds(start, size)
        grad = part_ref[at].astype(f32) + got_ref[at].astype(f32)
        normal, inv = normed(x_ref[at])
        grad_text = grad_hidden_ref[at] + norm_back(grad, normal, inv, ln1_gain_ref[...][None, :])
        grad_text_ref[at] = grad_text
        sums[1] = sums[1] + col_sum(grad * normal)
        sums[2] = sums[2] + col_sum(grad)
        if start < count:
            here = iota((size, 1), 0) + start < prefix
            embed = jnp.where(here, grad_text, 0.0).astype(bf16)
            embed_ref[at] = embed
            sums[0] = sums[0] + col_sum(embed.astype(f32))
            zed = slope_ref[at] * dot_nt(embed, w_patch_ref[...])
            zed_ref[at] = zed
            bn_sums = [bn_sums[0] + col_sum(zed * normal_ref[at]), bn_sums[1] + col_sum(zed)]
    small_ref[...] = jnp.zeros(small_ref.shape, f32)
    small_ref[0:1] = bn_sums[0]
    small_ref[1:2] = bn_sums[1]
    for at in range(3):
        small_ref[2 + at : 3 + at, :width] = sums[at]
    small_ref[5:8, :width] = late_ref[...]
    small_ref[8:9, : up_sum_ref.shape[1]] = up_sum_ref[...]
    small_ref[9:10, :width] = down_sum_ref[...]


def head_grads_kernel(
    step, idx_ref, grad_qkv_ref, a_low_ref, merged_ref, low_ref, keep_ref, send_ref
):
    top = bit_set(idx_ref, 0, step)
    width = merged_ref.shape[1]
    for t in range(3):
        put_half(keep_ref, send_ref, top, t * width, dot_tn(grad_qkv_ref[t], a_low_ref[...]))
    put_half(keep_ref, send_ref, top, 3 * width, dot_tn(merged_ref[...], low_ref[...]))


def cross_kernel(step, idx_ref, info_ref, normal_ref, centred_ref, keep_ref, send_ref):
    top = bit_set(idx_ref, 0, step)
    half = keep_ref.shape[0]
    first = idx_ref[1] * (2 * half)
    here = iota((normal_ref.shape[0], 1), 0) < info_ref[0:1, :1].astype(i32)
    for part in range(2):
        columns = pl.ds(pl.multiple_of(first + part * half, half), half)
        normal = jnp.where(here, normal_ref[:, columns], 0.0).astype(bf16)
        put_half(keep_ref, send_ref, top, part * half, dot_tn(normal, centred_ref[...]))


def part_grads_kernel(
    step, idx_ref, act_ref, embed_ref, zed_ref, centred_ref, keep_ref, send_ref
):
    top = bit_set(idx_ref, 0, step)
    half = keep_ref.shape[0]
    first = idx_ref[1] * (2 * half)
    for part in range(2):
        columns = pl.ds(pl.multiple_of(first + part * half, half), half)
        patch = dot_tn(act_ref[:, columns], embed_ref[...])
        stem = dot_tn(zed_ref[:, columns].astype(bf16), centred_ref[...])
        put_half(
            keep_ref, send_ref, top, part * half, jnp.concatenate([patch, stem], axis=1)
        )


def correct_kernel(
    steps,
    idx_ref,
    keep_ref,
    got_ref,
    cross_keep_ref,
    cross_got_ref,
    small_ref,
    inv_ref,
    bn_gain_ref,
    info_ref,
    out_ref,
):
    rows = out_ref.shape[0]
    width = cross_keep_ref.shape[1]
    cuts = [step for step, cut in steps if cut]
    size = rows << len(cuts)
    row = idx_ref[1] * size
    for step in cuts:
        size //= 2
        row = row + bit_set(idx_ref, 0, step) * size
    hot = iota((rows, inv_ref.shape[1]), 1) == iota((rows, inv_ref.shape[1]), 0) + row

    def column(value):
        return jnp.sum(jnp.where(hot, value, 0.0), axis=1, keepdims=True)

    factor = column(inv_ref[...] * bn_gain_ref[...][None, :])
    share = column(small_ref[0:1]) / info_ref[1:2, :1]
    total = keep_ref[...].astype(f32) + got_ref[...].astype(f32)
    cross = cross_keep_ref[...].astype(f32) + cross_got_ref[...].astype(f32)
    out_ref[:, :width] = total[:, :width].astype(out_ref.dtype)
    out_ref[:, width:] = (factor * (total[:, width:] - share * cross)).astype(out_ref.dtype)


def pixel_back_kernel(idx_ref, dest_ref, zed_ref, inv_ref, bn_gain_ref, w_stem_ref, slots_ref):
    slots, half = slots_ref.shape
    place = (iota((zed_ref.shape[0], slots), 0) == dest_ref[...]).astype(bf16)
    core = bit_set(idx_ref, 1, 1)
    weights = w_stem_ref[pl.ds(pl.multiple_of(core * half, half), half)]
    scaled = (zed_ref[...] * (inv_ref[...] * bn_gain_ref[...][None, :])).astype(bf16)
    rows = dot_nt(scaled, weights).astype(bf16)
    slots_ref[...] = dot_tn(place, rows).astype(bf16)


def pixel_rest_kernel(
    groups,
    idx_ref,
    owner_ref,
    info_ref,
    pixel_ref,
    w_stem_ref,
    mean_ref,
    inv_ref,
    bn_gain_ref,
    small_ref,
    out_ref,
):
    own = owner_ref[pl.ds(idx_ref[0], 1), :]
    live = jnp.sum((own < groups).astype(f32), axis=1, keepdims=True).astype(i32)
    total = info_ref[1:2, :1]
    pre = dot(pixel_ref[...].astype(bf16), w_stem_ref[...])
    normal = (pre - mean_ref[...]) * inv_ref[...]
    factor = inv_ref[...] * bn_gain_ref[...][None, :]
    rest = factor * (small_ref[1:2] / total + normal * (small_ref[0:1] / total))
    rest = jnp.where(iota((pixel_ref.shape[0], 1), 0) < live, rest, 0.0)
    out_ref[...] = dot_nt(rest.astype(bf16), w_stem_ref[...])


def pixel_kernel(idx_ref, slot_ref, mine_ref, other_ref, rest_ref, out_ref):
    slots, half = mine_ref.shape
    pick = (iota((slots, out_ref.shape[0]), 0) == slot_ref[...]).astype(bf16)
    core = bit_set(idx_ref, 1, 1)
    for side in range(2):
        value = jnp.where(core == side, mine_ref[...], other_ref[...])
        columns = slice(side * half, (side + 1) * half)
        out_ref[:, columns] = dot_tn(pick, value) - rest_ref[:, columns]


def widen_kernel(steps, idx_ref, *refs):
    out_ref = refs[-1]

    def store(row, value):
        out_ref[pl.ds(row, value.shape[0])] = value.astype(out_ref.dtype)

    place_pieces(idx_ref, refs[:-1], steps, store)


def widen_heads_kernel(steps, idx_ref, *refs):
    qkv_ref, out_ref, held_ref = refs[-3:]

    def store(row, value):
        held_ref[pl.ds(row, value.shape[0])] = value.astype(f32)

    place_pieces(idx_ref, refs[:-3], steps, store)
    start = 0
    for ref in (qkv_ref, out_ref):
        ref[...] = held_ref[pl.ds(start, ref.shape[0])].astype(ref.dtype)
        start += ref.shape[0]


def gather_mp_kernel(idx_ref, own_ref, far_ref, near_ref, patch_ref, stem_ref):
    part, wide = own_ref.shape
    width = wide // 2
    for flip, value in (
        (0, own_ref[...]),
        (2, far_ref[...]),
        (1, near_ref[pl.ds(0, part)]),
        (3, near_ref[pl.ds(part, part)]),
    ):
        at = bit_set(idx_ref, 1, 1) ^ (flip & 1)
        at = at + 2 * (bit_set(idx_ref, 1, 2) ^ (flip >> 1))
        place = pl.ds(pl.multiple_of(at * part, part), part)
        patch_ref[place] = value[:, :width].astype(f32)
        stem_ref[:, place] = value[:, width:].astype(f32).T


def shards(
    pixels,
    patch_owner,
    seq_lengths,
    text_embed,
    cotangent,
    w_stem,
    bn_gain,
    bn_bias,
    w_patch,
    b_patch,
    ln1_gain,
    ln1_bias,
    w_qkv,
    w_out,
    b_out,
    ln2_gain,
    ln2_bias,
    w_up,
    b_up,
    w_down,
    b_down,
):
    groups = lax.axis_size("dp")
    assert lax.axis_size("mp") == 4
    near, far = bits_of("mp")
    bits = bits_of("dp")
    count, pix = pixels.shape
    rows, width = text_embed.shape
    channels = w_stem.shape[1]
    local = w_out.shape[0]
    units = w_up.shape[1]
    capacity = count // groups
    idx = jnp.stack([lax.axis_index("dp"), lax.axis_index("mp")]).astype(i32)

    Order.last = ()
    stride = HEAD_ROWS + capacity
    slots = groups * stride
    half_pix = pix // 2
    own_qkv = jnp.swapaxes(w_qkv, 1, 2).reshape(3 * local, width)
    far_qkv = swap(own_qkv, "mp", far)
    far_out = swap(w_out, "mp", far)
    owners = patch_owner.reshape(groups, count)
    send_rows, slot, dest, info = call(
        functools.partial(first_kernel, groups),
        "first",
        [((slots, half_pix), bf16), ((1, count), i32), ((1, slots), i32), ((8, 128), f32)],
        idx,
        owners,
        pixels,
        w_stem,
        scratch=[pltpu.VMEM((HEAD_ROWS, half_pix), f32)],
        cost=4,
    )

    def exchange(values):
        return lax.all_to_all(
            values.reshape(groups, stride, half_pix), "dp", split_axis=0, concat_axis=0, tiled=True
        ).reshape(slots, half_pix)

    arrived = exchange(send_rows)
    grad_low, grad_act, down_sum = call(
        early_kernel,
        "early",
        [((rows, width), bf16), ((rows, units), f32), ((1, width), f32)],
        idx,
        cotangent,
        w_down,
        cost=2,
    )
    arrived_other = swap(arrived, "mp", near)
    centred, normal, stem_act, slope, x_rows, a_low, mean, inv = call(
        functools.partial(stem_kernel, groups),
        "stem",
        [
            ((count, pix), bf16),
            ((count, channels), f32),
            ((count, channels), bf16),
            ((count, channels), f32),
            ((rows, width), f32),
            ((rows, width), bf16),
            ((1, channels), f32),
            ((1, channels), f32),
        ],
        idx,
        info,
        dest,
        arrived,
        arrived_other,
        w_stem,
        bn_gain,
        bn_bias,
        w_patch,
        b_patch,
        text_embed,
        ln1_gain,
        ln1_bias,
        scratch=[pltpu.VMEM((count, pix), bf16)],
        cost=4,
    )
    head_shapes = [((rows, local), bf16)] * 4
    q_own, k_own, v_own, merged, attn = call(
        attention_kernel,
        "attention_own",
        head_shapes + [((rows, width), f32)],
        idx,
        info,
        seq_lengths,
        a_low,
        own_qkv,
        w_out,
        cost=4,
    )
    part = channels // 4
    part_steps = plan(bits, part)
    keep, send = call(
        functools.partial(cross_kernel, part_steps[0][0]),
        "cross",
        [((part // 2, pix), bf16)] * 2,
        idx,
        info,
        normal,
        centred,
        cost=1,
    )
    cross_sums = AllReduce(idx, keep, send, part_steps)
    q_far, k_far, v_far, _, attn = call(
        attention_kernel,
        "attention_far",
        head_shapes + [((rows, width), bf16)],
        idx,
        info,
        seq_lengths,
        a_low,
        far_qkv,
        far_out,
        attn,
        cost=4,
    )
    attn_got = swap(attn, "mp", near)
    cross_sums.scatter()
    half = (rows // 2, width)
    hidden, b_low, act, grad_mid, keep, send, up_sum = call(
        mlp_kernel,
        "mlp",
        [
            ((rows, width), f32),
            ((rows, width), bf16),
            ((rows, units), bf16),
            ((rows, units), bf16),
            (half, bf16),
            (half, bf16),
            ((1, units), f32),
        ],
        idx,
        x_rows,
        attn,
        attn_got,
        b_out,
        ln2_gain,
        ln2_bias,
        w_up,
        b_up,
        grad_act,
        cost=4,
    )
    grad_b = add(idx, keep, swap(send, "mp", near))
    grad_b_got = swap(grad_b, "mp", far)

    down_steps = plan(bits, units)
    up_steps = plan(bits[1:] + bits[:1], width)
    down_keep, down_send, up_keep, up_send = call(
        functools.partial(mlp_grads_kernel, (down_steps[0][0], up_steps[0][0])),
        "mlp_grads",
        [((units // 2, width), bf16)] * 2 + [((width // 2, units), bf16)] * 2,
        idx,
        b_low,
        act,
        grad_mid,
        grad_low,
        cost=3,
    )
    cross_keep, cross_got = cross_sums.last()
    down_sums = AllReduce(idx, down_keep, down_send, down_steps)
    up_sums = AllReduce(idx, up_keep, up_send, up_steps)
    keep, send = call(down_kernel, "down", [(half, bf16)] * 2, idx, act, w_down, cost=2)
    down_got = swap(send, "mp", near)
    grad_b_mine = add(idx, grad_b, grad_b_got)
    grad_b_other = swap(grad_b_mine, "mp", near)
    down = add(idx, keep, down_got)
    down_far = swap(down, "mp", far)

    grad_hidden, hidden_low, grad_own, grad_far, late_sums = call(
        hidden_back_kernel,
        "hidden_back",
        [
            ((rows, width), f32),
            ((rows, width), bf16),
            ((rows, local), bf16),
            ((rows, local), bf16),
            ((3, width), f32),
        ],
        idx,
        grad_b_mine,
        grad_b_other,
        cotangent,
        hidden,
        ln2_gain,
        w_out,
        far_out,
        cost=3,
    )
    grad_qkv, grad_a = call(
        attention_back_kernel,
        "attention_back_own",
        [((3, rows, local), bf16), ((rows, width), f32)],
        idx,
        info,
        seq_lengths,
        q_own,
        k_own,
        v_own,
        grad_own,
        own_qkv,
        cost=5,
    )
    heads_steps = plan(bits, 4 * local)
    keep, send = call(
        functools.partial(head_grads_kernel, heads_steps[0][0]),
        "head_grads",
        [((2 * local, width), bf16)] * 2,
        idx,
        grad_qkv,
        a_low,
        merged,
        hidden_low,
        cost=2,
    )
    heads_sums = AllReduce(idx, keep, send, heads_steps)
    down = add(idx, down, down_far)
    down_other = swap(down, "mp", near)
    down_sums.advance()
    _, grad_a = call(
        attention_back_kernel,
        "attention_back_far",
        [((3, rows, local), bf16), ((rows, width), bf16)],
        idx,
        info,
        seq_lengths,
        q_far,
        k_far,
        v_far,
        grad_far,
        far_qkv,
        grad_a,
        cost=5,
    )
    grad_a_got = swap(grad_a, "mp", near)
    up_sums.advance()
    (output,) = call(
        output_kernel, "output", [((rows, width), f32)], idx, hidden, down, down_other, b_down, cost=2
    )
    grad_text, grad_embed, grad_zed, small = call(
        text_back_kernel,
        "text_back",
        [
            ((rows, width), f32),
            ((count, width), bf16),
            ((count, channels), f32),
            ((10, channels), f32),
        ],
        idx,
        info,
        grad_a,
        grad_a_got,
        grad_hidden,
        x_rows,
        ln1_gain,
        normal,
        slope,
        w_patch,
        late_sums,
        up_sum,
        down_sum,
        cost=4,
    )
    small_got = swap(small, "dp", bits[0])
    keep, send = call(
        functools.partial(part_grads_kernel, part_steps[0][0]),
        "part_grads",
        [((part // 2, width + pix), bf16)] * 2,
        idx,
        stem_act,
        grad_embed,
        grad_zed,
        centred,
        cost=2,
    )
    part_sums = AllReduce(idx, keep, send, part_steps)
    down_sums.advance()
    (row_slots,) = call(
        pixel_back_kernel,
        "pixel_back",
        [((slots, half_pix), bf16)],
        idx,
        dest,
        grad_zed,
        inv,
        bn_gain,
        w_stem,
        cost=2,
    )
    returned = exchange(row_slots)
    small = add(idx, small, small_got)
    for step in bits[1:]:
        small_got = swap(small, "dp", step)
        if step == bits[1]:
            heads_sums.advance()
            part_sums.scatter()
            up_sums.advance()
        elif step == bits[2]:
            down_sums.advance()
            part_sums.scatter()
        small = add(idx, small, small_got)
    (rest,) = call(
        functools.partial(pixel_rest_kernel, groups),
        "pixel_rest",
        [((count, pix), f32)],
        idx,
        owners,
        info,
        pixels,
        w_stem,
        mean,
        inv,
        bn_gain,
        small,
        cost=2,
    )
    keep, got = part_sums.last()
    (piece,) = call(
        functools.partial(correct_kernel, part_steps),
        "correct",
        [(keep.shape, bf16)],
        idx,
        keep,
        got,
        cross_keep,
        cross_got,
        small,
        inv,
        bn_gain,
        info,
        cost=1,
    )
    parts = Gather(idx, piece, part_steps)
    heads_sums.advance()
    up_sums.advance()
    down_sums.advance()
    parts.advance()
    returned_other = swap(returned, "mp", near)
    heads_sums.advance()
    up_sums.advance()
    (grad_pixels,) = call(
        pixel_kernel,
        "pixel",
        [((count, pix), f32)],
        idx,
        slot,
        returned,
        returned_other,
        rest,
        cost=2,
    )
    parts.advance()
    down_sums.advance()
    heads_sums.advance()
    up_sums.advance()
    (parts,) = call(
        functools.partial(widen_kernel, part_steps),
        "join_parts",
        [((part, width + pix), bf16)],
        idx,
        *parts.finish(),
    )
    parts_far = swap(parts, "mp", far)
    heads_sums.advance()
    (grad_w_down,) = call(
        functools.partial(widen_kernel, down_steps),
        "wide_down",
        [((units, width), f32)],
        idx,
        *down_sums.finish(),
        cost=2,
    )
    (grad_w_up,) = call(
        functools.partial(widen_kernel, up_steps),
        "wide_up",
        [((width, units), f32)],
        idx,
        *up_sums.finish(),
        cost=2,
    )
    parts_near = swap(join(idx, [parts, parts_far]), "mp", near)
    grad_w_qkv, grad_w_out = call(
        functools.partial(widen_heads_kernel, heads_steps),
        "wide_heads",
        [((3 * local, width), f32), ((local, width), f32)],
        idx,
        *heads_sums.finish(),
        scratch=[pltpu.VMEM((4 * local, width), f32)],
        cost=2,
    )
    grad_w_qkv = jnp.swapaxes(grad_w_qkv.reshape(3, local, width), 1, 2)
    grad_w_patch, grad_w_stem = call(
        gather_mp_kernel,
        "wide_parts",
        [((channels, width), f32), ((pix, channels), f32)],
        idx,
        parts,
        parts_far,
        parts_near,
        cost=4,
    )
    return (
        output,
        grad_pixels,
        grad_text,
        grad_w_stem,
        small[0],
        small[1],
        grad_w_patch,
        small[2, :width],
        small[3, :width],
        small[4, :width],
        grad_w_qkv,
        grad_w_out,
        small[5, :width],
        small[6, :width],
        small[7, :width],
        grad_w_up,
        small[8, :units],
        grad_w_down,
        small[9, :width],
    )


def solution(mesh):
    in_specs = (
        P("dp", None),
        P(),
        P("dp", None),
        P("dp", None),
        P("dp", None),
        P(),
        P(),
        P(),
        P(),
        P(),
        P(),
        P(),
        P(None, None, "mp"),
        P("mp", None),
        P(),
        P(),
        P(),
        P(None, "mp"),
        P("mp"),
        P("mp", None),
        P(),
    )
    out_specs = (
        P("dp", None),
        P("dp", None),
        P("dp", None),
        P(),
        P(),
        P(),
        P(),
        P(),
        P(),
        P(),
        P(None, None, "mp"),
        P("mp", None),
        P(),
        P(),
        P(),
        P(None, "mp"),
        P("mp"),
        P("mp", None),
        P(),
    )
    return jax.shard_map(shards, mesh=mesh, in_specs=in_specs, out_specs=out_specs, check_vma=False)
```

```python
import functools

import jax
import jax.numpy as jnp
from jax import lax
from jax.experimental import pallas as pl
from jax.experimental.pallas import tpu as pltpu
from jax.sharding import PartitionSpec as P

HEAD = 64
BLK = 256
SCALE = HEAD ** (-0.5)

norm_eps = 1e-05
masked_score = -1e30
f32 = jnp.float32
bf16 = jnp.bfloat16
i32 = jnp.int32


def dot(left, right):
    return lax.dot_general(left, right, (((1,), (0,)), ((), ())), preferred_element_type=f32)


def dot_tn(left, right):
    return lax.dot_general(left, right, (((0,), (0,)), ((), ())), preferred_element_type=f32)


def dot_nt(left, right):
    return lax.dot_general(left, right, (((1,), (1,)), ((), ())), preferred_element_type=f32)


def iota(shape, dim):
    return lax.broadcasted_iota(i32, shape, dim)


def gelu_parts(values):
    cdf = 0.5 * (1.0 + lax.erf(values * (0.5**0.5)))
    pdf = jnp.exp(-0.5 * values * values) * 0.3989422804014327
    return cdf, cdf + values * pdf


def normed(values):
    center = values - jnp.mean(values, axis=-1, keepdims=True)
    inv_std = lax.rsqrt(jnp.mean(center * center, axis=-1, keepdims=True) + norm_eps)
    return center * inv_std, inv_std


def norm_back(grad_out, normal, inv_std, gain):
    scaled = grad_out * gain
    return inv_std * (
        scaled
        - jnp.mean(scaled, axis=-1, keepdims=True)
        - normal * jnp.mean(scaled * normal, axis=-1, keepdims=True)
    )


def col_sum(values):
    return jnp.sum(values, axis=0, keepdims=True)


VMEM = pl.BlockSpec(memory_space=pltpu.VMEM)
SMEM = pl.BlockSpec(memory_space=pltpu.SMEM)
ANY = pl.BlockSpec(memory_space=pl.ANY)
HBM = pl.BlockSpec(memory_space=pltpu.HBM)
PER_US = 1e10
HEAD_ROWS = 16
DOWN_ORDER = (1, 0, 2)
UP_ORDER = (0, 1, 2)
HEADS_ORDER = (0, 1, 2)
PART_ORDER = (0, 1, 2)


class Order:
    last = ()


def call(kernel, name, outs, *args, scratch=(), cost=1.0, place=None, hbm=()):
    shapes = [jax.ShapeDtypeStruct(s, t) for s, t in outs]
    shapes.append(jax.ShapeDtypeStruct((8, 128), f32))
    first, after = len(args), Order.last
    at_mark = first + len(after) + len(outs)

    def body(*refs):
        refs[at_mark][...] = jnp.zeros((8, 128), f32)
        kernel(*refs[:first], *refs[first + len(after) : at_mark], *refs[at_mark + 1 :])

    *results, mark = pl.pallas_call(
        body,
        name=name,
        out_shape=shapes,
        in_specs=[SMEM]
        + [ANY if at in hbm else VMEM for at in range(1, first)]
        + [ANY] * len(after),
        out_specs=[place or VMEM] * len(outs) + [VMEM],
        scratch_shapes=list(scratch),
        compiler_params=pltpu.CompilerParams(vmem_limit_bytes=20 << 20),
        cost_estimate=pl.CostEstimate(
            flops=int(cost * PER_US), bytes_accessed=0, transcendentals=0
        ),
    )(*args, *after)
    Order.last = (mark,)
    return results


def bits_of(axis):
    size = lax.axis_size(axis)
    bits = []
    step = 1
    while step < size:
        bits.append(step)
        step *= 2
    assert step == size
    return bits


def swap(values, axis, step):
    size = lax.axis_size(axis)
    return lax.ppermute(values, axis, [(i, i ^ step) for i in range(size)])


def put_half(keep_ref, send_ref, top, start, value):
    half = keep_ref.shape[0]
    at = pl.ds(start % half, value.shape[0])
    mine = top == (start // half)

    @pl.when(mine)
    def _():
        keep_ref[at] = value.astype(keep_ref.dtype)

    @pl.when(jnp.logical_not(mine))
    def _():
        send_ref[at] = value.astype(send_ref.dtype)


def bit_set(idx_ref, which, step):
    return (idx_ref[which] // step) % 2


def places(bits, order):
    return [bits[at] for at in order] if len(bits) == len(order) else bits


def plan(order, rows):
    steps = []
    for step in order:
        cut = rows % 32 == 0
        rows = rows // 2 if cut else rows
        steps.append((step, cut))
    return steps


def add_split_kernel(step, idx_ref, keep_ref, got_ref, next_ref, send_ref):
    top = bit_set(idx_ref, 0, step)
    half = next_ref.shape[0]
    for part in range(2):
        at = pl.ds(part * half, half)
        total = keep_ref[at].astype(f32) + got_ref[at].astype(f32)
        put_half(next_ref, send_ref, top, part * half, total)


def land_kernel(idx_ref, in_ref, out_ref):
    out_ref[...] = in_ref[...]


def tick_kernel(idx_ref):
    pass


def tick(idx):
    call(tick_kernel, "tick", [], idx, cost=4)


def add_kernel(idx_ref, keep_ref, got_ref, out_ref):
    out_ref[...] = (keep_ref[...].astype(f32) + got_ref[...].astype(f32)).astype(out_ref.dtype)


def add(idx, keep, got, name="add"):
    return call(add_kernel, name, [(keep.shape, keep.dtype)], idx, keep, got)[0]


def join_kernel(idx_ref, *refs):
    out_ref = refs[-1]
    start = 0
    for ref in refs[:-1]:
        out_ref[pl.ds(start, ref.shape[0])] = ref[...]
        start += ref.shape[0]


def join(idx, pieces, name="join"):
    if len(pieces) == 1:
        return pieces[0]
    rows = sum(p.shape[0] for p in pieces)
    outs = [((rows, pieces[0].shape[1]), pieces[0].dtype)]
    return call(join_kernel, name, outs, idx, *pieces, cost=0.5)[0]


class Gather:
    def __init__(self, name, idx, piece, steps):
        self.name, self.idx, self.pieces = name, idx, [piece]
        self.back = [step for step, cut in reversed(steps) if cut]
        self.send(piece)

    def send(self, held):
        self.held = held
        self.pieces.append(swap(held, "dp", self.back[len(self.pieces) - 1]))

    def advance(self):
        if len(self.pieces) <= len(self.back):
            self.send(join(self.idx, self.pieces, f"{self.name}_join{len(self.pieces)}"))
            return True
        return False

    def finish(self):
        while self.advance():
            pass
        return self.pieces


class AllReduce:
    def __init__(self, name, idx, keep, send, steps):
        self.name, self.idx, self.steps, self.gather = name, idx, steps, None
        self.keep, self.at = keep, 0
        self.got = swap(send, "dp", steps[0][0])

    def scatter(self):
        idx, at = self.idx, self.at + 1
        if at == len(self.steps):
            return add(idx, self.keep, self.got, f"{self.name}_last")
        step, cut = self.steps[at]
        self.at = at
        if cut:
            half = (self.keep.shape[0] // 2, self.keep.shape[1])
            self.keep, send = call(
                functools.partial(add_split_kernel, step),
                f"{self.name}_split{at}",
                [(half, self.keep.dtype)] * 2,
                idx,
                self.keep,
                self.got,
            )
        else:
            self.keep = send = add(idx, self.keep, self.got, f"{self.name}_add{at}")
        self.got = swap(send, "dp", step)
        return None

    def last(self):
        while self.at + 1 < len(self.steps):
            self.scatter()
        return self.keep, self.got

    def advance(self):
        if self.gather is not None:
            return self.gather.advance()
        piece = self.scatter()
        if piece is not None:
            self.gather = Gather(self.name, self.idx, piece, self.steps)
        return True

    def finish(self):
        while self.advance():
            pass
        return self.gather.pieces


def piece_row(idx_ref, steps, rows, count):
    cuts = [step for step, cut in steps if cut]
    back = list(reversed(cuts))
    row, size = 0, rows << len(cuts)
    for step in cuts:
        size //= 2
        bit = bit_set(idx_ref, 0, step)
        row = row + (1 - bit if (count >> back.index(step)) & 1 else bit) * size
    return pl.multiple_of(row, rows)


def each_piece(piece_refs, rows):
    count = 0
    for ref in piece_refs:
        for start in range(0, ref.shape[0], rows):
            yield count, ref, pl.ds(start, rows)
            count += 1


def per_group(shape, dim, stride):
    at = iota(shape, dim)
    group = jnp.floor((at.astype(f32) + 0.5) * (1.0 / stride)).astype(i32)
    return group, at - group * stride


def first_kernel(
    groups,
    idx_ref,
    owner_ref,
    pixel_hbm,
    w_stem_hbm,
    send_ref,
    slot_ref,
    dest_ref,
    info_ref,
    sums_ref,
    pixel_ref,
    w_stem_ref,
    sems,
):
    copies = [
        pltpu.make_async_copy(pixel_hbm, pixel_ref, sems.at[0]),
        pltpu.make_async_copy(w_stem_hbm, w_stem_ref, sems.at[1]),
    ]
    for copy in copies:
        copy.start()
    count, pix = pixel_ref.shape
    half = pix // 2
    slots = send_ref.shape[0]
    stride = slots // groups
    core = bit_set(idx_ref, 1, 1)
    table = owner_ref[...]
    own = owner_ref[pl.ds(idx_ref[0], 1), :]
    own_live = jnp.sum((own < groups).astype(f32), axis=1, keepdims=True).astype(i32)
    hot = (iota((groups, count), 0) == own).astype(f32)
    before = (iota((count, count), 0) < iota((count, count), 1)).astype(bf16)
    rank = jnp.sum(hot * dot(hot.astype(bf16), before), axis=0, keepdims=True).astype(i32)
    slot = jnp.where(own < groups, own * stride + HEAD_ROWS + rank, -1)
    slot_ref[...] = slot
    sources = jnp.sum((table == idx_ref[0]).astype(f32), axis=1, keepdims=True)
    lower = (iota((groups, groups), 1) < iota((groups, groups), 0)).astype(bf16)
    starts = dot(lower, jnp.broadcast_to(sources, (groups, 128)).astype(bf16))[:, :1].astype(i32)
    within = iota((groups, slots), 1) - stride * iota((groups, slots), 0) - HEAD_ROWS
    taken = (within >= 0) & (within < sources.astype(i32))
    dest_ref[...] = jnp.max(jnp.where(taken, starts + within, -1), axis=0, keepdims=True)
    prefix = jnp.sum(sources, axis=0, keepdims=True)
    live = jnp.sum((table < groups).astype(f32), axis=1, keepdims=True)
    live_total = jnp.sum(live, axis=0, keepdims=True)
    info_ref[...] = jnp.where(iota(info_ref.shape, 0) == 0, prefix, live_total)
    for copy in copies:
        copy.wait()
    low = pixel_ref[...].astype(bf16)
    live_low = jnp.where(iota((count, 1), 0) < own_live, low, jnp.zeros((), bf16))
    pre = dot(live_low, w_stem_ref[...])
    value = jnp.where(core == 0, col_sum(pre), col_sum(pre * pre))
    left, right = low[:, :half], low[:, half:]
    mine = jnp.where(core == 0, left, right)
    live_mine = jnp.where(core == 0, live_low[:, :half], live_low[:, half:])
    sums_ref[...] = jnp.zeros(sums_ref.shape, f32)
    for part in range(3):
        rounded = value.astype(bf16).astype(f32)
        for row in range(value.shape[1] // 128):
            sums_ref[row : row + 1, part * 128 : part * 128 + 128] = rounded[
                :, row * 128 : row * 128 + 128
            ]
        value = value - rounded
    value = col_sum(live_mine.astype(f32))
    for part in range(3):
        rounded = value.astype(bf16).astype(f32)
        sums_ref[8 + part : 9 + part] = rounded
        value = value - rounded
    pick = (iota((slots, count), 0) == slot).astype(bf16)
    _, place = per_group((slots, HEAD_ROWS), 0, stride)
    spread = (place == iota((slots, HEAD_ROWS), 1)).astype(bf16)
    send_ref[...] = (dot(pick, mine) + dot(spread, sums_ref[...].astype(bf16))).astype(bf16)


def gathered_sums(ref, groups):
    slots = ref.shape[0]
    _, place = per_group((HEAD_ROWS, slots), 1, slots // groups)
    collect = (place == iota((HEAD_ROWS, slots), 0)).astype(bf16)
    total = dot(collect, ref[...])
    value = total[:8, :128] + total[:8, 128:256] + total[:8, 256:384]
    pixel_sum = total[8:9] + total[9:10] + total[10:11]
    return jnp.concatenate([value[row : row + 1] for row in range(8)], axis=1), pixel_sum


def early_kernel(idx_ref, cot_ref, w_down_ref, low_ref, act_ref, sum_ref):
    total = jnp.zeros(sum_ref.shape, f32)
    for start in range(0, cot_ref.shape[0], BLK):
        at = pl.ds(start, BLK)
        cot = cot_ref[at]
        low = cot.astype(bf16)
        low_ref[at] = low
        act_ref[at] = dot_nt(low, w_down_ref[...])
        total = total + col_sum(cot)
    sum_ref[...] = total


def stem_kernel(
    groups,
    idx_ref,
    info_ref,
    dest_ref,
    mine_ref,
    other_ref,
    w_stem_ref,
    bn_gain_ref,
    bn_bias_ref,
    w_patch_ref,
    b_patch_ref,
    text_ref,
    ln1_gain_ref,
    ln1_bias_ref,
    centred_ref,
    normal_ref,
    act_ref,
    slope_ref,
    x_ref,
    a_low_ref,
    mean_ref,
    inv_ref,
    low_ref,
):
    count, pix = centred_ref.shape
    slots = mine_ref.shape[0]
    prefix = info_ref[0:1, :1].astype(i32)
    total = info_ref[1:2, :1]
    core = bit_set(idx_ref, 1, 1)
    sums, pixel_sums = zip(gathered_sums(mine_ref, groups), gathered_sums(other_ref, groups), strict=True)
    first, second = jnp.where(core == 0, sums[0], sums[1]), jnp.where(core == 0, sums[1], sums[0])
    mean = first / total
    inv = lax.rsqrt(second / total - mean * mean + norm_eps)
    mean_ref[...] = mean
    inv_ref[...] = inv
    halves = [
        (
            jnp.where(core == at, mine_ref[...], other_ref[...]),
            jnp.where(core == at, pixel_sums[0], pixel_sums[1]) / total,
        )
        for at in range(2)
    ]
    for start, size in stem_blocks(count, text_ref.shape[0]):
        at = pl.ds(start, size)
        x = text_ref[at]
        if start < count:
            place = (iota((size, slots), 0) + start == dest_ref[...]).astype(bf16)
            for side, (half_rows, half_mean) in enumerate(halves):
                packed = dot(place, half_rows)
                columns = pl.ds(side * (pix // 2), pix // 2)
                low_ref[at, columns] = packed.astype(bf16)
                centred_ref[at, columns] = (packed - half_mean).astype(bf16)
            normal = (dot(low_ref[at], w_stem_ref[...]) - mean) * inv
            normal_ref[at] = normal
            bn_out = normal * bn_gain_ref[...][None, :] + bn_bias_ref[...][None, :]
            cdf, slope = gelu_parts(bn_out)
            slope_ref[at] = slope
            act = (bn_out * cdf).astype(bf16)
            act_ref[at] = act
            embedded = (dot(act, w_patch_ref[...]) + b_patch_ref[...][None, :]).astype(bf16)
            here = iota((size, 1), 0) + start < prefix
            x = x + jnp.where(here, embedded.astype(f32), 0.0)
        x_ref[at] = x
        normal_one, _ = normed(x)
        a_low_ref[at] = (normal_one * ln1_gain_ref[...][None, :] + ln1_bias_ref[...][None, :]).astype(bf16)


def stem_blocks(count, rows):
    half = count // 2
    return [(0, half), (half, half)] + ([(count, rows - count)] if rows > count else [])


def segments(seq_ref, shape, dim):
    rows = iota(shape, dim)
    end = jnp.zeros((1, 1), i32)
    segment = jnp.zeros(shape, i32)
    for at in range(seq_ref.shape[1]):
        end = end + seq_ref[0:1, at : at + 1]
        segment = segment + (end <= rows).astype(i32)
    return segment


def head_lanes(width, head):
    lane = iota((1, width), 1)
    return (lane >= head * HEAD) & (lane < (head + 1) * HEAD)


def attention_kernel(
    idx_ref,
    info_ref,
    seq_ref,
    a_low_ref,
    w_qkv_ref,
    *refs,
):
    q_ref, k_ref, v_ref, merged_ref = refs[:4]
    rows = a_low_ref.shape[0]
    width = merged_ref.shape[1]
    low = a_low_ref[...]
    for t, (ref, scale) in enumerate(((q_ref, SCALE), (k_ref, 1.0), (v_ref, 1.0))):
        part = dot_nt(low, w_qkv_ref[pl.ds(t * width, width)])
        ref[...] = (part * scale if scale != 1.0 else part).astype(bf16)
    prefix = info_ref[0:1, :1].astype(i32)
    key_rows, query_rows = iota((rows, rows), 1), iota((rows, rows), 0)
    visible = (segments(seq_ref, (rows, 1), 0) == segments(seq_ref, (1, rows), 1)) & (
        (key_rows <= query_rows) | (key_rows < prefix)
    )
    bias = jnp.where(visible, 0.0, masked_score)
    zero = jnp.zeros((), bf16)
    merged = jnp.zeros((rows, width), f32)
    for head in range(width // HEAD):
        mask = head_lanes(width, head)
        scores = dot_nt(jnp.where(mask, q_ref[...], zero), k_ref[...]) + bias
        weights = jnp.exp(scores - jnp.max(scores, axis=-1, keepdims=True))
        share = 1.0 / jnp.sum(weights, axis=-1, keepdims=True)
        merged = jnp.where(mask, dot(weights.astype(bf16), v_ref[...]) * share, merged)
    merged_ref[...] = merged.astype(bf16)


def attention_out_kernel(idx_ref, own_ref, w_own_ref, far_ref, w_far_ref, out_ref):
    total = dot(own_ref[...], w_own_ref[...]) + dot(far_ref[...], w_far_ref[...])
    out_ref[...] = total.astype(out_ref.dtype)


def mlp_kernel(
    idx_ref,
    x_ref,
    part_ref,
    got_ref,
    b_out_ref,
    ln2_gain_ref,
    ln2_bias_ref,
    w_up_ref,
    b_up_ref,
    grad_act_ref,
    hidden_ref,
    b_low_ref,
    act_ref,
    grad_mid_ref,
    keep_ref,
    send_ref,
    sum_ref,
):
    top = bit_set(idx_ref, 1, 1)
    total = jnp.zeros(sum_ref.shape, f32)
    for start in range(0, x_ref.shape[0], BLK):
        at = pl.ds(start, BLK)
        attn = part_ref[at].astype(f32) + got_ref[at].astype(f32)
        hidden = x_ref[at] + attn + b_out_ref[...][None, :]
        hidden_ref[at] = hidden
        normal, _ = normed(hidden)
        b_low = (normal * ln2_gain_ref[...][None, :] + ln2_bias_ref[...][None, :]).astype(bf16)
        b_low_ref[at] = b_low
        middle = dot(b_low, w_up_ref[...]) + b_up_ref[...][None, :]
        cdf, slope = gelu_parts(middle)
        act_ref[at] = (middle * cdf).astype(bf16)
        grad_mid = (slope * grad_act_ref[at]).astype(bf16)
        grad_mid_ref[at] = grad_mid
        total = total + col_sum(grad_mid.astype(f32))
        put_half(keep_ref, send_ref, top, start, dot_nt(grad_mid, w_up_ref[...]))
    sum_ref[...] = total


def mlp_grads_kernel(
    steps,
    idx_ref,
    b_low_ref,
    act_ref,
    grad_mid_ref,
    grad_low_ref,
    down_keep_ref,
    down_send_ref,
    up_keep_ref,
    up_send_ref,
):
    for step, left, right, keep, send in (
        (steps[0], act_ref, grad_low_ref, down_keep_ref, down_send_ref),
        (steps[1], b_low_ref, grad_mid_ref, up_keep_ref, up_send_ref),
    ):
        top = bit_set(idx_ref, 0, step)
        half = keep.shape[0]
        for start in (0, half):
            put_half(keep, send, top, start, dot_tn(left[:, pl.ds(start, half)], right[...]))


def down_kernel(idx_ref, act_ref, w_down_ref, keep_ref, send_ref):
    top = bit_set(idx_ref, 1, 1)
    for start in range(0, act_ref.shape[0], BLK):
        put_half(keep_ref, send_ref, top, start, dot(act_ref[pl.ds(start, BLK)], w_down_ref[...]))


def output_kernel(
    idx_ref, hidden_ref, mine_ref, other_ref, b_down_ref, out_ref, held_ref, sems
):
    top = bit_set(idx_ref, 1, 1)
    half = mine_ref.shape[0]
    copies = []
    for start in range(0, hidden_ref.shape[0], BLK):
        at = pl.ds(start, BLK)
        down = pick_half(mine_ref, other_ref, top, start, half)
        held_ref[at] = hidden_ref[at] + down + b_down_ref[...][None, :]
        copies.append(
            pltpu.make_async_copy(held_ref.at[at], out_ref.at[at], sems.at[start // BLK])
        )
        copies[-1].start()
    for copy in copies:
        copy.wait()


def pick_half(mine_ref, other_ref, top, start, half):
    at = pl.ds(start % half, BLK)
    mine = top == (start // half)
    return jnp.where(mine, mine_ref[at].astype(f32), other_ref[at].astype(f32))


def hidden_back_kernel(
    idx_ref,
    mine_ref,
    other_ref,
    cot_ref,
    hidden_ref,
    ln2_gain_ref,
    w_out_own_ref,
    w_out_far_ref,
    grad_hidden_ref,
    low_ref,
    own_ref,
    far_ref,
    sums_ref,
):
    top = bit_set(idx_ref, 1, 1)
    half = mine_ref.shape[0]
    width = cot_ref.shape[1]
    sums = [jnp.zeros((1, width), f32)] * 3
    for start in range(0, cot_ref.shape[0], BLK):
        at = pl.ds(start, BLK)
        grad = pick_half(mine_ref, other_ref, top, start, half)
        normal, inv = normed(hidden_ref[at])
        grad_hidden = cot_ref[at] + norm_back(grad, normal, inv, ln2_gain_ref[...][None, :])
        grad_hidden_ref[at] = grad_hidden
        low = grad_hidden.astype(bf16)
        low_ref[at] = low
        own_ref[at] = dot_nt(low, w_out_own_ref[...]).astype(bf16)
        far_ref[at] = dot_nt(low, w_out_far_ref[...]).astype(bf16)
        sums = [
            sums[0] + col_sum(grad_hidden),
            sums[1] + col_sum(grad * normal),
            sums[2] + col_sum(grad),
        ]
    for at in range(3):
        sums_ref[at : at + 1] = sums[at]


def attention_back_kernel(
    idx_ref,
    info_ref,
    seq_ref,
    q_ref,
    k_ref,
    v_ref,
    grad_ref,
    w_qkv_ref,
    *refs,
):
    base_ref = refs[0] if len(refs) == 3 else None
    grad_qkv_ref, out_ref = refs[-2:]
    rows, width = q_ref.shape
    prefix = info_ref[0:1, :1].astype(i32)
    zero = jnp.zeros((), bf16)
    key_rows, query_rows = iota((rows, rows), 0), iota((rows, rows), 1)
    visible = (segments(seq_ref, (rows, 1), 0) == segments(seq_ref, (1, rows), 1)) & (
        (key_rows <= query_rows) | (key_rows < prefix)
    )
    bias = jnp.where(visible, 0.0, masked_score)
    grad_values = jnp.zeros((rows, width), f32)
    grad_keys = jnp.zeros((rows, width), f32)
    grad_queries = jnp.zeros((rows, width), f32)
    for head in range(width // HEAD):
        mask = head_lanes(width, head)
        query = jnp.where(mask, q_ref[...], zero)
        grad = jnp.where(mask, grad_ref[...], zero)
        scores = dot_nt(k_ref[...], query) + bias
        weights = jnp.exp(scores - jnp.max(scores, axis=0, keepdims=True))
        probs = weights * (1.0 / jnp.sum(weights, axis=0, keepdims=True))
        grad_weights = dot_nt(v_ref[...], grad)
        delta = jnp.sum(probs * grad_weights, axis=0, keepdims=True)
        grad_scores = (probs * (grad_weights - delta)).astype(bf16)
        grad_values = grad_values + dot(probs.astype(bf16), grad)
        grad_keys = grad_keys + dot(grad_scores, query)
        grad_queries = jnp.where(mask, dot_tn(grad_scores, k_ref[...]), grad_queries)
    total = jnp.zeros((rows, w_qkv_ref.shape[1]), f32)
    for t, value in enumerate((grad_queries * SCALE, grad_keys, grad_values)):
        low = value.astype(bf16)
        grad_qkv_ref[t] = low
        total = total + dot(low, w_qkv_ref[pl.ds(t * width, width)])
    if base_ref is not None:
        total = total + base_ref[...]
    out_ref[...] = total.astype(out_ref.dtype)


def text_back_kernel(
    idx_ref,
    info_ref,
    part_ref,
    got_ref,
    grad_hidden_ref,
    x_ref,
    ln1_gain_ref,
    normal_ref,
    slope_ref,
    w_patch_ref,
    late_ref,
    up_sum_ref,
    down_sum_ref,
    grad_text_ref,
    embed_ref,
    zed_ref,
    small_ref,
):
    count, channels = normal_ref.shape
    width = x_ref.shape[1]
    prefix = info_ref[0:1, :1].astype(i32)
    bn_sums = [jnp.zeros((1, channels), f32)] * 2
    sums = [jnp.zeros((1, width), f32)] * 3
    for start, size in stem_blocks(count, x_ref.shape[0]):
        at = pl.ds(start, size)
        grad = part_ref[at].astype(f32) + got_ref[at].astype(f32)
        normal, inv = normed(x_ref[at])
        grad_text = grad_hidden_ref[at] + norm_back(grad, normal, inv, ln1_gain_ref[...][None, :])
        grad_text_ref[at] = grad_text
        sums[1] = sums[1] + col_sum(grad * normal)
        sums[2] = sums[2] + col_sum(grad)
        if start < count:
            here = iota((size, 1), 0) + start < prefix
            embed = jnp.where(here, grad_text, 0.0).astype(bf16)
            embed_ref[at] = embed
            sums[0] = sums[0] + col_sum(embed.astype(f32))
            zed = slope_ref[at] * dot_nt(embed, w_patch_ref[...])
            zed_ref[at] = zed
            bn_sums = [bn_sums[0] + col_sum(zed * normal_ref[at]), bn_sums[1] + col_sum(zed)]
    small_ref[...] = jnp.zeros(small_ref.shape, f32)
    small_ref[0:1] = bn_sums[0]
    small_ref[1:2] = bn_sums[1]
    for at in range(3):
        small_ref[2 + at : 3 + at, :width] = sums[at]
    small_ref[5:8, :width] = late_ref[...]
    small_ref[8:9, : up_sum_ref.shape[1]] = up_sum_ref[...]
    small_ref[9:10, :width] = down_sum_ref[...]


def head_grads_kernel(
    step, idx_ref, grad_qkv_ref, a_low_ref, merged_ref, low_ref, keep_ref, send_ref
):
    top = bit_set(idx_ref, 0, step)
    width = merged_ref.shape[1]
    for t in range(3):
        put_half(keep_ref, send_ref, top, t * width, dot_tn(grad_qkv_ref[t], a_low_ref[...]))
    put_half(keep_ref, send_ref, top, 3 * width, dot_tn(merged_ref[...], low_ref[...]))


def part_grads_kernel(
    step,
    idx_ref,
    info_ref,
    act_ref,
    embed_ref,
    zed_ref,
    normal_ref,
    centred_ref,
    keep_ref,
    send_ref,
):
    top = bit_set(idx_ref, 0, step)
    half = keep_ref.shape[0]
    first = idx_ref[1] * (2 * half)
    here = iota((normal_ref.shape[0], 1), 0) < info_ref[0:1, :1].astype(i32)
    for part in range(2):
        columns = pl.ds(pl.multiple_of(first + part * half, half), half)
        normal = jnp.where(here, normal_ref[:, columns], 0.0).astype(bf16)
        values = [
            dot_tn(act_ref[:, columns], embed_ref[...]),
            dot_tn(zed_ref[:, columns].astype(bf16), centred_ref[...]),
            dot_tn(normal, centred_ref[...]),
        ]
        put_half(keep_ref, send_ref, top, part * half, jnp.concatenate(values, axis=1))


def correct_kernel(
    steps,
    idx_ref,
    keep_ref,
    got_ref,
    small_ref,
    inv_ref,
    bn_gain_ref,
    info_ref,
    out_ref,
):
    rows = out_ref.shape[0]
    width = out_ref.shape[1] // 2
    cuts = [step for step, cut in steps if cut]
    size = rows << len(cuts)
    row = idx_ref[1] * size
    for step in cuts:
        size //= 2
        row = row + bit_set(idx_ref, 0, step) * size
    hot = iota((rows, inv_ref.shape[1]), 1) == iota((rows, inv_ref.shape[1]), 0) + row

    def column(value):
        return jnp.sum(jnp.where(hot, value, 0.0), axis=1, keepdims=True)

    factor = column(inv_ref[...] * bn_gain_ref[...][None, :])
    share = column(small_ref[0:1]) / info_ref[1:2, :1]
    total = keep_ref[...].astype(f32) + got_ref[...].astype(f32)
    stem = factor * (total[:, width : 2 * width] - share * total[:, 2 * width :])
    out_ref[:, :width] = total[:, :width].astype(out_ref.dtype)
    out_ref[:, width:] = stem.astype(out_ref.dtype)


def pixel_back_kernel(idx_ref, dest_ref, zed_ref, inv_ref, bn_gain_ref, w_stem_ref, slots_ref):
    slots, half = slots_ref.shape
    place = (iota((zed_ref.shape[0], slots), 0) == dest_ref[...]).astype(bf16)
    core = bit_set(idx_ref, 1, 1)
    weights = w_stem_ref[pl.ds(pl.multiple_of(core * half, half), half)]
    scaled = (zed_ref[...] * (inv_ref[...] * bn_gain_ref[...][None, :])).astype(bf16)
    rows = dot_nt(scaled, weights).astype(bf16)
    slots_ref[...] = dot_tn(place, rows).astype(bf16)


def pixel_rest_kernel(
    groups,
    idx_ref,
    owner_ref,
    info_ref,
    pixel_ref,
    w_stem_ref,
    mean_ref,
    inv_ref,
    bn_gain_ref,
    small_ref,
    out_ref,
):
    own = owner_ref[pl.ds(idx_ref[0], 1), :]
    live = jnp.sum((own < groups).astype(f32), axis=1, keepdims=True).astype(i32)
    total = info_ref[1:2, :1]
    pre = dot(pixel_ref[...].astype(bf16), w_stem_ref[...])
    normal = (pre - mean_ref[...]) * inv_ref[...]
    factor = inv_ref[...] * bn_gain_ref[...][None, :]
    rest = factor * (small_ref[1:2] / total + normal * (small_ref[0:1] / total))
    rest = jnp.where(iota((pixel_ref.shape[0], 1), 0) < live, rest, 0.0)
    out_ref[...] = dot_nt(rest.astype(bf16), w_stem_ref[...])


def pixel_kernel(
    idx_ref, slot_ref, mine_ref, other_ref, rest_ref, out_ref, held_ref, sems
):
    copies = []
    slots, half = mine_ref.shape
    pick = (iota((slots, out_ref.shape[0]), 0) == slot_ref[...]).astype(bf16)
    core = bit_set(idx_ref, 1, 1)
    for side in range(2):
        value = jnp.where(core == side, mine_ref[...], other_ref[...])
        columns = pl.ds(side * half, half)
        held_ref[:, columns] = dot_tn(pick, value) - rest_ref[:, columns]
        copies.append(
            pltpu.make_async_copy(held_ref.at[:, columns], out_ref.at[:, columns], sems.at[side])
        )
        copies[-1].start()
    for copy in copies:
        copy.wait()


def widen_kernel(steps, idx_ref, *refs):
    pieces, (out_ref, held_ref, sems) = refs[:-3], refs[-3:]
    rows = pieces[0].shape[0]
    copies = []
    for count, ref, at in each_piece(pieces, rows):
        here = pl.ds(count * rows, rows)
        held_ref[here] = ref[at].astype(f32)
        to = pl.ds(piece_row(idx_ref, steps, rows, count), rows)
        copies.append(pltpu.make_async_copy(held_ref.at[here], out_ref.at[to], sems.at[count]))
        copies[-1].start()
    for copy in copies:
        copy.wait()


def widen_two_kernel(steps, idx_ref, *refs):
    pieces, (first_ref, second_ref, held_ref, sems) = refs[:-4], refs[-4:]
    rows = pieces[0].shape[0]
    for count, ref, at in each_piece(pieces, rows):
        held_ref[pl.ds(piece_row(idx_ref, steps, rows, count), rows)] = ref[at].astype(f32)
    split = first_ref.shape[0]
    copies = [
        pltpu.make_async_copy(held_ref.at[pl.ds(0, split)], first_ref, sems.at[0]),
        pltpu.make_async_copy(
            held_ref.at[pl.ds(split, second_ref.shape[0])], second_ref, sems.at[1]
        ),
    ]
    for copy in copies:
        copy.start()
    for copy in copies:
        copy.wait()


def widen_parts_kernel(
    steps,
    idx_ref,
    held_ref,
    last_ref,
    far_held_ref,
    far_last_ref,
    near_ref,
    near_far_ref,
    patch_ref,
    stem_ref,
    patch_rows_ref,
    stem_rows_ref,
    turned_ref,
    sems,
):
    width = patch_ref.shape[1]
    part = near_ref.shape[0]
    rows = part >> sum(cut for _, cut in steps)
    for flip, refs in (
        (0, (held_ref, last_ref)),
        (2, (far_held_ref, far_last_ref)),
        (1, (near_ref,)),
        (3, (near_far_ref,)),
    ):
        at = bit_set(idx_ref, 1, 1) ^ (flip & 1)
        at = at + 2 * (bit_set(idx_ref, 1, 2) ^ (flip >> 1))
        for count, ref, here in each_piece(refs, rows):
            row = at * part + piece_row(idx_ref, steps, rows, count)
            to = pl.ds(pl.multiple_of(row, rows), rows)
            patch_rows_ref[to] = ref[here, :width].astype(f32)
            stem_rows_ref[to] = ref[here, width:].astype(f32)
    copies = [pltpu.make_async_copy(patch_rows_ref, patch_ref, sems.at[0])]
    copies[0].start()
    for at in range(4):
        columns = pl.ds(at * part, part)
        turned_ref[:, columns] = stem_rows_ref[columns].T
        copies.append(
            pltpu.make_async_copy(
                turned_ref.at[:, columns], stem_ref.at[:, columns], sems.at[1 + at]
            )
        )
        copies[-1].start()
    for copy in copies:
        copy.wait()


def shards(
    pixels,
    patch_owner,
    seq_lengths,
    text_embed,
    cotangent,
    w_stem,
    bn_gain,
    bn_bias,
    w_patch,
    b_patch,
    ln1_gain,
    ln1_bias,
    w_qkv,
    w_out,
    b_out,
    ln2_gain,
    ln2_bias,
    w_up,
    b_up,
    w_down,
    b_down,
):
    groups = lax.axis_size("dp")
    assert lax.axis_size("mp") == 4
    near, far = bits_of("mp")
    bits = bits_of("dp")
    count, pix = pixels.shape
    rows, width = text_embed.shape
    channels = w_stem.shape[1]
    local = w_out.shape[0]
    units = w_up.shape[1]
    capacity = count // groups
    idx = jnp.stack([lax.axis_index("dp"), lax.axis_index("mp")]).astype(i32)

    Order.last = ()
    stride = HEAD_ROWS + capacity
    slots = groups * stride
    half_pix = pix // 2
    own_qkv = jnp.swapaxes(w_qkv, 1, 2).reshape(3 * local, width)
    far_qkv = swap(own_qkv, "mp", far)
    far_out = swap(w_out, "mp", far)
    owners = patch_owner.reshape(groups, count)
    send_rows, slot, dest, info = call(
        functools.partial(first_kernel, groups),
        "first",
        [((slots, half_pix), bf16), ((1, count), i32), ((1, slots), i32), ((8, 128), f32)],
        idx,
        owners,
        pixels,
        w_stem,
        scratch=[
            pltpu.VMEM((HEAD_ROWS, half_pix), f32),
            pltpu.VMEM((count, pix), f32),
            pltpu.VMEM((pix, channels), bf16),
            pltpu.SemaphoreType.DMA((2,)),
        ],
        cost=4,
        hbm=(2, 3),
    )

    def exchange(values):
        return lax.all_to_all(
            values.reshape(groups, stride, half_pix), "dp", split_axis=0, concat_axis=0, tiled=True
        ).reshape(slots, half_pix)

    arrived = exchange(send_rows)
    grad_low, grad_act, down_sum = call(
        early_kernel,
        "early",
        [((rows, width), bf16), ((rows, units), f32), ((1, width), f32)],
        idx,
        cotangent,
        w_down,
        cost=2,
    )
    (arrived,) = call(land_kernel, "land", [((slots, half_pix), bf16)], idx, arrived, cost=1)
    arrived_other = swap(arrived, "mp", near)
    tick(idx)
    centred, normal, stem_act, slope, x_rows, a_low, mean, inv = call(
        functools.partial(stem_kernel, groups),
        "stem",
        [
            ((count, pix), bf16),
            ((count, channels), f32),
            ((count, channels), bf16),
            ((count, channels), f32),
            ((rows, width), f32),
            ((rows, width), bf16),
            ((1, channels), f32),
            ((1, channels), f32),
        ],
        idx,
        info,
        dest,
        arrived,
        arrived_other,
        w_stem,
        bn_gain,
        bn_bias,
        w_patch,
        b_patch,
        text_embed,
        ln1_gain,
        ln1_bias,
        scratch=[pltpu.VMEM((count, pix), bf16)],
        cost=4,
    )
    head_shapes = [((rows, local), bf16)] * 4
    q_own, k_own, v_own, merged = call(
        attention_kernel,
        "attention_own",
        head_shapes,
        idx,
        info,
        seq_lengths,
        a_low,
        own_qkv,
        cost=4,
    )
    q_far, k_far, v_far, merged_far = call(
        attention_kernel,
        "attention_far",
        head_shapes,
        idx,
        info,
        seq_lengths,
        a_low,
        far_qkv,
        cost=4,
    )
    (attn,) = call(
        attention_out_kernel,
        "attention_out",
        [((rows, width), bf16)],
        idx,
        merged,
        w_out,
        merged_far,
        far_out,
    )
    attn_got = swap(attn, "mp", near)
    half = (rows // 2, width)
    hidden, b_low, act, grad_mid, keep, send, up_sum = call(
        mlp_kernel,
        "mlp",
        [
            ((rows, width), f32),
            ((rows, width), bf16),
            ((rows, units), bf16),
            ((rows, units), bf16),
            (half, bf16),
            (half, bf16),
            ((1, units), f32),
        ],
        idx,
        x_rows,
        attn,
        attn_got,
        b_out,
        ln2_gain,
        ln2_bias,
        w_up,
        b_up,
        grad_act,
        cost=4,
    )
    grad_b_near = swap(send, "mp", near)
    out_keep, send = call(down_kernel, "down", [(half, bf16)] * 2, idx, act, w_down, cost=2)
    out_near = swap(send, "mp", near)
    grad_b = add(idx, keep, grad_b_near, "grad_b1")
    grad_b_got = swap(grad_b, "mp", far)
    down_steps = plan(places(bits, DOWN_ORDER), units)
    up_steps = plan(places(bits, UP_ORDER), width)
    down_keep, down_send, up_keep, up_send = call(
        functools.partial(mlp_grads_kernel, (down_steps[0][0], up_steps[0][0])),
        "mlp_grads",
        [((units // 2, width), bf16)] * 2 + [((width // 2, units), bf16)] * 2,
        idx,
        b_low,
        act,
        grad_mid,
        grad_low,
        cost=3,
    )
    down_sums = AllReduce("down", idx, down_keep, down_send, down_steps)
    up_sums = AllReduce("up", idx, up_keep, up_send, up_steps)
    out = add(idx, out_keep, out_near, "out1")
    out_got = swap(out, "mp", far)
    grad_b_mine = add(idx, grad_b, grad_b_got, "grad_b2")
    grad_b_other = swap(grad_b_mine, "mp", near)
    tick(idx)

    grad_hidden, hidden_low, grad_own, grad_far, late_sums = call(
        hidden_back_kernel,
        "hidden_back",
        [
            ((rows, width), f32),
            ((rows, width), bf16),
            ((rows, local), bf16),
            ((rows, local), bf16),
            ((3, width), f32),
        ],
        idx,
        grad_b_mine,
        grad_b_other,
        cotangent,
        hidden,
        ln2_gain,
        w_out,
        far_out,
        cost=3,
    )
    grad_qkv, grad_a = call(
        attention_back_kernel,
        "attention_back_own",
        [((3, rows, local), bf16), ((rows, width), f32)],
        idx,
        info,
        seq_lengths,
        q_own,
        k_own,
        v_own,
        grad_own,
        own_qkv,
        cost=5,
    )
    _, grad_a = call(
        attention_back_kernel,
        "attention_back_far",
        [((3, rows, local), bf16), ((rows, width), bf16)],
        idx,
        info,
        seq_lengths,
        q_far,
        k_far,
        v_far,
        grad_far,
        far_qkv,
        grad_a,
        cost=5,
    )
    grad_a_got = swap(grad_a, "mp", near)
    up_sums.advance()
    grad_text, grad_embed, grad_zed, small = call(
        text_back_kernel,
        "text_back",
        [
            ((rows, width), f32),
            ((count, width), bf16),
            ((count, channels), f32),
            ((10, channels), f32),
        ],
        idx,
        info,
        grad_a,
        grad_a_got,
        grad_hidden,
        x_rows,
        ln1_gain,
        normal,
        slope,
        w_patch,
        late_sums,
        up_sum,
        down_sum,
        cost=4,
    )
    small_got = swap(small, "dp", bits[0])
    part = channels // 4
    part_steps = plan(places(bits, PART_ORDER), part)
    keep, send = call(
        functools.partial(part_grads_kernel, part_steps[0][0]),
        "part_grads",
        [((part // 2, width + 2 * pix), bf16)] * 2,
        idx,
        info,
        stem_act,
        grad_embed,
        grad_zed,
        normal,
        centred,
        cost=2,
    )
    part_sums = AllReduce("part", idx, keep, send, part_steps)
    small = add(idx, small, small_got, "small0")
    small_got = swap(small, "dp", bits[1])
    out = add(idx, out, out_got, "out2")
    out_other = swap(out, "mp", near)
    up_sums.advance()
    for step in bits[2:]:
        small = add(idx, small, small_got, f"small{step}")
        small_got = swap(small, "dp", step)
    (row_slots,) = call(
        pixel_back_kernel,
        "pixel_back",
        [((slots, half_pix), bf16)],
        idx,
        dest,
        grad_zed,
        inv,
        bn_gain,
        w_stem,
        cost=2,
    )
    returned = exchange(row_slots)
    (output,) = call(
        output_kernel,
        "output",
        [((rows, width), f32)],
        idx,
        hidden,
        out,
        out_other,
        b_down,
        scratch=[pltpu.VMEM((rows, width), f32), pltpu.SemaphoreType.DMA((rows // BLK,))],
        cost=2,
        place=HBM,
    )
    small = add(idx, small, small_got, "small_last")
    part_sums.scatter()
    heads_steps = plan(places(bits, HEADS_ORDER), 4 * local)
    keep, send = call(
        functools.partial(head_grads_kernel, heads_steps[0][0]),
        "head_grads",
        [((2 * local, width), bf16)] * 2,
        idx,
        grad_qkv,
        a_low,
        merged,
        hidden_low,
        cost=2,
    )
    heads_sums = AllReduce("heads", idx, keep, send, heads_steps)
    down_sums.advance()
    up_sums.advance()
    (rest,) = call(
        functools.partial(pixel_rest_kernel, groups),
        "pixel_rest",
        [((count, pix), f32)],
        idx,
        owners,
        info,
        pixels,
        w_stem,
        mean,
        inv,
        bn_gain,
        small,
        cost=2,
    )
    part_sums.scatter()
    up_sums.advance()
    heads_sums.advance()
    returned_other = swap(returned, "mp", near)
    keep, got = part_sums.last()
    (piece,) = call(
        functools.partial(correct_kernel, part_steps),
        "correct",
        [((keep.shape[0], width + pix), bf16)],
        idx,
        keep,
        got,
        small,
        inv,
        bn_gain,
        info,
        cost=1,
    )
    parts = Gather("part", idx, piece, part_steps)
    up_sums.advance()
    (grad_pixels,) = call(
        pixel_kernel,
        "pixel",
        [((count, pix), f32)],
        idx,
        slot,
        returned,
        returned_other,
        rest,
        scratch=[pltpu.VMEM((count, pix), f32), pltpu.SemaphoreType.DMA((2,))],
        cost=2,
        place=HBM,
    )
    heads_sums.advance()
    down_sums.advance()
    parts.advance()
    heads_sums.advance()

    def widen(name, sums, steps, total):
        pieces = sums.finish()
        cols = pieces[0].shape[1]
        return call(
            functools.partial(widen_kernel, steps),
            name,
            [((total, cols), f32)],
            idx,
            *pieces,
            scratch=[
                pltpu.VMEM((total, cols), f32),
                pltpu.SemaphoreType.DMA((total // pieces[0].shape[0],)),
            ],
            cost=2,
            place=HBM,
        )[0]

    grad_w_up = widen("wide_up", up_sums, up_steps, width)
    down_sums.advance()
    parts.finish()
    held, last = parts.held, parts.pieces[-1]
    far_held = swap(held, "mp", far)
    heads_sums.advance()
    down_sums.advance()
    near_own = swap(join(idx, [held, last], "parts_own"), "mp", near)
    far_last = swap(last, "mp", far)
    heads_sums.advance()
    down_sums.advance()
    near_far = swap(join(idx, [far_held, far_last], "parts_far"), "mp", near)
    tick(idx)
    grad_w_patch, grad_w_stem = call(
        functools.partial(widen_parts_kernel, part_steps),
        "wide_parts",
        [((channels, width), f32), ((pix, channels), f32)],
        idx,
        held,
        last,
        far_held,
        far_last,
        near_own,
        near_far,
        scratch=[
            pltpu.VMEM((channels, width), f32),
            pltpu.VMEM((channels, pix), f32),
            pltpu.VMEM((pix, channels), f32),
            pltpu.SemaphoreType.DMA((5,)),
        ],
        cost=4,
        place=HBM,
    )
    grad_w_qkv, grad_w_out = call(
        functools.partial(widen_two_kernel, heads_steps),
        "wide_heads",
        [((3 * local, width), f32), ((local, width), f32)],
        idx,
        *heads_sums.finish(),
        scratch=[pltpu.VMEM((4 * local, width), f32), pltpu.SemaphoreType.DMA((2,))],
        cost=2,
        place=HBM,
    )
    grad_w_qkv = jnp.swapaxes(grad_w_qkv.reshape(3, local, width), 1, 2)
    grad_w_down = widen("wide_down", down_sums, down_steps, units)
    return (
        output,
        grad_pixels,
        grad_text,
        grad_w_stem,
        small[0],
        small[1],
        grad_w_patch,
        small[2, :width],
        small[3, :width],
        small[4, :width],
        grad_w_qkv,
        grad_w_out,
        small[5, :width],
        small[6, :width],
        small[7, :width],
        grad_w_up,
        small[8, :units],
        grad_w_down,
        small[9, :width],
    )


def solution(mesh):
    in_specs = (
        P("dp", None),
        P(),
        P("dp", None),
        P("dp", None),
        P("dp", None),
        P(),
        P(),
        P(),
        P(),
        P(),
        P(),
        P(),
        P(None, None, "mp"),
        P("mp", None),
        P(),
        P(),
        P(),
        P(None, "mp"),
        P("mp"),
        P("mp", None),
        P(),
    )
    out_specs = (
        P("dp", None),
        P("dp", None),
        P("dp", None),
        P(),
        P(),
        P(),
        P(),
        P(),
        P(),
        P(),
        P(None, None, "mp"),
        P("mp", None),
        P(),
        P(),
        P(),
        P(None, "mp"),
        P("mp"),
        P("mp", None),
        P(),
    )
    return jax.shard_map(shards, mesh=mesh, in_specs=in_specs, out_specs=out_specs, check_vma=False)
```

```python
import functools

import jax
import jax.numpy as jnp
from jax import lax
from jax.experimental import pallas as pl
from jax.experimental.pallas import tpu as pltpu
from jax.sharding import PartitionSpec as P

HEAD = 64
BLK = 256
SCALE = HEAD ** (-0.5)

norm_eps = 1e-05
masked_score = -1e30
f32 = jnp.float32
bf16 = jnp.bfloat16
i32 = jnp.int32


def dot(left, right):
    return lax.dot_general(left, right, (((1,), (0,)), ((), ())), preferred_element_type=f32)


def dot_tn(left, right):
    return lax.dot_general(left, right, (((0,), (0,)), ((), ())), preferred_element_type=f32)


def dot_nt(left, right):
    return lax.dot_general(left, right, (((1,), (1,)), ((), ())), preferred_element_type=f32)


def iota(shape, dim):
    return lax.broadcasted_iota(i32, shape, dim)


def gelu_parts(values):
    cdf = 0.5 * (1.0 + lax.erf(values * (0.5**0.5)))
    pdf = jnp.exp(-0.5 * values * values) * 0.3989422804014327
    return cdf, cdf + values * pdf


def normed(values):
    center = values - jnp.mean(values, axis=-1, keepdims=True)
    inv_std = lax.rsqrt(jnp.mean(center * center, axis=-1, keepdims=True) + norm_eps)
    return center * inv_std, inv_std


def norm_back(grad_out, normal, inv_std, gain):
    scaled = grad_out * gain
    return inv_std * (
        scaled
        - jnp.mean(scaled, axis=-1, keepdims=True)
        - normal * jnp.mean(scaled * normal, axis=-1, keepdims=True)
    )


def col_sum(values):
    return jnp.sum(values, axis=0, keepdims=True)


VMEM = pl.BlockSpec(memory_space=pltpu.VMEM)
SMEM = pl.BlockSpec(memory_space=pltpu.SMEM)
ANY = pl.BlockSpec(memory_space=pl.ANY)
HBM = pl.BlockSpec(memory_space=pltpu.HBM)
PER_US = 1e10
HEAD_ROWS = 16
DOWN_ORDER = (1, 0, 2)
UP_ORDER = (0, 1, 2)
HEADS_ORDER = (0, 1, 2)
PART_ORDER = (0, 1, 2)


class Place:
    def __getitem__(self, at):
        return lax.axis_index(("dp", "mp")[at])


class Order:
    last = ()


def call(kernel, name, outs, *args, scratch=(), cost=1.0, place=None, hbm=()):
    shapes = [jax.ShapeDtypeStruct(s, t) for s, t in outs]
    shapes.append(jax.ShapeDtypeStruct((8, 128), f32))
    args = args[1:]
    first, after = len(args), Order.last
    at_mark = first + len(after) + len(outs)

    def body(*refs):
        refs[at_mark][...] = jnp.zeros((8, 128), f32)
        kernel(Place(), *refs[:first], *refs[first + len(after) : at_mark], *refs[at_mark + 1 :])

    *results, mark = pl.pallas_call(
        body,
        name=name,
        out_shape=shapes,
        in_specs=[HBM if at + 1 in hbm else VMEM for at in range(first)] + [ANY] * len(after),
        out_specs=[place or VMEM] * len(outs) + [VMEM],
        scratch_shapes=list(scratch),
        compiler_params=pltpu.CompilerParams(vmem_limit_bytes=(20 if cost > 1 else 6) << 20),
        cost_estimate=pl.CostEstimate(
            flops=int(cost * PER_US), bytes_accessed=0, transcendentals=0
        ),
    )(*args, *after)
    Order.last = (mark,)
    return results


def bits_of(axis):
    size = lax.axis_size(axis)
    bits = []
    step = 1
    while step < size:
        bits.append(step)
        step *= 2
    assert step == size
    return bits


def swap(values, axis, step):
    size = lax.axis_size(axis)
    return lax.ppermute(values, axis, [(i, i ^ step) for i in range(size)])


def put_half(keep_ref, send_ref, top, start, value):
    half = keep_ref.shape[0]
    at = pl.ds(start % half, value.shape[0])
    mine = top == (start // half)

    @pl.when(mine)
    def _():
        keep_ref[at] = value.astype(keep_ref.dtype)

    @pl.when(jnp.logical_not(mine))
    def _():
        send_ref[at] = value.astype(send_ref.dtype)


def bit_set(idx_ref, which, step):
    return (idx_ref[which] // step) % 2


def places(bits, order):
    return [bits[at] for at in order] if len(bits) == len(order) else bits


def plan(order, rows):
    steps = []
    for step in order:
        cut = rows % 32 == 0
        rows = rows // 2 if cut else rows
        steps.append((step, cut))
    return steps


def add_split_kernel(step, idx_ref, keep_ref, got_ref, next_ref, send_ref):
    top = bit_set(idx_ref, 0, step)
    half = next_ref.shape[0]
    for part in range(2):
        at = pl.ds(part * half, half)
        total = keep_ref[at].astype(f32) + got_ref[at].astype(f32)
        put_half(next_ref, send_ref, top, part * half, total)


def land_kernel(idx_ref, in_ref, out_ref):
    out_ref[...] = in_ref[...]


def tick_kernel(idx_ref):
    pass


def tick(idx):
    call(tick_kernel, "tick", [], idx, cost=4)


def add_kernel(idx_ref, keep_ref, got_ref, out_ref):
    out_ref[...] = (keep_ref[...].astype(f32) + got_ref[...].astype(f32)).astype(out_ref.dtype)


def add(idx, keep, got, name="add"):
    return call(add_kernel, name, [(keep.shape, keep.dtype)], idx, keep, got)[0]


def join_kernel(idx_ref, *refs):
    out_ref = refs[-1]
    start = 0
    for ref in refs[:-1]:
        out_ref[pl.ds(start, ref.shape[0])] = ref[...]
        start += ref.shape[0]


def join(idx, pieces, name="join"):
    if len(pieces) == 1:
        return pieces[0]
    rows = sum(p.shape[0] for p in pieces)
    outs = [((rows, pieces[0].shape[1]), pieces[0].dtype)]
    return call(join_kernel, name, outs, idx, *pieces, cost=0.5)[0]


class Gather:
    def __init__(self, name, idx, piece, steps):
        self.name, self.idx, self.pieces = name, idx, [piece]
        self.back = [step for step, cut in reversed(steps) if cut]
        self.send(piece)

    def send(self, held):
        self.held = held
        self.pieces.append(swap(held, "dp", self.back[len(self.pieces) - 1]))

    def advance(self):
        if len(self.pieces) <= len(self.back):
            self.send(join(self.idx, self.pieces, f"{self.name}_join{len(self.pieces)}"))
            return True
        return False

    def finish(self):
        while self.advance():
            pass
        return self.pieces


class AllReduce:
    def __init__(self, name, idx, keep, send, steps):
        self.name, self.idx, self.steps, self.gather = name, idx, steps, None
        self.keep, self.at = keep, 0
        self.got = swap(send, "dp", steps[0][0])

    def scatter(self):
        idx, at = self.idx, self.at + 1
        if at == len(self.steps):
            return add(idx, self.keep, self.got, f"{self.name}_last")
        step, cut = self.steps[at]
        self.at = at
        if cut:
            half = (self.keep.shape[0] // 2, self.keep.shape[1])
            self.keep, send = call(
                functools.partial(add_split_kernel, step),
                f"{self.name}_split{at}",
                [(half, self.keep.dtype)] * 2,
                idx,
                self.keep,
                self.got,
            )
        else:
            self.keep = send = add(idx, self.keep, self.got, f"{self.name}_add{at}")
        self.got = swap(send, "dp", step)
        return None

    def last(self):
        while self.at + 1 < len(self.steps):
            self.scatter()
        return self.keep, self.got

    def advance(self):
        if self.gather is not None:
            return self.gather.advance()
        piece = self.scatter()
        if piece is not None:
            self.gather = Gather(self.name, self.idx, piece, self.steps)
        return True

    def finish(self):
        while self.advance():
            pass
        return self.gather.pieces


def piece_row(idx_ref, steps, rows, count):
    cuts = [step for step, cut in steps if cut]
    back = list(reversed(cuts))
    row, size = 0, rows << len(cuts)
    for step in cuts:
        size //= 2
        bit = bit_set(idx_ref, 0, step)
        row = row + (1 - bit if (count >> back.index(step)) & 1 else bit) * size
    return pl.multiple_of(row, rows)


def each_piece(piece_refs, rows):
    count = 0
    for ref in piece_refs:
        for start in range(0, ref.shape[0], rows):
            yield count, ref, pl.ds(start, rows)
            count += 1


def per_group(shape, dim, stride):
    at = iota(shape, dim)
    group = jnp.floor((at.astype(f32) + 0.5) * (1.0 / stride)).astype(i32)
    return group, at - group * stride


def first_kernel(
    groups,
    idx_ref,
    owner_ref,
    pixel_hbm,
    w_stem_hbm,
    send_ref,
    slot_ref,
    dest_ref,
    info_ref,
    sums_ref,
    pixel_ref,
    w_stem_ref,
    sems,
):
    copies = [
        pltpu.make_async_copy(pixel_hbm, pixel_ref, sems.at[0]),
        pltpu.make_async_copy(w_stem_hbm, w_stem_ref, sems.at[1]),
    ]
    for copy in copies:
        copy.start()
    count, pix = pixel_ref.shape
    half = pix // 2
    slots = send_ref.shape[0]
    stride = slots // groups
    core = bit_set(idx_ref, 1, 1)
    table = owner_ref[...]
    own = owner_ref[pl.ds(idx_ref[0], 1), :]
    own_live = jnp.sum((own < groups).astype(f32), axis=1, keepdims=True).astype(i32)
    hot = (iota((groups, count), 0) == own).astype(f32)
    before = (iota((count, count), 0) < iota((count, count), 1)).astype(bf16)
    rank = jnp.sum(hot * dot(hot.astype(bf16), before), axis=0, keepdims=True).astype(i32)
    slot = jnp.where(own < groups, own * stride + HEAD_ROWS + rank, -1)
    slot_ref[...] = slot
    sources = jnp.sum((table == idx_ref[0]).astype(f32), axis=1, keepdims=True)
    lower = (iota((groups, groups), 1) < iota((groups, groups), 0)).astype(bf16)
    starts = dot(lower, jnp.broadcast_to(sources, (groups, 128)).astype(bf16))[:, :1].astype(i32)
    within = iota((groups, slots), 1) - stride * iota((groups, slots), 0) - HEAD_ROWS
    taken = (within >= 0) & (within < sources.astype(i32))
    dest_ref[...] = jnp.max(jnp.where(taken, starts + within, -1), axis=0, keepdims=True)
    prefix = jnp.sum(sources, axis=0, keepdims=True)
    live = jnp.sum((table < groups).astype(f32), axis=1, keepdims=True)
    live_total = jnp.sum(live, axis=0, keepdims=True)
    info_ref[...] = jnp.where(iota(info_ref.shape, 0) == 0, prefix, live_total)
    for copy in copies:
        copy.wait()
    low = pixel_ref[...].astype(bf16)
    live_low = jnp.where(iota((count, 1), 0) < own_live, low, jnp.zeros((), bf16))
    pre = dot(live_low, w_stem_ref[...])
    value = jnp.where(core == 0, col_sum(pre), col_sum(pre * pre))
    left, right = low[:, :half], low[:, half:]
    mine = jnp.where(core == 0, left, right)
    live_mine = jnp.where(core == 0, live_low[:, :half], live_low[:, half:])
    sums_ref[...] = jnp.zeros(sums_ref.shape, f32)
    for part in range(3):
        rounded = value.astype(bf16).astype(f32)
        for row in range(value.shape[1] // 128):
            sums_ref[row : row + 1, part * 128 : part * 128 + 128] = rounded[
                :, row * 128 : row * 128 + 128
            ]
        value = value - rounded
    value = col_sum(live_mine.astype(f32))
    for part in range(3):
        rounded = value.astype(bf16).astype(f32)
        sums_ref[8 + part : 9 + part] = rounded
        value = value - rounded
    pick = (iota((slots, count), 0) == slot).astype(bf16)
    _, place = per_group((slots, HEAD_ROWS), 0, stride)
    spread = (place == iota((slots, HEAD_ROWS), 1)).astype(bf16)
    send_ref[...] = (dot(pick, mine) + dot(spread, sums_ref[...].astype(bf16))).astype(bf16)


def gathered_sums(ref, groups):
    slots = ref.shape[0]
    _, place = per_group((HEAD_ROWS, slots), 1, slots // groups)
    collect = (place == iota((HEAD_ROWS, slots), 0)).astype(bf16)
    total = dot(collect, ref[...])
    value = total[:8, :128] + total[:8, 128:256] + total[:8, 256:384]
    pixel_sum = total[8:9] + total[9:10] + total[10:11]
    return jnp.concatenate([value[row : row + 1] for row in range(8)], axis=1), pixel_sum


def early_kernel(idx_ref, cot_ref, w_down_ref, low_ref, act_ref, sum_ref):
    total = jnp.zeros(sum_ref.shape, f32)
    for start in range(0, cot_ref.shape[0], BLK):
        at = pl.ds(start, BLK)
        cot = cot_ref[at]
        low = cot.astype(bf16)
        low_ref[at] = low
        act_ref[at] = dot_nt(low, w_down_ref[...])
        total = total + col_sum(cot)
    sum_ref[...] = total


def stem_kernel(
    groups,
    idx_ref,
    info_ref,
    dest_ref,
    mine_ref,
    other_ref,
    w_stem_ref,
    bn_gain_ref,
    bn_bias_ref,
    w_patch_ref,
    b_patch_ref,
    text_ref,
    ln1_gain_ref,
    ln1_bias_ref,
    centred_ref,
    normal_ref,
    act_ref,
    slope_ref,
    x_ref,
    a_low_ref,
    mean_ref,
    inv_ref,
    low_ref,
):
    count, pix = centred_ref.shape
    slots = mine_ref.shape[0]
    prefix = info_ref[0:1, :1].astype(i32)
    total = info_ref[1:2, :1]
    core = bit_set(idx_ref, 1, 1)
    sums, pixel_sums = zip(gathered_sums(mine_ref, groups), gathered_sums(other_ref, groups), strict=True)
    first, second = jnp.where(core == 0, sums[0], sums[1]), jnp.where(core == 0, sums[1], sums[0])
    mean = first / total
    inv = lax.rsqrt(second / total - mean * mean + norm_eps)
    mean_ref[...] = mean
    inv_ref[...] = inv
    halves = [
        (
            jnp.where(core == at, mine_ref[...], other_ref[...]),
            jnp.where(core == at, pixel_sums[0], pixel_sums[1]) / total,
        )
        for at in range(2)
    ]
    for start, size in stem_blocks(count, text_ref.shape[0]):
        at = pl.ds(start, size)
        x = text_ref[at]
        if start < count:
            place = (iota((size, slots), 0) + start == dest_ref[...]).astype(bf16)
            for side, (half_rows, half_mean) in enumerate(halves):
                packed = dot(place, half_rows)
                columns = pl.ds(side * (pix // 2), pix // 2)
                low_ref[at, columns] = packed.astype(bf16)
                centred_ref[at, columns] = (packed - half_mean).astype(bf16)
            normal = (dot(low_ref[at], w_stem_ref[...]) - mean) * inv
            normal_ref[at] = normal
            bn_out = normal * bn_gain_ref[...][None, :] + bn_bias_ref[...][None, :]
            cdf, slope = gelu_parts(bn_out)
            slope_ref[at] = slope
            act = (bn_out * cdf).astype(bf16)
            act_ref[at] = act
            embedded = (dot(act, w_patch_ref[...]) + b_patch_ref[...][None, :]).astype(bf16)
            here = iota((size, 1), 0) + start < prefix
            x = x + jnp.where(here, embedded.astype(f32), 0.0)
        x_ref[at] = x
        normal_one, _ = normed(x)
        a_low_ref[at] = (normal_one * ln1_gain_ref[...][None, :] + ln1_bias_ref[...][None, :]).astype(bf16)


def stem_blocks(count, rows):
    half = count // 2
    return [(0, half), (half, half)] + ([(count, rows - count)] if rows > count else [])


def segments(seq_ref, shape, dim):
    rows = iota(shape, dim)
    end = jnp.zeros((1, 1), i32)
    segment = jnp.zeros(shape, i32)
    for at in range(seq_ref.shape[1]):
        end = end + seq_ref[0:1, at : at + 1]
        segment = segment + (end <= rows).astype(i32)
    return segment


def head_lanes(width, head):
    lane = iota((1, width), 1)
    return (lane >= head * HEAD) & (lane < (head + 1) * HEAD)


def attention_kernel(
    idx_ref,
    info_ref,
    seq_ref,
    a_low_ref,
    w_qkv_ref,
    *refs,
):
    q_ref, k_ref, v_ref, merged_ref = refs[:4]
    rows = a_low_ref.shape[0]
    width = merged_ref.shape[1]
    low = a_low_ref[...]
    for t, (ref, scale) in enumerate(((q_ref, SCALE), (k_ref, 1.0), (v_ref, 1.0))):
        part = dot_nt(low, w_qkv_ref[pl.ds(t * width, width)])
        ref[...] = (part * scale if scale != 1.0 else part).astype(bf16)
    prefix = info_ref[0:1, :1].astype(i32)
    key_rows, query_rows = iota((rows, rows), 1), iota((rows, rows), 0)
    visible = (segments(seq_ref, (rows, 1), 0) == segments(seq_ref, (1, rows), 1)) & (
        (key_rows <= query_rows) | (key_rows < prefix)
    )
    bias = jnp.where(visible, 0.0, masked_score)
    zero = jnp.zeros((), bf16)
    merged = jnp.zeros((rows, width), f32)
    for head in range(width // HEAD):
        mask = head_lanes(width, head)
        scores = dot_nt(jnp.where(mask, q_ref[...], zero), k_ref[...]) + bias
        weights = jnp.exp(scores - jnp.max(scores, axis=-1, keepdims=True))
        share = 1.0 / jnp.sum(weights, axis=-1, keepdims=True)
        merged = jnp.where(mask, dot(weights.astype(bf16), v_ref[...]) * share, merged)
    merged_ref[...] = merged.astype(bf16)


def attention_out_kernel(idx_ref, own_ref, w_own_ref, far_ref, w_far_ref, out_ref):
    total = dot(own_ref[...], w_own_ref[...]) + dot(far_ref[...], w_far_ref[...])
    out_ref[...] = total.astype(out_ref.dtype)


def mlp_kernel(
    idx_ref,
    x_ref,
    part_ref,
    got_ref,
    b_out_ref,
    ln2_gain_ref,
    ln2_bias_ref,
    w_up_ref,
    b_up_ref,
    grad_act_ref,
    hidden_ref,
    b_low_ref,
    act_ref,
    grad_mid_ref,
    keep_ref,
    send_ref,
    sum_ref,
):
    top = bit_set(idx_ref, 1, 1)
    half = keep_ref.shape[0]
    sum_ref[...] = jnp.zeros(sum_ref.shape, f32)

    def step(part, carry):
        at = pl.ds(pl.multiple_of(part * half, half), half)
        attn = part_ref[at].astype(f32) + got_ref[at].astype(f32)
        hidden = x_ref[at] + attn + b_out_ref[...][None, :]
        hidden_ref[at] = hidden
        normal, _ = normed(hidden)
        b_low = (normal * ln2_gain_ref[...][None, :] + ln2_bias_ref[...][None, :]).astype(bf16)
        b_low_ref[at] = b_low
        middle = dot(b_low, w_up_ref[...]) + b_up_ref[...][None, :]
        cdf, slope = gelu_parts(middle)
        act_ref[at] = (middle * cdf).astype(bf16)
        grad_mid = (slope * grad_act_ref[at]).astype(bf16)
        grad_mid_ref[at] = grad_mid
        sum_ref[...] += col_sum(grad_mid.astype(f32))
        back = dot_nt(grad_mid, w_up_ref[...]).astype(bf16)

        @pl.when(top == part)
        def _():
            keep_ref[...] = back

        @pl.when(top != part)
        def _():
            send_ref[...] = back

        return carry

    lax.fori_loop(0, 2, step, 0)


def mlp_grads_kernel(
    steps,
    idx_ref,
    b_low_ref,
    act_ref,
    grad_mid_ref,
    grad_low_ref,
    down_keep_ref,
    down_send_ref,
    up_keep_ref,
    up_send_ref,
):
    for step, left, right, keep, send in (
        (steps[0], act_ref, grad_low_ref, down_keep_ref, down_send_ref),
        (steps[1], b_low_ref, grad_mid_ref, up_keep_ref, up_send_ref),
    ):
        top = bit_set(idx_ref, 0, step)
        half = keep.shape[0]
        for start in (0, half):
            put_half(keep, send, top, start, dot_tn(left[:, pl.ds(start, half)], right[...]))


def down_kernel(idx_ref, act_ref, w_down_ref, keep_ref, send_ref):
    top = bit_set(idx_ref, 1, 1)
    for start in range(0, act_ref.shape[0], BLK):
        put_half(keep_ref, send_ref, top, start, dot(act_ref[pl.ds(start, BLK)], w_down_ref[...]))


def output_kernel(
    idx_ref, hidden_ref, mine_ref, other_ref, b_down_ref, out_ref, held_ref, sems
):
    top = bit_set(idx_ref, 1, 1)
    half = mine_ref.shape[0]
    copies = []
    for start in range(0, hidden_ref.shape[0], BLK):
        at = pl.ds(start, BLK)
        down = pick_half(mine_ref, other_ref, top, start, half)
        held_ref[at] = hidden_ref[at] + down + b_down_ref[...][None, :]
        copies.append(
            pltpu.make_async_copy(held_ref.at[at], out_ref.at[at], sems.at[start // BLK])
        )
        copies[-1].start()
    for copy in copies:
        copy.wait()


def pick_half(mine_ref, other_ref, top, start, half):
    at = pl.ds(start % half, BLK)
    mine = top == (start // half)
    return jnp.where(mine, mine_ref[at].astype(f32), other_ref[at].astype(f32))


def hidden_back_kernel(
    idx_ref,
    mine_ref,
    other_ref,
    cot_ref,
    hidden_ref,
    ln2_gain_ref,
    w_out_own_ref,
    w_out_far_ref,
    grad_hidden_ref,
    low_ref,
    own_ref,
    far_ref,
    sums_ref,
):
    top = bit_set(idx_ref, 1, 1)
    half = mine_ref.shape[0]
    width = cot_ref.shape[1]
    sums = [jnp.zeros((1, width), f32)] * 3
    for start in range(0, cot_ref.shape[0], BLK):
        at = pl.ds(start, BLK)
        grad = pick_half(mine_ref, other_ref, top, start, half)
        normal, inv = normed(hidden_ref[at])
        grad_hidden = cot_ref[at] + norm_back(grad, normal, inv, ln2_gain_ref[...][None, :])
        grad_hidden_ref[at] = grad_hidden
        low = grad_hidden.astype(bf16)
        low_ref[at] = low
        own_ref[at] = dot_nt(low, w_out_own_ref[...]).astype(bf16)
        far_ref[at] = dot_nt(low, w_out_far_ref[...]).astype(bf16)
        sums = [
            sums[0] + col_sum(grad_hidden),
            sums[1] + col_sum(grad * normal),
            sums[2] + col_sum(grad),
        ]
    for at in range(3):
        sums_ref[at : at + 1] = sums[at]


def attention_back_kernel(
    idx_ref,
    info_ref,
    seq_ref,
    q_ref,
    k_ref,
    v_ref,
    grad_ref,
    w_qkv_ref,
    *refs,
):
    base_ref = refs[0] if len(refs) == 3 else None
    grad_qkv_ref, out_ref = refs[-2:]
    rows, width = q_ref.shape
    prefix = info_ref[0:1, :1].astype(i32)
    zero = jnp.zeros((), bf16)
    key_rows, query_rows = iota((rows, rows), 0), iota((rows, rows), 1)
    visible = (segments(seq_ref, (rows, 1), 0) == segments(seq_ref, (1, rows), 1)) & (
        (key_rows <= query_rows) | (key_rows < prefix)
    )
    bias = jnp.where(visible, 0.0, masked_score)
    grad_values = jnp.zeros((rows, width), f32)
    grad_keys = jnp.zeros((rows, width), f32)
    grad_queries = jnp.zeros((rows, width), f32)
    for head in range(width // HEAD):
        mask = head_lanes(width, head)
        query = jnp.where(mask, q_ref[...], zero)
        grad = jnp.where(mask, grad_ref[...], zero)
        scores = dot_nt(k_ref[...], query) + bias
        weights = jnp.exp(scores - jnp.max(scores, axis=0, keepdims=True))
        probs = weights * (1.0 / jnp.sum(weights, axis=0, keepdims=True))
        grad_weights = dot_nt(v_ref[...], grad)
        delta = jnp.sum(probs * grad_weights, axis=0, keepdims=True)
        grad_scores = (probs * (grad_weights - delta)).astype(bf16)
        grad_values = grad_values + dot(probs.astype(bf16), grad)
        grad_keys = grad_keys + dot(grad_scores, query)
        grad_queries = jnp.where(mask, dot_tn(grad_scores, k_ref[...]), grad_queries)
    total = jnp.zeros((rows, w_qkv_ref.shape[1]), f32)
    for t, value in enumerate((grad_queries * SCALE, grad_keys, grad_values)):
        low = value.astype(bf16)
        grad_qkv_ref[t] = low
        total = total + dot(low, w_qkv_ref[pl.ds(t * width, width)])
    if base_ref is not None:
        total = total + base_ref[...]
    out_ref[...] = total.astype(out_ref.dtype)


def text_back_kernel(
    idx_ref,
    info_ref,
    part_ref,
    got_ref,
    grad_hidden_ref,
    x_ref,
    ln1_gain_ref,
    normal_ref,
    slope_ref,
    w_patch_ref,
    late_ref,
    up_sum_ref,
    down_sum_ref,
    grad_text_ref,
    embed_ref,
    zed_ref,
    small_ref,
):
    count, channels = normal_ref.shape
    width = x_ref.shape[1]
    prefix = info_ref[0:1, :1].astype(i32)
    bn_sums = [jnp.zeros((1, channels), f32)] * 2
    sums = [jnp.zeros((1, width), f32)] * 3
    for start, size in stem_blocks(count, x_ref.shape[0]):
        at = pl.ds(start, size)
        grad = part_ref[at].astype(f32) + got_ref[at].astype(f32)
        normal, inv = normed(x_ref[at])
        grad_text = grad_hidden_ref[at] + norm_back(grad, normal, inv, ln1_gain_ref[...][None, :])
        grad_text_ref[at] = grad_text
        sums[1] = sums[1] + col_sum(grad * normal)
        sums[2] = sums[2] + col_sum(grad)
        if start < count:
            here = iota((size, 1), 0) + start < prefix
            embed = jnp.where(here, grad_text, 0.0).astype(bf16)
            embed_ref[at] = embed
            sums[0] = sums[0] + col_sum(embed.astype(f32))
            zed = slope_ref[at] * dot_nt(embed, w_patch_ref[...])
            zed_ref[at] = zed
            bn_sums = [bn_sums[0] + col_sum(zed * normal_ref[at]), bn_sums[1] + col_sum(zed)]
    small_ref[...] = jnp.zeros(small_ref.shape, f32)
    small_ref[0:1] = bn_sums[0]
    small_ref[1:2] = bn_sums[1]
    for at in range(3):
        small_ref[2 + at : 3 + at, :width] = sums[at]
    small_ref[5:8, :width] = late_ref[...]
    small_ref[8:9, : up_sum_ref.shape[1]] = up_sum_ref[...]
    small_ref[9:10, :width] = down_sum_ref[...]


def head_grads_kernel(
    step, idx_ref, grad_qkv_ref, a_low_ref, merged_ref, low_ref, keep_ref, send_ref
):
    top = bit_set(idx_ref, 0, step)
    width = merged_ref.shape[1]
    for t in range(3):
        put_half(keep_ref, send_ref, top, t * width, dot_tn(grad_qkv_ref[t], a_low_ref[...]))
    put_half(keep_ref, send_ref, top, 3 * width, dot_tn(merged_ref[...], low_ref[...]))


def part_grads_kernel(
    step,
    idx_ref,
    info_ref,
    act_ref,
    embed_ref,
    zed_ref,
    normal_ref,
    centred_ref,
    keep_ref,
    send_ref,
):
    top = bit_set(idx_ref, 0, step)
    half = keep_ref.shape[0]
    first = idx_ref[1] * (2 * half)
    here = iota((normal_ref.shape[0], 1), 0) < info_ref[0:1, :1].astype(i32)
    for part in range(2):
        columns = pl.ds(pl.multiple_of(first + part * half, half), half)
        normal = jnp.where(here, normal_ref[:, columns], 0.0).astype(bf16)
        values = [
            dot_tn(act_ref[:, columns], embed_ref[...]),
            dot_tn(zed_ref[:, columns].astype(bf16), centred_ref[...]),
            dot_tn(normal, centred_ref[...]),
        ]
        put_half(keep_ref, send_ref, top, part * half, jnp.concatenate(values, axis=1))


def correct_kernel(
    steps,
    idx_ref,
    keep_ref,
    got_ref,
    small_ref,
    inv_ref,
    bn_gain_ref,
    info_ref,
    out_ref,
):
    rows = out_ref.shape[0]
    width = out_ref.shape[1] // 2
    cuts = [step for step, cut in steps if cut]
    size = rows << len(cuts)
    row = idx_ref[1] * size
    for step in cuts:
        size //= 2
        row = row + bit_set(idx_ref, 0, step) * size
    hot = iota((rows, inv_ref.shape[1]), 1) == iota((rows, inv_ref.shape[1]), 0) + row

    def column(value):
        return jnp.sum(jnp.where(hot, value, 0.0), axis=1, keepdims=True)

    factor = column(inv_ref[...] * bn_gain_ref[...][None, :])
    share = column(small_ref[0:1]) / info_ref[1:2, :1]
    total = keep_ref[...].astype(f32) + got_ref[...].astype(f32)
    stem = factor * (total[:, width : 2 * width] - share * total[:, 2 * width :])
    out_ref[:, :width] = total[:, :width].astype(out_ref.dtype)
    out_ref[:, width:] = stem.astype(out_ref.dtype)


def pixel_back_kernel(idx_ref, dest_ref, zed_ref, inv_ref, bn_gain_ref, w_stem_ref, slots_ref):
    slots, half = slots_ref.shape
    place = (iota((zed_ref.shape[0], slots), 0) == dest_ref[...]).astype(bf16)
    core = bit_set(idx_ref, 1, 1)
    weights = w_stem_ref[pl.ds(pl.multiple_of(core * half, half), half)]
    scaled = (zed_ref[...] * (inv_ref[...] * bn_gain_ref[...][None, :])).astype(bf16)
    rows = dot_nt(scaled, weights).astype(bf16)
    slots_ref[...] = dot_tn(place, rows).astype(bf16)


def pixel_rest_kernel(
    groups,
    idx_ref,
    owner_ref,
    info_ref,
    pixel_ref,
    w_stem_ref,
    mean_ref,
    inv_ref,
    bn_gain_ref,
    small_ref,
    out_ref,
):
    own = owner_ref[pl.ds(idx_ref[0], 1), :]
    live = jnp.sum((own < groups).astype(f32), axis=1, keepdims=True).astype(i32)
    total = info_ref[1:2, :1]
    pre = dot(pixel_ref[...].astype(bf16), w_stem_ref[...])
    normal = (pre - mean_ref[...]) * inv_ref[...]
    factor = inv_ref[...] * bn_gain_ref[...][None, :]
    rest = factor * (small_ref[1:2] / total + normal * (small_ref[0:1] / total))
    rest = jnp.where(iota((pixel_ref.shape[0], 1), 0) < live, rest, 0.0)
    out_ref[...] = dot_nt(rest.astype(bf16), w_stem_ref[...])


def pixel_kernel(
    idx_ref, slot_ref, mine_ref, other_ref, rest_ref, out_ref, held_ref, sems
):
    copies = []
    slots, half = mine_ref.shape
    pick = (iota((slots, out_ref.shape[0]), 0) == slot_ref[...]).astype(bf16)
    core = bit_set(idx_ref, 1, 1)
    for side in range(2):
        value = jnp.where(core == side, mine_ref[...], other_ref[...])
        columns = pl.ds(side * half, half)
        held_ref[:, columns] = dot_tn(pick, value) - rest_ref[:, columns]
        copies.append(
            pltpu.make_async_copy(held_ref.at[:, columns], out_ref.at[:, columns], sems.at[side])
        )
        copies[-1].start()
    for copy in copies:
        copy.wait()


def widen_kernel(steps, idx_ref, *refs):
    pieces, (out_ref, held_ref, sems) = refs[:-3], refs[-3:]
    rows = pieces[0].shape[0]
    copies = []
    for count, ref, at in each_piece(pieces, rows):
        here = pl.ds(count * rows, rows)
        held_ref[here] = ref[at].astype(f32)
        to = pl.ds(piece_row(idx_ref, steps, rows, count), rows)
        copies.append(pltpu.make_async_copy(held_ref.at[here], out_ref.at[to], sems.at[count]))
        copies[-1].start()
    for copy in copies:
        copy.wait()


def widen_two_kernel(steps, idx_ref, *refs):
    pieces, (first_ref, second_ref, held_ref, sems) = refs[:-4], refs[-4:]
    rows = pieces[0].shape[0]
    for count, ref, at in each_piece(pieces, rows):
        held_ref[pl.ds(piece_row(idx_ref, steps, rows, count), rows)] = ref[at].astype(f32)
    split = first_ref.shape[0]
    copies = [
        pltpu.make_async_copy(held_ref.at[pl.ds(0, split)], first_ref, sems.at[0]),
        pltpu.make_async_copy(
            held_ref.at[pl.ds(split, second_ref.shape[0])], second_ref, sems.at[1]
        ),
    ]
    for copy in copies:
        copy.start()
    for copy in copies:
        copy.wait()


def widen_parts_kernel(
    steps,
    idx_ref,
    held_ref,
    last_ref,
    far_held_ref,
    far_last_ref,
    near_ref,
    near_far_ref,
    patch_ref,
    stem_ref,
    patch_rows_ref,
    stem_rows_ref,
    turned_ref,
    sems,
):
    width = patch_ref.shape[1]
    part = near_ref.shape[0]
    rows = part >> sum(cut for _, cut in steps)
    for flip, refs in (
        (0, (held_ref, last_ref)),
        (2, (far_held_ref, far_last_ref)),
        (1, (near_ref,)),
        (3, (near_far_ref,)),
    ):
        at = bit_set(idx_ref, 1, 1) ^ (flip & 1)
        at = at + 2 * (bit_set(idx_ref, 1, 2) ^ (flip >> 1))
        for count, ref, here in each_piece(refs, rows):
            row = at * part + piece_row(idx_ref, steps, rows, count)
            to = pl.ds(pl.multiple_of(row, rows), rows)
            patch_rows_ref[to] = ref[here, :width].astype(f32)
            stem_rows_ref[to] = ref[here, width:].astype(f32)
    copies = [pltpu.make_async_copy(patch_rows_ref, patch_ref, sems.at[0])]
    copies[0].start()
    for at in range(4):
        columns = pl.ds(at * part, part)
        turned_ref[:, columns] = stem_rows_ref[columns].T
        copies.append(
            pltpu.make_async_copy(
                turned_ref.at[:, columns], stem_ref.at[:, columns], sems.at[1 + at]
            )
        )
        copies[-1].start()
    for copy in copies:
        copy.wait()


def shards(
    pixels,
    patch_owner,
    seq_lengths,
    text_embed,
    cotangent,
    w_stem,
    bn_gain,
    bn_bias,
    w_patch,
    b_patch,
    ln1_gain,
    ln1_bias,
    w_qkv,
    w_out,
    b_out,
    ln2_gain,
    ln2_bias,
    w_up,
    b_up,
    w_down,
    b_down,
):
    groups = lax.axis_size("dp")
    assert lax.axis_size("mp") == 4
    near, far = bits_of("mp")
    bits = bits_of("dp")
    count, pix = pixels.shape
    rows, width = text_embed.shape
    channels = w_stem.shape[1]
    local = w_out.shape[0]
    units = w_up.shape[1]
    capacity = count // groups
    idx = jnp.stack([lax.axis_index("dp"), lax.axis_index("mp")]).astype(i32)

    Order.last = ()
    stride = HEAD_ROWS + capacity
    slots = groups * stride
    half_pix = pix // 2
    own_qkv = jnp.swapaxes(w_qkv, 1, 2).reshape(3 * local, width)
    far_qkv = swap(own_qkv, "mp", far)
    far_out = swap(w_out, "mp", far)
    owners = patch_owner.reshape(groups, count)
    send_rows, slot, dest, info = call(
        functools.partial(first_kernel, groups),
        "first",
        [((slots, half_pix), bf16), ((1, count), i32), ((1, slots), i32), ((8, 128), f32)],
        idx,
        owners,
        pixels,
        w_stem,
        scratch=[
            pltpu.VMEM((HEAD_ROWS, half_pix), f32),
            pltpu.VMEM((count, pix), f32),
            pltpu.VMEM((pix, channels), bf16),
            pltpu.SemaphoreType.DMA((2,)),
        ],
        cost=4,
        hbm=(2, 3),
    )

    def exchange(values):
        return lax.all_to_all(
            values.reshape(groups, stride, half_pix), "dp", split_axis=0, concat_axis=0, tiled=True
        ).reshape(slots, half_pix)

    arrived = exchange(send_rows)
    grad_low, grad_act, down_sum = call(
        early_kernel,
        "early",
        [((rows, width), bf16), ((rows, units), f32), ((1, width), f32)],
        idx,
        cotangent,
        w_down,
        cost=2,
    )
    (arrived,) = call(land_kernel, "land", [((slots, half_pix), bf16)], idx, arrived, cost=1)
    arrived_other = swap(arrived, "mp", near)
    tick(idx)
    centred, normal, stem_act, slope, x_rows, a_low, mean, inv = call(
        functools.partial(stem_kernel, groups),
        "stem",
        [
            ((count, pix), bf16),
            ((count, channels), f32),
            ((count, channels), bf16),
            ((count, channels), f32),
            ((rows, width), f32),
            ((rows, width), bf16),
            ((1, channels), f32),
            ((1, channels), f32),
        ],
        idx,
        info,
        dest,
        arrived,
        arrived_other,
        w_stem,
        bn_gain,
        bn_bias,
        w_patch,
        b_patch,
        text_embed,
        ln1_gain,
        ln1_bias,
        scratch=[pltpu.VMEM((count, pix), bf16)],
        cost=4,
    )
    head_shapes = [((rows, local), bf16)] * 4
    q_own, k_own, v_own, merged = call(
        attention_kernel,
        "attention_own",
        head_shapes,
        idx,
        info,
        seq_lengths,
        a_low,
        own_qkv,
        cost=4,
    )
    q_far, k_far, v_far, merged_far = call(
        attention_kernel,
        "attention_far",
        head_shapes,
        idx,
        info,
        seq_lengths,
        a_low,
        far_qkv,
        cost=4,
    )
    (attn,) = call(
        attention_out_kernel,
        "attention_out",
        [((rows, width), bf16)],
        idx,
        merged,
        w_out,
        merged_far,
        far_out,
    )
    attn_got = swap(attn, "mp", near)
    half = (rows // 2, width)
    hidden, b_low, act, grad_mid, keep, send, up_sum = call(
        mlp_kernel,
        "mlp",
        [
            ((rows, width), f32),
            ((rows, width), bf16),
            ((rows, units), bf16),
            ((rows, units), bf16),
            (half, bf16),
            (half, bf16),
            ((1, units), f32),
        ],
        idx,
        x_rows,
        attn,
        attn_got,
        b_out,
        ln2_gain,
        ln2_bias,
        w_up,
        b_up,
        grad_act,
        cost=4,
    )
    grad_b_near = swap(send, "mp", near)
    out_keep, send = call(down_kernel, "down", [(half, bf16)] * 2, idx, act, w_down, cost=2)
    out_near = swap(send, "mp", near)
    grad_b = add(idx, keep, grad_b_near, "grad_b1")
    grad_b_got = swap(grad_b, "mp", far)
    down_steps = plan(places(bits, DOWN_ORDER), units)
    up_steps = plan(places(bits, UP_ORDER), width)
    down_keep, down_send, up_keep, up_send = call(
        functools.partial(mlp_grads_kernel, (down_steps[0][0], up_steps[0][0])),
        "mlp_grads",
        [((units // 2, width), bf16)] * 2 + [((width // 2, units), bf16)] * 2,
        idx,
        b_low,
        act,
        grad_mid,
        grad_low,
        cost=3,
    )
    down_sums = AllReduce("down", idx, down_keep, down_send, down_steps)
    up_sums = AllReduce("up", idx, up_keep, up_send, up_steps)
    out = add(idx, out_keep, out_near, "out1")
    out_got = swap(out, "mp", far)
    grad_b_mine = add(idx, grad_b, grad_b_got, "grad_b2")
    grad_b_other = swap(grad_b_mine, "mp", near)
    tick(idx)

    grad_hidden, hidden_low, grad_own, grad_far, late_sums = call(
        hidden_back_kernel,
        "hidden_back",
        [
            ((rows, width), f32),
            ((rows, width), bf16),
            ((rows, local), bf16),
            ((rows, local), bf16),
            ((3, width), f32),
        ],
        idx,
        grad_b_mine,
        grad_b_other,
        cotangent,
        hidden,
        ln2_gain,
        w_out,
        far_out,
        cost=3,
    )
    grad_qkv, grad_a = call(
        attention_back_kernel,
        "attention_back_own",
        [((3, rows, local), bf16), ((rows, width), f32)],
        idx,
        info,
        seq_lengths,
        q_own,
        k_own,
        v_own,
        grad_own,
        own_qkv,
        cost=5,
    )
    _, grad_a = call(
        attention_back_kernel,
        "attention_back_far",
        [((3, rows, local), bf16), ((rows, width), bf16)],
        idx,
        info,
        seq_lengths,
        q_far,
        k_far,
        v_far,
        grad_far,
        far_qkv,
        grad_a,
        cost=5,
    )
    grad_a_got = swap(grad_a, "mp", near)
    up_sums.advance()
    grad_text, grad_embed, grad_zed, small = call(
        text_back_kernel,
        "text_back",
        [
            ((rows, width), f32),
            ((count, width), bf16),
            ((count, channels), f32),
            ((10, channels), f32),
        ],
        idx,
        info,
        grad_a,
        grad_a_got,
        grad_hidden,
        x_rows,
        ln1_gain,
        normal,
        slope,
        w_patch,
        late_sums,
        up_sum,
        down_sum,
        cost=4,
    )
    small_got = swap(small, "dp", bits[0])
    part = channels // 4
    part_steps = plan(places(bits, PART_ORDER), part)
    keep, send = call(
        functools.partial(part_grads_kernel, part_steps[0][0]),
        "part_grads",
        [((part // 2, width + 2 * pix), bf16)] * 2,
        idx,
        info,
        stem_act,
        grad_embed,
        grad_zed,
        normal,
        centred,
        cost=2,
    )
    part_sums = AllReduce("part", idx, keep, send, part_steps)
    small = add(idx, small, small_got, "small0")
    small_got = swap(small, "dp", bits[1])
    out = add(idx, out, out_got, "out2")
    out_other = swap(out, "mp", near)
    up_sums.advance()
    for step in bits[2:]:
        small = add(idx, small, small_got, f"small{step}")
        small_got = swap(small, "dp", step)
    (row_slots,) = call(
        pixel_back_kernel,
        "pixel_back",
        [((slots, half_pix), bf16)],
        idx,
        dest,
        grad_zed,
        inv,
        bn_gain,
        w_stem,
        cost=2,
    )
    returned = exchange(row_slots)
    (output,) = call(
        output_kernel,
        "output",
        [((rows, width), f32)],
        idx,
        hidden,
        out,
        out_other,
        b_down,
        scratch=[pltpu.VMEM((rows, width), f32), pltpu.SemaphoreType.DMA((rows // BLK,))],
        cost=2,
        place=HBM,
    )
    small = add(idx, small, small_got, "small_last")
    part_sums.scatter()
    heads_steps = plan(places(bits, HEADS_ORDER), 4 * local)
    keep, send = call(
        functools.partial(head_grads_kernel, heads_steps[0][0]),
        "head_grads",
        [((2 * local, width), bf16)] * 2,
        idx,
        grad_qkv,
        a_low,
        merged,
        hidden_low,
        cost=2,
    )
    heads_sums = AllReduce("heads", idx, keep, send, heads_steps)
    down_sums.advance()
    up_sums.advance()
    (rest,) = call(
        functools.partial(pixel_rest_kernel, groups),
        "pixel_rest",
        [((count, pix), f32)],
        idx,
        owners,
        info,
        pixels,
        w_stem,
        mean,
        inv,
        bn_gain,
        small,
        cost=2,
    )
    part_sums.scatter()
    up_sums.advance()
    heads_sums.advance()
    returned_other = swap(returned, "mp", near)
    keep, got = part_sums.last()
    (piece,) = call(
        functools.partial(correct_kernel, part_steps),
        "correct",
        [((keep.shape[0], width + pix), bf16)],
        idx,
        keep,
        got,
        small,
        inv,
        bn_gain,
        info,
        cost=1,
    )
    parts = Gather("part", idx, piece, part_steps)
    up_sums.advance()
    (grad_pixels,) = call(
        pixel_kernel,
        "pixel",
        [((count, pix), f32)],
        idx,
        slot,
        returned,
        returned_other,
        rest,
        scratch=[pltpu.VMEM((count, pix), f32), pltpu.SemaphoreType.DMA((2,))],
        cost=2,
        place=HBM,
    )
    heads_sums.advance()
    down_sums.advance()
    parts.advance()
    heads_sums.advance()

    def widen(name, sums, steps, total):
        pieces = sums.finish()
        cols = pieces[0].shape[1]
        return call(
            functools.partial(widen_kernel, steps),
            name,
            [((total, cols), f32)],
            idx,
            *pieces,
            scratch=[
                pltpu.VMEM((total, cols), f32),
                pltpu.SemaphoreType.DMA((total // pieces[0].shape[0],)),
            ],
            cost=2,
            place=HBM,
        )[0]

    grad_w_up = widen("wide_up", up_sums, up_steps, width)
    down_sums.advance()
    parts.finish()
    held, last = parts.held, parts.pieces[-1]
    far_held = swap(held, "mp", far)
    heads_sums.advance()
    down_sums.advance()
    near_own = swap(join(idx, [held, last], "parts_own"), "mp", near)
    far_last = swap(last, "mp", far)
    heads_sums.advance()
    down_sums.advance()
    near_far = swap(join(idx, [far_held, far_last], "parts_far"), "mp", near)
    tick(idx)
    grad_w_patch, grad_w_stem = call(
        functools.partial(widen_parts_kernel, part_steps),
        "wide_parts",
        [((channels, width), f32), ((pix, channels), f32)],
        idx,
        held,
        last,
        far_held,
        far_last,
        near_own,
        near_far,
        scratch=[
            pltpu.VMEM((channels, width), f32),
            pltpu.VMEM((channels, pix), f32),
            pltpu.VMEM((pix, channels), f32),
            pltpu.SemaphoreType.DMA((5,)),
        ],
        cost=4,
        place=HBM,
    )
    grad_w_qkv, grad_w_out = call(
        functools.partial(widen_two_kernel, heads_steps),
        "wide_heads",
        [((3 * local, width), f32), ((local, width), f32)],
        idx,
        *heads_sums.finish(),
        scratch=[pltpu.VMEM((4 * local, width), f32), pltpu.SemaphoreType.DMA((2,))],
        cost=2,
        place=HBM,
    )
    grad_w_qkv = jnp.swapaxes(grad_w_qkv.reshape(3, local, width), 1, 2)
    grad_w_down = widen("wide_down", down_sums, down_steps, units)
    return (
        output,
        grad_pixels,
        grad_text,
        grad_w_stem,
        small[0],
        small[1],
        grad_w_patch,
        small[2, :width],
        small[3, :width],
        small[4, :width],
        grad_w_qkv,
        grad_w_out,
        small[5, :width],
        small[6, :width],
        small[7, :width],
        grad_w_up,
        small[8, :units],
        grad_w_down,
        small[9, :width],
    )


def solution(mesh):
    in_specs = (
        P("dp", None),
        P(),
        P("dp", None),
        P("dp", None),
        P("dp", None),
        P(),
        P(),
        P(),
        P(),
        P(),
        P(),
        P(),
        P(None, None, "mp"),
        P("mp", None),
        P(),
        P(),
        P(),
        P(None, "mp"),
        P("mp"),
        P("mp", None),
        P(),
    )
    out_specs = (
        P("dp", None),
        P("dp", None),
        P("dp", None),
        P(),
        P(),
        P(),
        P(),
        P(),
        P(),
        P(),
        P(None, None, "mp"),
        P("mp", None),
        P(),
        P(),
        P(),
        P(None, "mp"),
        P("mp"),
        P("mp", None),
        P(),
    )
    return jax.shard_map(shards, mesh=mesh, in_specs=in_specs, out_specs=out_specs, check_vma=False)
```

```python
import functools

import jax
import jax.numpy as jnp
from jax import lax
from jax.experimental import pallas as pl
from jax.experimental.pallas import tpu as pltpu
from jax.sharding import PartitionSpec as P

HEAD = 64
BLK = 256
SCALE = HEAD ** (-0.5)

norm_eps = 1e-05
masked_score = -1e30
f32 = jnp.float32
bf16 = jnp.bfloat16
i32 = jnp.int32


def dot(left, right):
    return lax.dot_general(left, right, (((1,), (0,)), ((), ())), preferred_element_type=f32)


def dot_tn(left, right):
    return lax.dot_general(left, right, (((0,), (0,)), ((), ())), preferred_element_type=f32)


def dot_nt(left, right):
    return lax.dot_general(left, right, (((1,), (1,)), ((), ())), preferred_element_type=f32)


def iota(shape, dim):
    return lax.broadcasted_iota(i32, shape, dim)


def gelu_parts(values):
    cdf = 0.5 * (1.0 + lax.erf(values * (0.5**0.5)))
    pdf = jnp.exp(-0.5 * values * values) * 0.3989422804014327
    return cdf, cdf + values * pdf


def normed(values):
    center = values - jnp.mean(values, axis=-1, keepdims=True)
    inv_std = lax.rsqrt(jnp.mean(center * center, axis=-1, keepdims=True) + norm_eps)
    return center * inv_std, inv_std


def norm_back(grad_out, normal, inv_std, gain):
    scaled = grad_out * gain
    return inv_std * (
        scaled
        - jnp.mean(scaled, axis=-1, keepdims=True)
        - normal * jnp.mean(scaled * normal, axis=-1, keepdims=True)
    )


def col_sum(values):
    return jnp.sum(values, axis=0, keepdims=True)


VMEM = pl.BlockSpec(memory_space=pltpu.VMEM)
SMEM = pl.BlockSpec(memory_space=pltpu.SMEM)
ANY = pl.BlockSpec(memory_space=pl.ANY)
HBM = pl.BlockSpec(memory_space=pltpu.HBM)
PER_US = 1e10
HEAD_ROWS = 16
DOWN_ORDER = (1, 0, 2)
UP_ORDER = (0, 1, 2)
HEADS_ORDER = (0, 1, 2)
PART_ORDER = (0, 1, 2)


class Place:
    def __getitem__(self, at):
        return lax.axis_index(("dp", "mp")[at])


class Order:
    last = ()


def call(kernel, name, outs, *args, scratch=(), cost=1.0, place=None, hbm=()):
    shapes = [jax.ShapeDtypeStruct(s, t) for s, t in outs]
    shapes.append(jax.ShapeDtypeStruct((8, 128), f32))
    args = args[1:]
    first, after = len(args), Order.last
    at_mark = first + len(after) + len(outs)

    def body(*refs):
        refs[at_mark][...] = jnp.zeros((8, 128), f32)
        kernel(Place(), *refs[:first], *refs[first + len(after) : at_mark], *refs[at_mark + 1 :])

    *results, mark = pl.pallas_call(
        body,
        name=name,
        out_shape=shapes,
        in_specs=[HBM if at + 1 in hbm else VMEM for at in range(first)] + [ANY] * len(after),
        out_specs=[place or VMEM] * len(outs) + [VMEM],
        scratch_shapes=list(scratch),
        compiler_params=pltpu.CompilerParams(vmem_limit_bytes=(20 if cost > 1 else 6) << 20),
        cost_estimate=pl.CostEstimate(
            flops=int(cost * PER_US), bytes_accessed=0, transcendentals=0
        ),
    )(*args, *after)
    Order.last = (mark,)
    return results


def bits_of(axis):
    size = lax.axis_size(axis)
    bits = []
    step = 1
    while step < size:
        bits.append(step)
        step *= 2
    assert step == size
    return bits


def swap(values, axis, step):
    size = lax.axis_size(axis)
    return lax.ppermute(values, axis, [(i, i ^ step) for i in range(size)])


def put_half(keep_ref, send_ref, top, start, value):
    half = keep_ref.shape[0]
    at = pl.ds(start % half, value.shape[0])
    mine = top == (start // half)

    @pl.when(mine)
    def _():
        keep_ref[at] = value.astype(keep_ref.dtype)

    @pl.when(jnp.logical_not(mine))
    def _():
        send_ref[at] = value.astype(send_ref.dtype)


def bit_set(idx_ref, which, step):
    return (idx_ref[which] // step) % 2


def places(bits, order):
    return [bits[at] for at in order] if len(bits) == len(order) else bits


def plan(order, rows):
    steps = []
    for step in order:
        cut = rows % 32 == 0
        rows = rows // 2 if cut else rows
        steps.append((step, cut))
    return steps


def add_split_kernel(step, idx_ref, keep_ref, got_ref, next_ref, send_ref):
    top = bit_set(idx_ref, 0, step)
    half = next_ref.shape[0]
    for part in range(2):
        at = pl.ds(part * half, half)
        total = keep_ref[at].astype(f32) + got_ref[at].astype(f32)
        put_half(next_ref, send_ref, top, part * half, total)


def land_kernel(idx_ref, in_ref, out_ref):
    out_ref[...] = in_ref[...]


def land_two_kernel(idx_ref, in_ref, more_ref, out_ref, out_more_ref):
    out_ref[...] = in_ref[...]
    out_more_ref[...] = more_ref[...]


def tick_kernel(idx_ref):
    pass


def tick(idx):
    call(tick_kernel, "tick", [], idx, cost=4)


def add_kernel(idx_ref, keep_ref, got_ref, out_ref):
    out_ref[...] = (keep_ref[...].astype(f32) + got_ref[...].astype(f32)).astype(out_ref.dtype)


def add(idx, keep, got, name="add"):
    return call(add_kernel, name, [(keep.shape, keep.dtype)], idx, keep, got)[0]


def join_kernel(idx_ref, *refs):
    out_ref = refs[-1]
    start = 0
    for ref in refs[:-1]:
        out_ref[pl.ds(start, ref.shape[0])] = ref[...]
        start += ref.shape[0]


def join(idx, pieces, name="join"):
    if len(pieces) == 1:
        return pieces[0]
    rows = sum(p.shape[0] for p in pieces)
    outs = [((rows, pieces[0].shape[1]), pieces[0].dtype)]
    return call(join_kernel, name, outs, idx, *pieces, cost=0.5)[0]


class Gather:
    def __init__(self, name, idx, piece, steps):
        self.name, self.idx, self.pieces = name, idx, [piece]
        self.back = [step for step, cut in reversed(steps) if cut]
        self.send(piece)

    def send(self, held):
        self.held = held
        self.pieces.append(swap(held, "dp", self.back[len(self.pieces) - 1]))

    def advance(self):
        if len(self.pieces) <= len(self.back):
            self.send(join(self.idx, self.pieces, f"{self.name}_join{len(self.pieces)}"))
            return True
        return False

    def finish(self):
        while self.advance():
            pass
        return self.pieces


class AllReduce:
    def __init__(self, name, idx, keep, send, steps):
        self.name, self.idx, self.steps, self.gather = name, idx, steps, None
        self.keep, self.at = keep, 0
        self.got = swap(send, "dp", steps[0][0])

    def scatter(self):
        idx, at = self.idx, self.at + 1
        if at == len(self.steps):
            return add(idx, self.keep, self.got, f"{self.name}_last")
        step, cut = self.steps[at]
        self.at = at
        if cut:
            half = (self.keep.shape[0] // 2, self.keep.shape[1])
            self.keep, send = call(
                functools.partial(add_split_kernel, step),
                f"{self.name}_split{at}",
                [(half, self.keep.dtype)] * 2,
                idx,
                self.keep,
                self.got,
            )
        else:
            self.keep = send = add(idx, self.keep, self.got, f"{self.name}_add{at}")
        self.got = swap(send, "dp", step)
        return None

    def last(self):
        while self.at + 1 < len(self.steps):
            self.scatter()
        return self.keep, self.got

    def advance(self):
        if self.gather is not None:
            return self.gather.advance()
        piece = self.scatter()
        if piece is not None:
            self.gather = Gather(self.name, self.idx, piece, self.steps)
        return True

    def finish(self):
        while self.advance():
            pass
        return self.gather.pieces


def piece_row(idx_ref, steps, rows, count):
    cuts = [step for step, cut in steps if cut]
    back = list(reversed(cuts))
    row, size = 0, rows << len(cuts)
    for step in cuts:
        size //= 2
        bit = bit_set(idx_ref, 0, step)
        row = row + (1 - bit if (count >> back.index(step)) & 1 else bit) * size
    return pl.multiple_of(row, rows)


def each_piece(piece_refs, rows):
    count = 0
    for ref in piece_refs:
        for start in range(0, ref.shape[0], rows):
            yield count, ref, pl.ds(start, rows)
            count += 1


def per_group(shape, dim, stride):
    at = iota(shape, dim)
    group = jnp.floor((at.astype(f32) + 0.5) * (1.0 / stride)).astype(i32)
    return group, at - group * stride


def first_kernel(
    groups,
    idx_ref,
    owner_ref,
    pixel_hbm,
    w_stem_hbm,
    send_ref,
    slot_ref,
    dest_ref,
    info_ref,
    sums_ref,
    pixel_ref,
    w_stem_ref,
    sems,
):
    copies = [
        pltpu.make_async_copy(pixel_hbm, pixel_ref, sems.at[0]),
        pltpu.make_async_copy(w_stem_hbm, w_stem_ref, sems.at[1]),
    ]
    for copy in copies:
        copy.start()
    count, pix = pixel_ref.shape
    half = pix // 2
    slots = send_ref.shape[0]
    stride = slots // groups
    core = bit_set(idx_ref, 1, 1)
    table = owner_ref[...]
    own = owner_ref[pl.ds(idx_ref[0], 1), :]
    own_live = jnp.sum((own < groups).astype(f32), axis=1, keepdims=True).astype(i32)
    hot = (iota((groups, count), 0) == own).astype(f32)
    before = (iota((count, count), 0) < iota((count, count), 1)).astype(bf16)
    rank = jnp.sum(hot * dot(hot.astype(bf16), before), axis=0, keepdims=True).astype(i32)
    slot = jnp.where(own < groups, own * stride + HEAD_ROWS + rank, -1)
    slot_ref[...] = slot
    sources = jnp.sum((table == idx_ref[0]).astype(f32), axis=1, keepdims=True)
    lower = (iota((groups, groups), 1) < iota((groups, groups), 0)).astype(bf16)
    starts = dot(lower, jnp.broadcast_to(sources, (groups, 128)).astype(bf16))[:, :1].astype(i32)
    within = iota((groups, slots), 1) - stride * iota((groups, slots), 0) - HEAD_ROWS
    taken = (within >= 0) & (within < sources.astype(i32))
    dest_ref[...] = jnp.max(jnp.where(taken, starts + within, -1), axis=0, keepdims=True)
    prefix = jnp.sum(sources, axis=0, keepdims=True)
    live = jnp.sum((table < groups).astype(f32), axis=1, keepdims=True)
    live_total = jnp.sum(live, axis=0, keepdims=True)
    info_ref[...] = jnp.where(iota(info_ref.shape, 0) == 0, prefix, live_total)
    for copy in copies:
        copy.wait()
    low = pixel_ref[...].astype(bf16)
    live_low = jnp.where(iota((count, 1), 0) < own_live, low, jnp.zeros((), bf16))
    pre = dot(live_low, w_stem_ref[...])
    value = jnp.where(core == 0, col_sum(pre), col_sum(pre * pre))
    left, right = low[:, :half], low[:, half:]
    mine = jnp.where(core == 0, left, right)
    live_mine = jnp.where(core == 0, live_low[:, :half], live_low[:, half:])
    sums_ref[...] = jnp.zeros(sums_ref.shape, f32)
    for part in range(3):
        rounded = value.astype(bf16).astype(f32)
        for row in range(value.shape[1] // 128):
            sums_ref[row : row + 1, part * 128 : part * 128 + 128] = rounded[
                :, row * 128 : row * 128 + 128
            ]
        value = value - rounded
    value = col_sum(live_mine.astype(f32))
    for part in range(3):
        rounded = value.astype(bf16).astype(f32)
        sums_ref[8 + part : 9 + part] = rounded
        value = value - rounded
    pick = (iota((slots, count), 0) == slot).astype(bf16)
    _, place = per_group((slots, HEAD_ROWS), 0, stride)
    spread = (place == iota((slots, HEAD_ROWS), 1)).astype(bf16)
    send_ref[...] = (dot(pick, mine) + dot(spread, sums_ref[...].astype(bf16))).astype(bf16)


def gathered_sums(ref, groups):
    slots = ref.shape[0]
    _, place = per_group((HEAD_ROWS, slots), 1, slots // groups)
    collect = (place == iota((HEAD_ROWS, slots), 0)).astype(bf16)
    total = dot(collect, ref[...])
    value = total[:8, :128] + total[:8, 128:256] + total[:8, 256:384]
    pixel_sum = total[8:9] + total[9:10] + total[10:11]
    return jnp.concatenate([value[row : row + 1] for row in range(8)], axis=1), pixel_sum


def early_kernel(idx_ref, cot_ref, w_down_ref, low_ref, act_ref, sum_ref):
    total = jnp.zeros(sum_ref.shape, f32)
    for start in range(0, cot_ref.shape[0], BLK):
        at = pl.ds(start, BLK)
        cot = cot_ref[at]
        low = cot.astype(bf16)
        low_ref[at] = low
        act_ref[at] = dot_nt(low, w_down_ref[...])
        total = total + col_sum(cot)
    sum_ref[...] = total


def stem_kernel(
    groups,
    idx_ref,
    info_ref,
    dest_ref,
    mine_ref,
    other_ref,
    w_stem_ref,
    bn_gain_ref,
    bn_bias_ref,
    w_patch_ref,
    b_patch_ref,
    text_ref,
    ln1_gain_ref,
    ln1_bias_ref,
    centred_ref,
    normal_ref,
    act_ref,
    slope_ref,
    x_ref,
    a_low_ref,
    mean_ref,
    inv_ref,
    low_ref,
):
    count, pix = centred_ref.shape
    slots = mine_ref.shape[0]
    prefix = info_ref[0:1, :1].astype(i32)
    total = info_ref[1:2, :1]
    core = bit_set(idx_ref, 1, 1)
    sums, pixel_sums = zip(gathered_sums(mine_ref, groups), gathered_sums(other_ref, groups), strict=True)
    first, second = jnp.where(core == 0, sums[0], sums[1]), jnp.where(core == 0, sums[1], sums[0])
    mean = first / total
    inv = lax.rsqrt(second / total - mean * mean + norm_eps)
    mean_ref[...] = mean
    inv_ref[...] = inv
    halves = [
        (
            jnp.where(core == at, mine_ref[...], other_ref[...]),
            jnp.where(core == at, pixel_sums[0], pixel_sums[1]) / total,
        )
        for at in range(2)
    ]
    for start, size in stem_blocks(count, text_ref.shape[0]):
        at = pl.ds(start, size)
        x = text_ref[at]
        if start < count:
            place = (iota((size, slots), 0) + start == dest_ref[...]).astype(bf16)
            for side, (half_rows, half_mean) in enumerate(halves):
                packed = dot(place, half_rows)
                columns = pl.ds(side * (pix // 2), pix // 2)
                low_ref[at, columns] = packed.astype(bf16)
                centred_ref[at, columns] = (packed - half_mean).astype(bf16)
            normal = (dot(low_ref[at], w_stem_ref[...]) - mean) * inv
            normal_ref[at] = normal
            bn_out = normal * bn_gain_ref[...][None, :] + bn_bias_ref[...][None, :]
            cdf, slope = gelu_parts(bn_out)
            slope_ref[at] = slope
            act = (bn_out * cdf).astype(bf16)
            act_ref[at] = act
            embedded = (dot(act, w_patch_ref[...]) + b_patch_ref[...][None, :]).astype(bf16)
            here = iota((size, 1), 0) + start < prefix
            x = x + jnp.where(here, embedded.astype(f32), 0.0)
        x_ref[at] = x
        normal_one, _ = normed(x)
        a_low_ref[at] = (normal_one * ln1_gain_ref[...][None, :] + ln1_bias_ref[...][None, :]).astype(bf16)


def stem_blocks(count, rows):
    half = count // 2
    return [(0, half), (half, half)] + ([(count, rows - count)] if rows > count else [])


def segments(seq_ref, shape, dim):
    rows = iota(shape, dim)
    end = jnp.zeros((1, 1), i32)
    segment = jnp.zeros(shape, i32)
    for at in range(seq_ref.shape[1]):
        end = end + seq_ref[0:1, at : at + 1]
        segment = segment + (end <= rows).astype(i32)
    return segment


def head_lanes(width, head):
    lane = iota((1, width), 1)
    return (lane >= head * HEAD) & (lane < (head + 1) * HEAD)


def attention_kernel(
    idx_ref,
    info_ref,
    seq_ref,
    a_low_ref,
    w_qkv_ref,
    *refs,
):
    q_ref, k_ref, v_ref, merged_ref = refs[:4]
    rows = a_low_ref.shape[0]
    width = merged_ref.shape[1]
    low = a_low_ref[...]
    for t, (ref, scale) in enumerate(((q_ref, SCALE), (k_ref, 1.0), (v_ref, 1.0))):
        part = dot_nt(low, w_qkv_ref[pl.ds(t * width, width)])
        ref[...] = (part * scale if scale != 1.0 else part).astype(bf16)
    prefix = info_ref[0:1, :1].astype(i32)
    key_rows, query_rows = iota((rows, rows), 1), iota((rows, rows), 0)
    visible = (segments(seq_ref, (rows, 1), 0) == segments(seq_ref, (1, rows), 1)) & (
        (key_rows <= query_rows) | (key_rows < prefix)
    )
    bias = jnp.where(visible, 0.0, masked_score)
    zero = jnp.zeros((), bf16)
    merged = jnp.zeros((rows, width), f32)
    for head in range(width // HEAD):
        mask = head_lanes(width, head)
        scores = dot_nt(jnp.where(mask, q_ref[...], zero), k_ref[...]) + bias
        weights = jnp.exp(scores - jnp.max(scores, axis=-1, keepdims=True))
        share = 1.0 / jnp.sum(weights, axis=-1, keepdims=True)
        merged = jnp.where(mask, dot(weights.astype(bf16), v_ref[...]) * share, merged)
    merged_ref[...] = merged.astype(bf16)


def attention_out_kernel(idx_ref, own_ref, w_own_ref, far_ref, w_far_ref, out_ref):
    total = dot(own_ref[...], w_own_ref[...]) + dot(far_ref[...], w_far_ref[...])
    out_ref[...] = total.astype(out_ref.dtype)


def mlp_kernel(
    idx_ref,
    x_ref,
    part_ref,
    got_ref,
    b_out_ref,
    ln2_gain_ref,
    ln2_bias_ref,
    w_up_ref,
    b_up_ref,
    grad_act_ref,
    hidden_ref,
    b_low_ref,
    act_ref,
    grad_mid_ref,
    keep_ref,
    send_ref,
    sum_ref,
):
    top = bit_set(idx_ref, 1, 1)
    half = keep_ref.shape[0]
    sum_ref[...] = jnp.zeros(sum_ref.shape, f32)

    def step(part, carry):
        at = pl.ds(pl.multiple_of(part * half, half), half)
        attn = part_ref[at].astype(f32) + got_ref[at].astype(f32)
        hidden = x_ref[at] + attn + b_out_ref[...][None, :]
        hidden_ref[at] = hidden
        normal, _ = normed(hidden)
        b_low = (normal * ln2_gain_ref[...][None, :] + ln2_bias_ref[...][None, :]).astype(bf16)
        b_low_ref[at] = b_low
        middle = dot(b_low, w_up_ref[...]) + b_up_ref[...][None, :]
        cdf, slope = gelu_parts(middle)
        act_ref[at] = (middle * cdf).astype(bf16)
        grad_mid = (slope * grad_act_ref[at]).astype(bf16)
        grad_mid_ref[at] = grad_mid
        sum_ref[...] += col_sum(grad_mid.astype(f32))
        back = dot_nt(grad_mid, w_up_ref[...]).astype(bf16)

        @pl.when(top == part)
        def _():
            keep_ref[...] = back

        @pl.when(top != part)
        def _():
            send_ref[...] = back

        return carry

    lax.fori_loop(0, 2, step, 0)


def mlp_grads_kernel(
    steps,
    idx_ref,
    b_low_ref,
    act_ref,
    grad_mid_ref,
    grad_low_ref,
    down_keep_ref,
    down_send_ref,
    up_keep_ref,
    up_send_ref,
):
    for step, left, right, keep, send in (
        (steps[0], act_ref, grad_low_ref, down_keep_ref, down_send_ref),
        (steps[1], b_low_ref, grad_mid_ref, up_keep_ref, up_send_ref),
    ):
        top = bit_set(idx_ref, 0, step)
        half = keep.shape[0]
        for start in (0, half):
            put_half(keep, send, top, start, dot_tn(left[:, pl.ds(start, half)], right[...]))


def down_kernel(idx_ref, act_ref, w_down_ref, keep_ref, send_ref):
    top = bit_set(idx_ref, 1, 1)
    for start in range(0, act_ref.shape[0], BLK):
        put_half(keep_ref, send_ref, top, start, dot(act_ref[pl.ds(start, BLK)], w_down_ref[...]))


def output_kernel(
    idx_ref, hidden_ref, mine_ref, other_ref, b_down_ref, out_ref, held_ref, sems
):
    top = bit_set(idx_ref, 1, 1)
    half = mine_ref.shape[0]
    copies = []
    for start in range(0, hidden_ref.shape[0], BLK):
        at = pl.ds(start, BLK)
        down = pick_half(mine_ref, other_ref, top, start, half)
        held_ref[at] = hidden_ref[at] + down + b_down_ref[...][None, :]
        copies.append(
            pltpu.make_async_copy(held_ref.at[at], out_ref.at[at], sems.at[start // BLK])
        )
        copies[-1].start()
    for copy in copies:
        copy.wait()


def pick_half(mine_ref, other_ref, top, start, half):
    at = pl.ds(start % half, BLK)
    mine = top == (start // half)
    return jnp.where(mine, mine_ref[at].astype(f32), other_ref[at].astype(f32))


def hidden_back_kernel(
    idx_ref,
    mine_ref,
    other_ref,
    cot_ref,
    hidden_ref,
    ln2_gain_ref,
    w_out_own_ref,
    w_out_far_ref,
    grad_hidden_ref,
    low_ref,
    own_ref,
    far_ref,
    sums_ref,
):
    top = bit_set(idx_ref, 1, 1)
    half = mine_ref.shape[0]
    width = cot_ref.shape[1]
    sums = [jnp.zeros((1, width), f32)] * 3
    for start in range(0, cot_ref.shape[0], BLK):
        at = pl.ds(start, BLK)
        grad = pick_half(mine_ref, other_ref, top, start, half)
        normal, inv = normed(hidden_ref[at])
        grad_hidden = cot_ref[at] + norm_back(grad, normal, inv, ln2_gain_ref[...][None, :])
        grad_hidden_ref[at] = grad_hidden
        low = grad_hidden.astype(bf16)
        low_ref[at] = low
        own_ref[at] = dot_nt(low, w_out_own_ref[...]).astype(bf16)
        far_ref[at] = dot_nt(low, w_out_far_ref[...]).astype(bf16)
        sums = [
            sums[0] + col_sum(grad_hidden),
            sums[1] + col_sum(grad * normal),
            sums[2] + col_sum(grad),
        ]
    for at in range(3):
        sums_ref[at : at + 1] = sums[at]


def attention_back_kernel(
    idx_ref,
    info_ref,
    seq_ref,
    q_ref,
    k_ref,
    v_ref,
    grad_ref,
    w_qkv_ref,
    *refs,
):
    base_ref = refs[0] if len(refs) == 3 else None
    grad_qkv_ref, out_ref = refs[-2:]
    rows, width = q_ref.shape
    prefix = info_ref[0:1, :1].astype(i32)
    zero = jnp.zeros((), bf16)
    key_rows, query_rows = iota((rows, rows), 0), iota((rows, rows), 1)
    visible = (segments(seq_ref, (rows, 1), 0) == segments(seq_ref, (1, rows), 1)) & (
        (key_rows <= query_rows) | (key_rows < prefix)
    )
    bias = jnp.where(visible, 0.0, masked_score)
    grad_values = jnp.zeros((rows, width), f32)
    grad_keys = jnp.zeros((rows, width), f32)
    grad_queries = jnp.zeros((rows, width), f32)
    for head in range(width // HEAD):
        mask = head_lanes(width, head)
        query = jnp.where(mask, q_ref[...], zero)
        grad = jnp.where(mask, grad_ref[...], zero)
        scores = dot_nt(k_ref[...], query) + bias
        weights = jnp.exp(scores - jnp.max(scores, axis=0, keepdims=True))
        probs = weights * (1.0 / jnp.sum(weights, axis=0, keepdims=True))
        grad_weights = dot_nt(v_ref[...], grad)
        delta = jnp.sum(probs * grad_weights, axis=0, keepdims=True)
        grad_scores = (probs * (grad_weights - delta)).astype(bf16)
        grad_values = grad_values + dot(probs.astype(bf16), grad)
        grad_keys = grad_keys + dot(grad_scores, query)
        grad_queries = jnp.where(mask, dot_tn(grad_scores, k_ref[...]), grad_queries)
    total = jnp.zeros((rows, w_qkv_ref.shape[1]), f32)
    for t, value in enumerate((grad_queries * SCALE, grad_keys, grad_values)):
        low = value.astype(bf16)
        grad_qkv_ref[t] = low
        total = total + dot(low, w_qkv_ref[pl.ds(t * width, width)])
    if base_ref is not None:
        total = total + base_ref[...]
    out_ref[...] = total.astype(out_ref.dtype)


def text_back_kernel(
    idx_ref,
    info_ref,
    part_ref,
    got_ref,
    grad_hidden_ref,
    x_ref,
    ln1_gain_ref,
    normal_ref,
    slope_ref,
    w_patch_ref,
    late_ref,
    up_sum_ref,
    down_sum_ref,
    grad_text_ref,
    embed_ref,
    zed_ref,
    small_ref,
):
    count, channels = normal_ref.shape
    width = x_ref.shape[1]
    prefix = info_ref[0:1, :1].astype(i32)
    bn_sums = [jnp.zeros((1, channels), f32)] * 2
    sums = [jnp.zeros((1, width), f32)] * 3
    for start, size in stem_blocks(count, x_ref.shape[0]):
        at = pl.ds(start, size)
        grad = part_ref[at].astype(f32) + got_ref[at].astype(f32)
        normal, inv = normed(x_ref[at])
        grad_text = grad_hidden_ref[at] + norm_back(grad, normal, inv, ln1_gain_ref[...][None, :])
        grad_text_ref[at] = grad_text
        sums[1] = sums[1] + col_sum(grad * normal)
        sums[2] = sums[2] + col_sum(grad)
        if start < count:
            here = iota((size, 1), 0) + start < prefix
            embed = jnp.where(here, grad_text, 0.0).astype(bf16)
            embed_ref[at] = embed
            sums[0] = sums[0] + col_sum(embed.astype(f32))
            zed = slope_ref[at] * dot_nt(embed, w_patch_ref[...])
            zed_ref[at] = zed
            bn_sums = [bn_sums[0] + col_sum(zed * normal_ref[at]), bn_sums[1] + col_sum(zed)]
    small_ref[...] = jnp.zeros(small_ref.shape, f32)
    small_ref[0:1] = bn_sums[0]
    small_ref[1:2] = bn_sums[1]
    for at in range(3):
        small_ref[2 + at : 3 + at, :width] = sums[at]
    small_ref[5:8, :width] = late_ref[...]
    small_ref[8:9, : up_sum_ref.shape[1]] = up_sum_ref[...]
    small_ref[9:10, :width] = down_sum_ref[...]


def head_grads_kernel(
    step, idx_ref, grad_qkv_ref, a_low_ref, merged_ref, low_ref, keep_ref, send_ref
):
    top = bit_set(idx_ref, 0, step)
    width = merged_ref.shape[1]
    for t in range(3):
        put_half(keep_ref, send_ref, top, t * width, dot_tn(grad_qkv_ref[t], a_low_ref[...]))
    put_half(keep_ref, send_ref, top, 3 * width, dot_tn(merged_ref[...], low_ref[...]))


def part_grads_kernel(
    step,
    idx_ref,
    info_ref,
    act_ref,
    embed_ref,
    zed_ref,
    normal_ref,
    centred_ref,
    keep_ref,
    send_ref,
):
    top = bit_set(idx_ref, 0, step)
    half = keep_ref.shape[0]
    first = idx_ref[1] * (2 * half)
    here = iota((normal_ref.shape[0], 1), 0) < info_ref[0:1, :1].astype(i32)
    for part in range(2):
        columns = pl.ds(pl.multiple_of(first + part * half, half), half)
        normal = jnp.where(here, normal_ref[:, columns], 0.0).astype(bf16)
        values = [
            dot_tn(act_ref[:, columns], embed_ref[...]),
            dot_tn(zed_ref[:, columns].astype(bf16), centred_ref[...]),
            dot_tn(normal, centred_ref[...]),
        ]
        put_half(keep_ref, send_ref, top, part * half, jnp.concatenate(values, axis=1))


def correct_kernel(
    steps,
    idx_ref,
    keep_ref,
    got_ref,
    small_ref,
    inv_ref,
    bn_gain_ref,
    info_ref,
    out_ref,
):
    rows = out_ref.shape[0]
    width = out_ref.shape[1] // 2
    cuts = [step for step, cut in steps if cut]
    size = rows << len(cuts)
    row = idx_ref[1] * size
    for step in cuts:
        size //= 2
        row = row + bit_set(idx_ref, 0, step) * size
    hot = iota((rows, inv_ref.shape[1]), 1) == iota((rows, inv_ref.shape[1]), 0) + row

    def column(value):
        return jnp.sum(jnp.where(hot, value, 0.0), axis=1, keepdims=True)

    factor = column(inv_ref[...] * bn_gain_ref[...][None, :])
    share = column(small_ref[0:1]) / info_ref[1:2, :1]
    total = keep_ref[...].astype(f32) + got_ref[...].astype(f32)
    stem = factor * (total[:, width : 2 * width] - share * total[:, 2 * width :])
    out_ref[:, :width] = total[:, :width].astype(out_ref.dtype)
    out_ref[:, width:] = stem.astype(out_ref.dtype)


def pixel_back_kernel(idx_ref, dest_ref, zed_ref, inv_ref, bn_gain_ref, w_stem_ref, slots_ref):
    slots, half = slots_ref.shape
    place = (iota((zed_ref.shape[0], slots), 0) == dest_ref[...]).astype(bf16)
    core = bit_set(idx_ref, 1, 1)
    weights = w_stem_ref[pl.ds(pl.multiple_of(core * half, half), half)]
    scaled = (zed_ref[...] * (inv_ref[...] * bn_gain_ref[...][None, :])).astype(bf16)
    rows = dot_nt(scaled, weights).astype(bf16)
    slots_ref[...] = dot_tn(place, rows).astype(bf16)


def pixel_rest_kernel(
    groups,
    idx_ref,
    owner_ref,
    info_ref,
    pixel_ref,
    w_stem_ref,
    mean_ref,
    inv_ref,
    bn_gain_ref,
    small_ref,
    out_ref,
):
    own = owner_ref[pl.ds(idx_ref[0], 1), :]
    live = jnp.sum((own < groups).astype(f32), axis=1, keepdims=True).astype(i32)
    total = info_ref[1:2, :1]
    pre = dot(pixel_ref[...].astype(bf16), w_stem_ref[...])
    normal = (pre - mean_ref[...]) * inv_ref[...]
    factor = inv_ref[...] * bn_gain_ref[...][None, :]
    rest = factor * (small_ref[1:2] / total + normal * (small_ref[0:1] / total))
    rest = jnp.where(iota((pixel_ref.shape[0], 1), 0) < live, rest, 0.0)
    out_ref[...] = dot_nt(rest.astype(bf16), w_stem_ref[...])


def pixel_kernel(
    idx_ref, slot_ref, mine_ref, other_ref, rest_ref, out_ref, held_ref, sems
):
    copies = []
    slots, half = mine_ref.shape
    pick = (iota((slots, out_ref.shape[0]), 0) == slot_ref[...]).astype(bf16)
    core = bit_set(idx_ref, 1, 1)
    for side in range(2):
        value = jnp.where(core == side, mine_ref[...], other_ref[...])
        columns = pl.ds(side * half, half)
        held_ref[:, columns] = dot_tn(pick, value) - rest_ref[:, columns]
        copies.append(
            pltpu.make_async_copy(held_ref.at[:, columns], out_ref.at[:, columns], sems.at[side])
        )
        copies[-1].start()
    for copy in copies:
        copy.wait()


def widen_kernel(steps, idx_ref, *refs):
    pieces, (out_ref, held_ref, sems) = refs[:-3], refs[-3:]
    rows = pieces[0].shape[0]
    copies = []
    for count, ref, at in each_piece(pieces, rows):
        here = pl.ds(count * rows, rows)
        held_ref[here] = ref[at].astype(f32)
        to = pl.ds(piece_row(idx_ref, steps, rows, count), rows)
        copies.append(pltpu.make_async_copy(held_ref.at[here], out_ref.at[to], sems.at[count]))
        copies[-1].start()
    for copy in copies:
        copy.wait()


def widen_two_kernel(steps, idx_ref, *refs):
    pieces, (first_ref, second_ref, held_ref, sems) = refs[:-4], refs[-4:]
    rows = pieces[0].shape[0]
    for count, ref, at in each_piece(pieces, rows):
        held_ref[pl.ds(piece_row(idx_ref, steps, rows, count), rows)] = ref[at].astype(f32)
    split = first_ref.shape[0]
    copies = [
        pltpu.make_async_copy(held_ref.at[pl.ds(0, split)], first_ref, sems.at[0]),
        pltpu.make_async_copy(
            held_ref.at[pl.ds(split, second_ref.shape[0])], second_ref, sems.at[1]
        ),
    ]
    for copy in copies:
        copy.start()
    for copy in copies:
        copy.wait()


def widen_parts_kernel(
    steps,
    idx_ref,
    held_ref,
    last_ref,
    far_held_ref,
    far_last_ref,
    near_ref,
    near_far_ref,
    patch_ref,
    stem_ref,
    patch_rows_ref,
    stem_rows_ref,
    turned_ref,
    sems,
):
    width = patch_ref.shape[1]
    part = near_ref.shape[0]
    rows = part >> sum(cut for _, cut in steps)
    for flip, refs in (
        (0, (held_ref, last_ref)),
        (2, (far_held_ref, far_last_ref)),
        (1, (near_ref,)),
        (3, (near_far_ref,)),
    ):
        at = bit_set(idx_ref, 1, 1) ^ (flip & 1)
        at = at + 2 * (bit_set(idx_ref, 1, 2) ^ (flip >> 1))
        for count, ref, here in each_piece(refs, rows):
            row = at * part + piece_row(idx_ref, steps, rows, count)
            to = pl.ds(pl.multiple_of(row, rows), rows)
            patch_rows_ref[to] = ref[here, :width].astype(f32)
            stem_rows_ref[to] = ref[here, width:].astype(f32)
    copies = [pltpu.make_async_copy(patch_rows_ref, patch_ref, sems.at[0])]
    copies[0].start()
    for at in range(4):
        columns = pl.ds(at * part, part)
        turned_ref[:, columns] = stem_rows_ref[columns].T
        copies.append(
            pltpu.make_async_copy(
                turned_ref.at[:, columns], stem_ref.at[:, columns], sems.at[1 + at]
            )
        )
        copies[-1].start()
    for copy in copies:
        copy.wait()


def shards(
    pixels,
    patch_owner,
    seq_lengths,
    text_embed,
    cotangent,
    w_stem,
    bn_gain,
    bn_bias,
    w_patch,
    b_patch,
    ln1_gain,
    ln1_bias,
    w_qkv,
    w_out,
    b_out,
    ln2_gain,
    ln2_bias,
    w_up,
    b_up,
    w_down,
    b_down,
):
    groups = lax.axis_size("dp")
    assert lax.axis_size("mp") == 4
    near, far = bits_of("mp")
    bits = bits_of("dp")
    count, pix = pixels.shape
    rows, width = text_embed.shape
    channels = w_stem.shape[1]
    local = w_out.shape[0]
    units = w_up.shape[1]
    capacity = count // groups
    idx = jnp.stack([lax.axis_index("dp"), lax.axis_index("mp")]).astype(i32)

    Order.last = ()
    stride = HEAD_ROWS + capacity
    slots = groups * stride
    half_pix = pix // 2
    own_qkv = jnp.swapaxes(w_qkv, 1, 2).reshape(3 * local, width)
    far_qkv = swap(own_qkv, "mp", far)
    far_out = swap(w_out, "mp", far)
    owners = patch_owner.reshape(groups, count)
    send_rows, slot, dest, info = call(
        functools.partial(first_kernel, groups),
        "first",
        [((slots, half_pix), bf16), ((1, count), i32), ((1, slots), i32), ((8, 128), f32)],
        idx,
        owners,
        pixels,
        w_stem,
        scratch=[
            pltpu.VMEM((HEAD_ROWS, half_pix), f32),
            pltpu.VMEM((count, pix), f32),
            pltpu.VMEM((pix, channels), bf16),
            pltpu.SemaphoreType.DMA((2,)),
        ],
        cost=4,
        hbm=(2, 3),
    )

    def exchange(values):
        return lax.all_to_all(
            values.reshape(groups, stride, half_pix), "dp", split_axis=0, concat_axis=0, tiled=True
        ).reshape(slots, half_pix)

    arrived = exchange(send_rows)
    grad_low, grad_act, down_sum = call(
        early_kernel,
        "early",
        [((rows, width), bf16), ((rows, units), f32), ((1, width), f32)],
        idx,
        cotangent,
        w_down,
        cost=2,
    )
    (arrived,) = call(land_kernel, "land", [((slots, half_pix), bf16)], idx, arrived, cost=1)
    arrived_other = swap(arrived, "mp", near)
    tick(idx)
    centred, normal, stem_act, slope, x_rows, a_low, mean, inv = call(
        functools.partial(stem_kernel, groups),
        "stem",
        [
            ((count, pix), bf16),
            ((count, channels), f32),
            ((count, channels), bf16),
            ((count, channels), f32),
            ((rows, width), f32),
            ((rows, width), bf16),
            ((1, channels), f32),
            ((1, channels), f32),
        ],
        idx,
        info,
        dest,
        arrived,
        arrived_other,
        w_stem,
        bn_gain,
        bn_bias,
        w_patch,
        b_patch,
        text_embed,
        ln1_gain,
        ln1_bias,
        scratch=[pltpu.VMEM((count, pix), bf16)],
        cost=4,
    )
    head_shapes = [((rows, local), bf16)] * 4
    q_own, k_own, v_own, merged = call(
        attention_kernel,
        "attention_own",
        head_shapes,
        idx,
        info,
        seq_lengths,
        a_low,
        own_qkv,
        cost=4,
    )
    q_far, k_far, v_far, merged_far = call(
        attention_kernel,
        "attention_far",
        head_shapes,
        idx,
        info,
        seq_lengths,
        a_low,
        far_qkv,
        cost=4,
    )
    (attn,) = call(
        attention_out_kernel,
        "attention_out",
        [((rows, width), bf16)],
        idx,
        merged,
        w_out,
        merged_far,
        far_out,
    )
    attn_got = swap(attn, "mp", near)
    far_qkv, far_out = call(
        land_two_kernel,
        "land_far",
        [(far_qkv.shape, bf16), (far_out.shape, bf16)],
        idx,
        far_qkv,
        far_out,
        cost=1,
    )
    half = (rows // 2, width)
    hidden, b_low, act, grad_mid, keep, send, up_sum = call(
        mlp_kernel,
        "mlp",
        [
            ((rows, width), f32),
            ((rows, width), bf16),
            ((rows, units), bf16),
            ((rows, units), bf16),
            (half, bf16),
            (half, bf16),
            ((1, units), f32),
        ],
        idx,
        x_rows,
        attn,
        attn_got,
        b_out,
        ln2_gain,
        ln2_bias,
        w_up,
        b_up,
        grad_act,
        cost=4,
    )
    grad_b_near = swap(send, "mp", near)
    out_keep, send = call(down_kernel, "down", [(half, bf16)] * 2, idx, act, w_down, cost=2)
    out_near = swap(send, "mp", near)
    grad_b = add(idx, keep, grad_b_near, "grad_b1")
    grad_b_got = swap(grad_b, "mp", far)
    down_steps = plan(places(bits, DOWN_ORDER), units)
    up_steps = plan(places(bits, UP_ORDER), width)
    down_keep, down_send, up_keep, up_send = call(
        functools.partial(mlp_grads_kernel, (down_steps[0][0], up_steps[0][0])),
        "mlp_grads",
        [((units // 2, width), bf16)] * 2 + [((width // 2, units), bf16)] * 2,
        idx,
        b_low,
        act,
        grad_mid,
        grad_low,
        cost=3,
    )
    down_sums = AllReduce("down", idx, down_keep, down_send, down_steps)
    up_sums = AllReduce("up", idx, up_keep, up_send, up_steps)
    out = add(idx, out_keep, out_near, "out1")
    out_got = swap(out, "mp", far)
    grad_b_mine = add(idx, grad_b, grad_b_got, "grad_b2")
    grad_b_other = swap(grad_b_mine, "mp", near)
    tick(idx)

    grad_hidden, hidden_low, grad_own, grad_far, late_sums = call(
        hidden_back_kernel,
        "hidden_back",
        [
            ((rows, width), f32),
            ((rows, width), bf16),
            ((rows, local), bf16),
            ((rows, local), bf16),
            ((3, width), f32),
        ],
        idx,
        grad_b_mine,
        grad_b_other,
        cotangent,
        hidden,
        ln2_gain,
        w_out,
        far_out,
        cost=3,
    )
    grad_qkv, grad_a = call(
        attention_back_kernel,
        "attention_back_own",
        [((3, rows, local), bf16), ((rows, width), f32)],
        idx,
        info,
        seq_lengths,
        q_own,
        k_own,
        v_own,
        grad_own,
        own_qkv,
        cost=5,
    )
    _, grad_a = call(
        attention_back_kernel,
        "attention_back_far",
        [((3, rows, local), bf16), ((rows, width), bf16)],
        idx,
        info,
        seq_lengths,
        q_far,
        k_far,
        v_far,
        grad_far,
        far_qkv,
        grad_a,
        cost=5,
    )
    grad_a_got = swap(grad_a, "mp", near)
    up_sums.advance()
    grad_text, grad_embed, grad_zed, small = call(
        text_back_kernel,
        "text_back",
        [
            ((rows, width), f32),
            ((count, width), bf16),
            ((count, channels), f32),
            ((10, channels), f32),
        ],
        idx,
        info,
        grad_a,
        grad_a_got,
        grad_hidden,
        x_rows,
        ln1_gain,
        normal,
        slope,
        w_patch,
        late_sums,
        up_sum,
        down_sum,
        cost=4,
    )
    small_got = swap(small, "dp", bits[0])
    part = channels // 4
    part_steps = plan(places(bits, PART_ORDER), part)
    keep, send = call(
        functools.partial(part_grads_kernel, part_steps[0][0]),
        "part_grads",
        [((part // 2, width + 2 * pix), bf16)] * 2,
        idx,
        info,
        stem_act,
        grad_embed,
        grad_zed,
        normal,
        centred,
        cost=2,
    )
    part_sums = AllReduce("part", idx, keep, send, part_steps)
    small = add(idx, small, small_got, "small0")
    small_got = swap(small, "dp", bits[1])
    out = add(idx, out, out_got, "out2")
    out_other = swap(out, "mp", near)
    up_sums.advance()
    for step in bits[2:]:
        small = add(idx, small, small_got, f"small{step}")
        small_got = swap(small, "dp", step)
    heads_steps = plan(places(bits, HEADS_ORDER), 4 * local)
    keep, send = call(
        functools.partial(head_grads_kernel, heads_steps[0][0]),
        "head_grads",
        [((2 * local, width), bf16)] * 2,
        idx,
        grad_qkv,
        a_low,
        merged,
        hidden_low,
        cost=2,
    )
    heads_sums = AllReduce("heads", idx, keep, send, heads_steps)
    (row_slots,) = call(
        pixel_back_kernel,
        "pixel_back",
        [((slots, half_pix), bf16)],
        idx,
        dest,
        grad_zed,
        inv,
        bn_gain,
        w_stem,
        cost=2,
    )
    returned = exchange(row_slots)
    (output,) = call(
        output_kernel,
        "output",
        [((rows, width), f32)],
        idx,
        hidden,
        out,
        out_other,
        b_down,
        scratch=[pltpu.VMEM((rows, width), f32), pltpu.SemaphoreType.DMA((rows // BLK,))],
        cost=2,
        place=HBM,
    )
    small = add(idx, small, small_got, "small_last")
    part_sums.scatter()
    down_sums.advance()
    up_sums.advance()
    (rest,) = call(
        functools.partial(pixel_rest_kernel, groups),
        "pixel_rest",
        [((count, pix), f32)],
        idx,
        owners,
        info,
        pixels,
        w_stem,
        mean,
        inv,
        bn_gain,
        small,
        cost=2,
    )
    part_sums.scatter()
    up_sums.advance()
    heads_sums.advance()
    returned_other = swap(returned, "mp", near)
    keep, got = part_sums.last()
    (piece,) = call(
        functools.partial(correct_kernel, part_steps),
        "correct",
        [((keep.shape[0], width + pix), bf16)],
        idx,
        keep,
        got,
        small,
        inv,
        bn_gain,
        info,
        cost=1,
    )
    parts = Gather("part", idx, piece, part_steps)
    up_sums.advance()
    (grad_pixels,) = call(
        pixel_kernel,
        "pixel",
        [((count, pix), f32)],
        idx,
        slot,
        returned,
        returned_other,
        rest,
        scratch=[pltpu.VMEM((count, pix), f32), pltpu.SemaphoreType.DMA((2,))],
        cost=2,
        place=HBM,
    )
    heads_sums.advance()
    down_sums.advance()
    parts.advance()
    heads_sums.advance()

    def widen(name, sums, steps, total):
        pieces = sums.finish()
        cols = pieces[0].shape[1]
        return call(
            functools.partial(widen_kernel, steps),
            name,
            [((total, cols), f32)],
            idx,
            *pieces,
            scratch=[
                pltpu.VMEM((total, cols), f32),
                pltpu.SemaphoreType.DMA((total // pieces[0].shape[0],)),
            ],
            cost=2,
            place=HBM,
        )[0]

    grad_w_up = widen("wide_up", up_sums, up_steps, width)
    down_sums.advance()
    parts.finish()
    held, last = parts.held, parts.pieces[-1]
    far_held = swap(held, "mp", far)
    heads_sums.advance()
    down_sums.advance()
    near_own = swap(join(idx, [held, last], "parts_own"), "mp", near)
    far_last = swap(last, "mp", far)
    heads_sums.advance()
    down_sums.advance()
    near_far = swap(join(idx, [far_held, far_last], "parts_far"), "mp", near)
    tick(idx)
    grad_w_patch, grad_w_stem = call(
        functools.partial(widen_parts_kernel, part_steps),
        "wide_parts",
        [((channels, width), f32), ((pix, channels), f32)],
        idx,
        held,
        last,
        far_held,
        far_last,
        near_own,
        near_far,
        scratch=[
            pltpu.VMEM((channels, width), f32),
            pltpu.VMEM((channels, pix), f32),
            pltpu.VMEM((pix, channels), f32),
            pltpu.SemaphoreType.DMA((5,)),
        ],
        cost=4,
        place=HBM,
    )
    grad_w_qkv, grad_w_out = call(
        functools.partial(widen_two_kernel, heads_steps),
        "wide_heads",
        [((3 * local, width), f32), ((local, width), f32)],
        idx,
        *heads_sums.finish(),
        scratch=[pltpu.VMEM((4 * local, width), f32), pltpu.SemaphoreType.DMA((2,))],
        cost=2,
        place=HBM,
    )
    grad_w_qkv = jnp.swapaxes(grad_w_qkv.reshape(3, local, width), 1, 2)
    grad_w_down = widen("wide_down", down_sums, down_steps, units)
    return (
        output,
        grad_pixels,
        grad_text,
        grad_w_stem,
        small[0],
        small[1],
        grad_w_patch,
        small[2, :width],
        small[3, :width],
        small[4, :width],
        grad_w_qkv,
        grad_w_out,
        small[5, :width],
        small[6, :width],
        small[7, :width],
        grad_w_up,
        small[8, :units],
        grad_w_down,
        small[9, :width],
    )


def solution(mesh):
    in_specs = (
        P("dp", None),
        P(),
        P("dp", None),
        P("dp", None),
        P("dp", None),
        P(),
        P(),
        P(),
        P(),
        P(),
        P(),
        P(),
        P(None, None, "mp"),
        P("mp", None),
        P(),
        P(),
        P(),
        P(None, "mp"),
        P("mp"),
        P("mp", None),
        P(),
    )
    out_specs = (
        P("dp", None),
        P("dp", None),
        P("dp", None),
        P(),
        P(),
        P(),
        P(),
        P(),
        P(),
        P(),
        P(None, None, "mp"),
        P("mp", None),
        P(),
        P(),
        P(),
        P(None, "mp"),
        P("mp"),
        P("mp", None),
        P(),
    )
    return jax.shard_map(shards, mesh=mesh, in_specs=in_specs, out_specs=out_specs, check_vma=False)
```
